128 devices in a mesh: gx: 16 (over z, x), gy: 8 (over y, core).
Axes of the slice: x: 4, y: 4, z: 4, core: 2. Of those that a mesh axis runs over, the one named last changes fastest.
Arguments:
- coarse_state: float32 [5, 256, 256, 128], P(None, 'gx', 'gy'), may hold values from -1 to 6, as said below
- fine_state: float32 [16, 8, 2, 5, 32, 1024], P('gx', 'gy'), may hold values from -1 to 6, as said below
- corners: int32 [8, 32, 3], P('gy'), may hold values from 0 to 240, as said below
- slot_patch: int32 [8, 32], P('gy'), may hold values from 0 to 31, each once within a row
Outputs:
- coarse_out: float32 [5, 256, 256, 128], P(None, 'gx', 'gy')
- fine_out: float32 [16, 8, 2, 5, 32, 1024], P('gx', 'gy')
The draws below stay inside these ranges and needn't reach their ends.
Inputs may be any that keep to these rules, and one draw needn't show every extreme that they name: `coarse_state`: each cell holds the conserved fields of a state with density and pressure between 0.5 and 2 and each velocity component between -0.5 and 0.5. `fine_state`: each cell holds the conserved fields of a state with density and pressure between 0.5 and 2 and each velocity component between -0.5 and 0.5. Coordinates are multiples of 16; corners[c, q, 1] lies in [c * 32, (c + 1) * 32); patches of a column are distinct and listed by ascending x; at most 4 patches of a column share one x, and some x has exactly 4 in every column. `slot_patch`: each row is a permutation of the patches of that column.
All inputs are finite; a program needn't handle non-finite values.
Results may differ from the reference program's by a relative error of at most 0.0003.
Values sent between devices are 32-bit elements; how exact they have to be, the bound alone decides.
A program may use at most 192 MiB of HBM per device.

```python
import jax
import jax.numpy as jnp
from jax import lax

PC = 16
PF = 32
ZB = 8
NZ = 128
NX = 256
NY = 256
SLOTS = 2
MOST = 4
PCOL = 32
N_GX = 16
N_GY = 8


def assemble(density, velocity, pressure, axis_pos):
    kinetic = 0.5 * density * (velocity[0] * velocity[0] + velocity[1] * velocity[1] + velocity[2] * velocity[2])
    fields = [density, density * velocity[0], density * velocity[1], density * velocity[2], pressure * 2.5 + kinetic]
    return jnp.stack(fields, axis=axis_pos)


def draw_coarse_state(key, part):
    key = jax.random.fold_in(key, 1)
    shape = (NX, NY, NZ)
    subkeys = jax.random.split(key, 3)
    density = jnp.exp(jax.random.uniform(subkeys[0], shape, jnp.float32, -0.693, 0.693))
    velocity = jnp.clip(0.2 * jax.random.normal(subkeys[1], (3,) + shape, jnp.float32), -0.5, 0.5)
    pressure = jnp.exp(jax.random.uniform(subkeys[2], shape, jnp.float32, -0.693, 0.693))
    return assemble(density, velocity, pressure, 0)


def draw_fine_state(key, part):
    key = jax.random.fold_in(key, 3)
    shape = (N_GX, N_GY, SLOTS, PF, PF * PF)
    subkeys = jax.random.split(key, 3)
    density = jnp.exp(jax.random.uniform(subkeys[0], shape, jnp.float32, -0.693, 0.693))
    velocity = jnp.clip(0.2 * jax.random.normal(subkeys[1], (3,) + shape, jnp.float32), -0.5, 0.5)
    pressure = jnp.exp(jax.random.uniform(subkeys[2], shape, jnp.float32, -0.693, 0.693))
    return assemble(density, velocity, pressure, 3)


def draw_corners(key, part):
    key = jax.random.fold_in(key, 2)
    surplus = MOST - SLOTS

    def one_column(column_key, column):
        center_key, move_key, place_key = jax.random.split(column_key, 3)
        center = jax.random.randint(center_key, (), 0, N_GX)
        block_ids = jnp.arange(N_GX)
        losing = (block_ids - (center + N_GX // 2 - surplus // 2)) % N_GX < surplus
        counts = SLOTS + jnp.where(block_ids == center, surplus, 0) - jnp.where(losing, 1, 0)
        for turn in range(6):
            chosen_pair = jax.random.randint(jax.random.fold_in(move_key, turn), (2,), 0, N_GX)
            allowed = (chosen_pair[0] != center) & (chosen_pair[1] != center) & (chosen_pair[0] != chosen_pair[1]) & (counts[chosen_pair[0]] > 0) & (counts[chosen_pair[1]] < MOST - 1)
            step_size = jnp.where(allowed, 1, 0)
            counts = counts.at[chosen_pair[0]].add(-step_size).at[chosen_pair[1]].add(step_size)
        block_ends = jnp.cumsum(counts)
        starts = block_ends - counts
        patch_ids = jnp.arange(N_GX * SLOTS)
        owner_block = jnp.sum(block_ends[None, :] <= patch_ids[:, None], axis=1)
        within = patch_ids - starts[owner_block]
        layouts = jax.vmap(lambda subkey: jax.random.permutation(subkey, 2 * ZB))(jax.random.split(place_key, N_GX))
        slot_spot = layouts[owner_block, within]
        return jnp.stack([owner_block * PC, (column * 2 + slot_spot // ZB) * PC, slot_spot % ZB * PC], axis=1).astype(jnp.int32)
    return jax.vmap(one_column)(jax.random.split(key, N_GY), jnp.arange(N_GY))


def setup_inputs(seed: int = 0) -> dict:
    arg_keys = jax.random.split(jax.random.key(seed), 5)
    coarse_state = draw_coarse_state(jax.random.fold_in(arg_keys[4], 71), 0)
    fine_state = draw_fine_state(jax.random.fold_in(arg_keys[4], 71), 0)
    corners = draw_corners(jax.random.fold_in(arg_keys[4], 71), 0)
    slot_patch = jax.vmap(lambda own: jax.random.permutation(own, PCOL))(jax.random.split(arg_keys[3], N_GY)).reshape((N_GY, PCOL)).astype(jnp.int32)
    return {"coarse_state": coarse_state, "fine_state": fine_state, "corners": corners, "slot_patch": slot_patch}


ADIABATIC = 1.4
COURANT = 0.05

def euler_flux(left_side, right_side, normal):

    def pieces(conserved):
        density = conserved[0]
        momentum = conserved[1:4]
        energy = conserved[4]
        velocity = momentum[normal] / density
        kinetic = 0.5 * (momentum[0] * momentum[0] + momentum[1] * momentum[1] + momentum[2] * momentum[2]) / density
        pressure = (ADIABATIC - 1.0) * (energy - kinetic)
        signal = jnp.abs(velocity) + jnp.sqrt(ADIABATIC * pressure / density)
        fluxes = [density * velocity, momentum[0] * velocity, momentum[1] * velocity, momentum[2] * velocity, (energy + pressure) * velocity]
        fluxes[1 + normal] = fluxes[1 + normal] + pressure
        return (jnp.stack(fluxes), signal)
    flow_low, speed_low = pieces(left_side)
    flow_high, speed_high = pieces(right_side)
    fastest = jnp.maximum(speed_low, speed_high)
    return 0.5 * (flow_low + flow_high) - 0.5 * fastest * (right_side - left_side)

def fine_step(blocks, ghosts):
    half_len = ghosts.shape[2]
    lifted = jnp.repeat(jnp.repeat(ghosts, 2, axis=2), 2, axis=3)
    ext_x = jnp.concatenate([lifted[:, 0:1], blocks, lifted[:, 1:2]], axis=1)
    ext_y = jnp.concatenate([lifted[:, 2][:, :, None, :], blocks, lifted[:, 3][:, :, None, :]], axis=2)
    ext_z = jnp.concatenate([lifted[:, 4][..., None], blocks, lifted[:, 5][..., None]], axis=3)
    flow_x = euler_flux(ext_x[:, :-1], ext_x[:, 1:], 0)
    flow_y = euler_flux(ext_y[:, :, :-1], ext_y[:, :, 1:], 1)
    flow_z = euler_flux(ext_z[..., :-1], ext_z[..., 1:], 2)
    updated = blocks - COURANT * (flow_x[:, 1:] - flow_x[:, :-1]) - COURANT * (flow_y[:, :, 1:] - flow_y[:, :, :-1]) - COURANT * (flow_z[..., 1:] - flow_z[..., :-1])
    edges = jnp.stack([flow_x[:, 0], flow_x[:, -1], flow_y[:, :, 0], flow_y[:, :, -1], flow_z[..., 0], flow_z[..., -1]], axis=1)
    shrunk = edges.reshape(5, 6, half_len, 2, half_len, 2).mean(axis=(3, 5))
    return (updated, shrunk)

def advance_patch(cell_data, old_faces, new_faces):
    edge_len = cell_data.shape[1]
    half_len = edge_len // 2
    blocks = cell_data.reshape(5, edge_len, edge_len, edge_len)
    first_step, flux_one = fine_step(blocks, old_faces.reshape(5, 6, half_len, half_len))
    second_step, flux_two = fine_step(first_step, (0.5 * (old_faces + new_faces)).reshape(5, 6, half_len, half_len))
    mean_flux = 0.5 * (flux_one + flux_two)
    coarse_avg = second_step.reshape(5, half_len, 2, half_len, 2, half_len, 2).mean(axis=(2, 4, 6))
    record = jnp.concatenate([coarse_avg.reshape(5, -1), mean_flux.reshape(5, -1)], axis=1)
    return (second_step.reshape(5, edge_len, edge_len * edge_len), record)

def slab_at(conserved, axis_pos, coordinate, corner):
    starts = [jnp.zeros((), jnp.int32), corner[0], corner[1], corner[2]]
    starts[axis_pos] = coordinate
    sizes = [5, PC, PC, PC]
    sizes[axis_pos] = 1
    return lax.dynamic_slice(conserved, starts, sizes).reshape(5, PC * PC)

def cycle_faces(conserved, corner, outward):
    extents = conserved.shape[1:]
    found = []
    for axis_pos in (1, 2, 3):
        corner_at = corner[axis_pos - 1]
        extent = extents[axis_pos - 1]
        if outward:
            lower_at, upper_at = (corner_at - 1, corner_at + PC)
        else:
            lower_at, upper_at = (corner_at, corner_at + PC - 1)
        found.append(slab_at(conserved, axis_pos, (lower_at % extent).astype(jnp.int32), corner))
        found.append(slab_at(conserved, axis_pos, (upper_at % extent).astype(jnp.int32), corner))
    return jnp.stack(found, axis=1)

def coarse_corrections(outer, inner, mean_flux):
    collected = []
    for face_id in range(6):
        if face_id % 2 == 0:
            coarse_flux = euler_flux(outer[:, face_id], inner[:, face_id], face_id // 2)
            collected.append(-COURANT * (mean_flux[:, face_id] - coarse_flux))
        else:
            coarse_flux = euler_flux(inner[:, face_id], outer[:, face_id], face_id // 2)
            collected.append(COURANT * (mean_flux[:, face_id] - coarse_flux))
    return jnp.stack(collected, axis=1)

def add_faces(conserved, corner, amounts):
    extents = conserved.shape[1:]
    for face_id in range(6):
        axis_pos = face_id // 2 + 1
        corner_at = corner[axis_pos - 1]
        extent = extents[axis_pos - 1]
        if face_id % 2 == 0:
            coordinate = ((corner_at - 1) % extent).astype(jnp.int32)
        else:
            coordinate = ((corner_at + PC) % extent).astype(jnp.int32)
        starts = [jnp.zeros((), jnp.int32), corner[0], corner[1], corner[2]]
        starts[axis_pos] = coordinate
        sizes = [5, PC, PC, PC]
        sizes[axis_pos] = 1
        current = lax.dynamic_slice(conserved, starts, sizes)
        conserved = lax.dynamic_update_slice(conserved, current + amounts[:, face_id].reshape(sizes), starts)
    return conserved

def coarse_advance(conserved):
    result = conserved
    for axis_pos in (1, 2, 3):
        neighbour = jnp.roll(conserved, -1, axis=axis_pos)
        fluxes = euler_flux(conserved, neighbour, axis_pos - 1)
        result = result - COURANT * (fluxes - jnp.roll(fluxes, 1, axis=axis_pos))
    return result

def reference(coarse_state, fine_state, corners, slot_patch):
    advanced = coarse_advance(coarse_state)
    lanes_x = jnp.arange(N_GX, dtype=jnp.int32)[:, None, None]
    lanes_y = jnp.arange(N_GY, dtype=jnp.int32)[None, :, None]
    lanes_s = jnp.arange(SLOTS, dtype=jnp.int32)[None, None, :]
    patch_ids = slot_patch[lanes_y, lanes_x * SLOTS + lanes_s]
    placed = corners[lanes_y, patch_ids].reshape(-1, 3)
    patches = fine_state.reshape(N_GX * N_GY * SLOTS, 5, PF, PF * PF)

    def advance_one(payload):
        cell_data, corner = payload
        return advance_patch(cell_data, cycle_faces(coarse_state, corner, True), cycle_faces(advanced, corner, True))
    fine_next, records = lax.map(advance_one, (patches, placed))

    def reflux_one(conserved, payload):
        record, corner = payload
        mean_flux = record[:, PC ** 3:].reshape(5, 6, PC * PC)
        amounts = coarse_corrections(cycle_faces(coarse_state, corner, True), cycle_faces(coarse_state, corner, False), mean_flux)
        return (add_faces(conserved, corner, amounts), None)
    refluxed, unused = lax.scan(reflux_one, advanced, (records, placed))

    def cover_one(conserved, payload):
        record, corner = payload
        starts = [jnp.zeros((), jnp.int32), corner[0], corner[1], corner[2]]
        return (lax.dynamic_update_slice(conserved, record[:, :PC ** 3].reshape(5, PC, PC, PC), starts), None)
    coarse_out, unused = lax.scan(cover_one, refluxed, (records, placed))
    return (coarse_out, fine_next.reshape(fine_state.shape))
```

```python
import functools

import jax
import jax.numpy as jnp
from jax import lax
from jax.experimental import pallas as pl
from jax.experimental.pallas import tpu as pltpu
from jax.sharding import PartitionSpec as P

F32 = jnp.float32
I32 = jnp.int32
MESH = pl.DeviceIdType.MESH
VMEM = pltpu.VMEM
SMEM = pltpu.SMEM
NGX = 16
NGY = 8
MOST = 4
PCOL = 32
YE = 48
XE = 20
LIMIT = 48 * 1024 * 1024


def lane_ids(rows=8):
    return lax.broadcasted_iota(I32, (rows, 128), 1)


def take(values, idx):
    return jnp.take_along_axis(values, idx, axis=1)


def prims(state):
    inv = 1.0 / state[0]
    vel = [state[1] * inv, state[2] * inv, state[3] * inv]
    kinetic = 0.5 * (state[1] * vel[0] + state[2] * vel[1] + state[3] * vel[2])
    pressure = 0.4 * (state[4] - kinetic)
    sound = jnp.sqrt(1.4 * pressure * inv)
    return vel, pressure, sound


def flow(state, vel, pressure, normal):
    out = [state[1 + normal], state[1] * vel, state[2] * vel, state[3] * vel, (state[4] + pressure) * vel]
    out[1 + normal] = out[1 + normal] + pressure
    return out


def side(state, normal, pre=None):
    vel, pressure, sound = prims(state) if pre is None else pre
    return state, flow(state, vel[normal], pressure, normal), jnp.abs(vel[normal]) + sound


def twice_flux(low, high):
    fastest = jnp.maximum(low[2], high[2])
    return [
        (low[1][f] + high[1][f]) - fastest * (high[0][f] - low[0][f]) for f in range(5)
    ]


def neighbours():
    gx, gy = lax.axis_index("gx"), lax.axis_index("gy")
    xs = (lax.rem(gx + NGX - 1, NGX), lax.rem(gx + 1, NGX))
    ys = (lax.rem(gy + NGY - 1, NGY), lax.rem(gy + 1, NGY))
    return gx, gy, xs, ys


def greet(devices):
    barrier = pltpu.get_barrier_semaphore()
    for device in devices:
        pl.semaphore_signal(barrier, inc=1, device_id=device, device_id_type=MESH)
    pl.semaphore_wait(barrier, len(devices))


def halo_kernel(c_ref, hx_ref, hy_ref, hc_ref, y_send, c_send, send_sem, recv_sem):
    gx, gy, xs, ys = neighbours()
    devices = [(xs[0], gy), (xs[1], gy), (gx, ys[0]), (gx, ys[1])]
    devices += [(xs[a], ys[b]) for a in range(2) for b in range(2)]
    greet(devices)
    copies = []

    def send(src, dst, number):
        copy = pltpu.make_async_remote_copy(
            src_ref=src,
            dst_ref=dst,
            send_sem=send_sem.at[number],
            recv_sem=recv_sem.at[number],
            device_id=devices[number],
            device_id_type=MESH,
        )
        copy.start()
        copies.append(copy)

    send(c_ref.at[:, pl.ds(0, 64), :], hx_ref.at[1], 0)
    send(c_ref.at[:, pl.ds(448, 64), :], hx_ref.at[0], 1)
    for end in range(2):
        for f in range(5):
            for r in range(2):
                y_send[end, f, r] = c_ref[f, pl.ds(30 * end + r, 16, stride=32), :]
        send(y_send.at[end], hy_ref.at[1 - end], 2 + end)
    c_send[...] = jnp.zeros_like(c_send)
    for a in range(2):
        for b in range(2):
            k = 2 * a + b
            for f in range(5):
                c_send[k, pl.ds(f, 1), :] = c_ref[f, pl.ds(15 * a * 32 + 31 * b, 1), :]
            send(c_send.at[k], hc_ref.at[3 - k], 4 + k)
    for copy in copies:
        copy.wait()


def halo(coarse):
    return pl.pallas_call(
        halo_kernel,
        out_shape=(
            jax.ShapeDtypeStruct((2, 5, 64, 128), F32),
            jax.ShapeDtypeStruct((2, 5, 2, 16, 128), F32),
            jax.ShapeDtypeStruct((4, 8, 128), F32),
        ),
        in_specs=[pl.BlockSpec(memory_space=VMEM)],
        out_specs=(pl.BlockSpec(memory_space=VMEM),) * 3,
        scratch_shapes=[
            VMEM((2, 5, 2, 16, 128), F32),
            VMEM((4, 8, 128), F32),
            pltpu.SemaphoreType.DMA((8,)),
            pltpu.SemaphoreType.DMA((8,)),
        ],
        compiler_params=pltpu.CompilerParams(
            collective_id=1, has_side_effects=True, vmem_limit_bytes=LIMIT
        ),
    )(coarse)


def coarse_kernel(
    corners, holders, c_ref, hx_ref, hy_ref, hc_ref,
    new_ref, pk_ref, fc_ref, tab,
    old, new, zc, first, copy_sem,
):
    me = lax.axis_index("gx")
    copies = []
    for x in range(16):
        copies.append(
            pltpu.make_async_copy(
                c_ref.at[:, pl.ds(32 * x, 32), :],
                old.at[:, pl.ds((x + 2) * YE + 8, 32), :],
                copy_sem.at[x],
            )
        )
    for number, (end, p, xi) in enumerate(((0, 0, 0), (0, 1, 1), (1, 0, 18), (1, 1, 19))):
        copies.append(
            pltpu.make_async_copy(
                hx_ref.at[end, :, pl.ds(32 * p, 32), :],
                old.at[:, pl.ds(xi * YE + 8, 32), :],
                copy_sem.at[16 + number],
            )
        )
    for copy in copies:
        copy.start()
    for f in range(5):
        for r in range(2):
            old[f, pl.ds(2 * YE + 6 + r, 16, stride=YE), :] = hy_ref[0, f, r]
            old[f, pl.ds(2 * YE + 40 + r, 16, stride=YE), :] = hy_ref[1, f, r]
        for a, xi in ((0, 1), (1, 18)):
            for b, yi in ((0, 7), (1, 40)):
                old[f, pl.ds(xi * YE + yi, 1), :] = hc_ref[2 * a + b, pl.ds(f, 1), :]

    def zero_first(b, carry):
        first[b] = 0
        return carry

    lax.fori_loop(0, NGX + 1, zero_first, 0)

    def count_one(q, carry):
        b = corners[q, 0] // 16
        first[b + 1] = first[b + 1] + 1
        return carry

    lax.fori_loop(0, PCOL, count_one, 0)

    def add_up(b, carry):
        first[b + 1] = first[b + 1] + first[b]
        return carry

    lax.fori_loop(0, NGX, add_up, 0)

    def zero_ret(i, carry):
        tab[i] = 0
        return carry

    lax.fori_loop(32, 128, zero_ret, 0)

    def slot_one(i, carry):
        q = holders[i]
        b = corners[q, 0] // 16
        row = b * MOST + q - first[b]
        tab[i] = row
        tab[32 + row] = i
        return carry

    lax.fori_loop(0, PCOL, slot_one, 0)
    mine = first[me]
    count = first[me + 1] - mine
    for r in range(MOST):
        q = jnp.minimum(mine + r, PCOL - 1)
        tab[96 + r] = lax.rem(corners[q, 1], 32)
        tab[100 + r] = corners[q, 2]
    tab[104] = count

    for copy in copies:
        copy.wait()

    lane = lane_ids()

    def advance(mid, xm, xp, ym, yp):
        pre = prims(mid)
        cx = side(mid, 0, pre)
        diff = twice_flux(cx, side(xp, 0))
        low = twice_flux(side(xm, 0), cx)
        total = [a - b for a, b in zip(diff, low)]
        cy = side(mid, 1, pre)
        up = twice_flux(cy, side(yp, 1))
        low = twice_flux(side(ym, 1), cy)
        total = [t + (a - b) for t, a, b in zip(total, up, low)]
        cz = side(mid, 2, pre)
        next_vel = pltpu.roll(pre[0][2], 127, axis=1)
        next_p = pltpu.roll(pre[1], 127, axis=1)
        next_u = [pltpu.roll(v, 127, axis=1) for v in mid]
        nz = (next_u, flow(next_u, next_vel, next_p, 2), pltpu.roll(cz[2], 127, axis=1))
        up = twice_flux(cz, nz)
        total = [t + (a - pltpu.roll(a, 1, axis=1)) for t, a in zip(total, up)]
        return [u - 0.025 * t for u, t in zip(mid, total)]

    def plane(xi, carry):
        for t in range(4):
            base = xi * YE + 8 + 8 * t

            def rows(start):
                return [old[f, pl.ds(start, 8), :] for f in range(5)]

            result = advance(rows(base), rows(base - YE), rows(base + YE), rows(base - 1), rows(base + 1))
            for f in range(5):
                new[f, pl.ds(base, 8), :] = result[f]
        return carry

    lax.fori_loop(1, 19, plane, 0)
    for yi in (7, 40):
        for half in range(2):
            base = (2 + 8 * half) * YE + yi

            def rows(start):
                return [old[f, pl.ds(start, 8, stride=YE), :] for f in range(5)]

            result = advance(rows(base), rows(base - YE), rows(base + YE), rows(base - 1), rows(base + 1))
            for f in range(5):
                new[f, pl.ds(base, 8, stride=YE), :] = result[f]
    writes = []
    for x in range(16):
        writes.append(
            pltpu.make_async_copy(
                new.at[:, pl.ds((x + 2) * YE + 8, 32), :],
                new_ref.at[:, pl.ds(32 * x, 32), :],
                copy_sem.at[x],
            )
        )
    for copy in writes:
        copy.start()

    zsel = lax.rem(lane_ids(32), 16)
    zpick = 16 * lax.rem(zsel, 8) + 15 * (zsel // 8)
    group = lane_ids(32) // 16
    for when, source in ((0, old), (1, new)):
        for f in range(5):
            for half in range(2):
                acc = None
                for x in range(8):
                    picked = take(source[f, pl.ds((2 + 8 * half + x) * YE + 8, 32), :], zpick)
                    acc = picked if acc is None else jnp.where(group == x, picked, acc)
                zc[when, f, half] = acc

    lane16 = lane_ids(16)
    is_lo = lax.rem(lane16, 32) < 16
    low_half = lax.rem(lane16, 16) < 8
    quarter = lane16 // 32
    sign = jnp.where(is_lo, 1.0, -1.0).astype(F32)

    def one_rank(r, carry):
        y0 = pl.multiple_of(tab[96 + r], 16)
        z0 = tab[100 + r]
        k = z0 // 16
        zidx = z0 + lax.rem(lane16, 16)

        def groups(source, when, outer):
            x_at = (1, 18) if outer else (2, 17)
            y_at = (y0 + 7, y0 + 24) if outer else (y0 + 8, y0 + 23)
            if outer:
                z_at = (8 + lax.rem(k + 7, 8), lax.rem(k + 1, 8))
            else:
                z_at = (k, 8 + k)
            sidx = lax.rem(lane16, 8) * 16 + jnp.where(is_lo, z_at[0], z_at[1])
            found = []
            for f in range(5):
                gx = [take(source[f, pl.ds(xi * YE + 8 + y0, 16), :], zidx) for xi in x_at]
                gy = [take(source[f, pl.ds(2 * YE + yi, 16, stride=YE), :], zidx) for yi in y_at]
                gz = [take(zc[when, f, half, pl.ds(y0, 16), :], sidx) for half in range(2)]
                found.append(
                    (
                        jnp.where(is_lo, gx[0], gx[1]),
                        jnp.where(is_lo, gy[0], gy[1]),
                        jnp.where(low_half, gz[0], gz[1]),
                    )
                )
            return found

        outer_old = groups(old, 0, True)
        outer_new = groups(new, 1, True)
        inner_old = groups(old, 0, False)

        def put(row, value):
            pk_ref[pl.ds(r * 8 + row, 16, stride=32), :] = value

        def by_quarter(a, b, c, d):
            return jnp.where(quarter == 0, a, jnp.where(quarter == 1, b, jnp.where(quarter == 2, c, d)))

        for f in range(5):
            put(f, by_quarter(*outer_old[f], outer_new[f][0]))
        put(5, by_quarter(outer_new[0][1], outer_new[0][2], outer_new[1][1], outer_new[1][2]))
        put(6, by_quarter(outer_new[2][1], outer_new[2][2], outer_new[3][1], outer_new[3][2]))
        put(7, by_quarter(outer_new[4][1], outer_new[4][2], outer_new[4][1], outer_new[4][2]))

        out = [by_quarter(*g, g[2]) for g in outer_old]
        ins = [by_quarter(*g, g[2]) for g in inner_old]

        def normal_side(state):
            vel, pressure, sound = prims(state)
            along = by_quarter(*vel, vel[2])
            flows = [
                by_quarter(state[1], state[2], state[3], state[3]),
                state[1] * along + jnp.where(quarter == 0, pressure, 0.0),
                state[2] * along + jnp.where(quarter == 1, pressure, 0.0),
                state[3] * along + jnp.where(quarter >= 2, pressure, 0.0),
                (state[4] + pressure) * along,
            ]
            return state, flows, jnp.abs(along) + sound

        a, b = normal_side(out), normal_side(ins)
        fastest = jnp.maximum(a[2], b[2]) * sign
        for f in range(5):
            fc_ref[r, f] = 0.5 * ((a[1][f] + b[1][f]) - fastest * (ins[f] - out[f]))
        return carry

    lax.fori_loop(0, MOST, one_rank, 0)
    for copy in writes:
        copy.wait()


def coarse_step(corners, holders, coarse, hx, hy, hc):
    return pl.pallas_call(
        coarse_kernel,
        out_shape=(
            jax.ShapeDtypeStruct((5, 512, 128), F32),
            jax.ShapeDtypeStruct((512, 128), F32),
            jax.ShapeDtypeStruct((MOST, 5, 16, 128), F32),
            jax.ShapeDtypeStruct((128,), I32),
        ),
        in_specs=[
            pl.BlockSpec(memory_space=SMEM),
            pl.BlockSpec(memory_space=SMEM),
            pl.BlockSpec(memory_space=pl.ANY),
            pl.BlockSpec(memory_space=pl.ANY),
            pl.BlockSpec(memory_space=VMEM),
            pl.BlockSpec(memory_space=VMEM),
        ],
        out_specs=(
            pl.BlockSpec(memory_space=pl.ANY),
            pl.BlockSpec(memory_space=VMEM),
            pl.BlockSpec(memory_space=VMEM),
            pl.BlockSpec(memory_space=SMEM),
        ),
        scratch_shapes=[
            VMEM((5, XE * YE, 128), F32),
            VMEM((5, XE * YE, 128), F32),
            VMEM((2, 5, 2, 32, 128), F32),
            SMEM((NGX + 1,), I32),
            pltpu.SemaphoreType.DMA((20,)),
        ],
        compiler_params=pltpu.CompilerParams(vmem_limit_bytes=LIMIT),
    )(corners, holders, coarse, hx, hy, hc)


def route_kernel(offset, per, tab, src_ref, out_ref, mid, sel, sem_a, sem_b, sem_c, sem_d, own_sem):
    me, gy = lax.axis_index("gx"), lax.axis_index("gy")
    others = [lax.rem(me + step, NGX) for step in range(1, NGX)]
    greet([(other, gy) for other in others])
    own = pltpu.make_async_copy(src_ref.at[me], mid.at[me], own_sem)
    own.start()
    first = []
    for number, other in enumerate(others):
        copy = pltpu.make_async_remote_copy(
            src_ref=src_ref.at[other],
            dst_ref=mid.at[me],
            send_sem=sem_a.at[number],
            recv_sem=sem_b.at[number],
            device_id=(other, gy),
            device_id_type=MESH,
        )
        copy.start()
        first.append(copy)
    own.wait()
    for copy in first:
        copy.wait()
    rows = src_ref.shape[1]

    def choose(d, carry):
        for s in range(per):
            at = tab[offset + d * per + s]
            sel[d, s] = mid[at // rows, lax.rem(at, rows)]
        return carry

    lax.fori_loop(0, NGX, choose, 0)
    own = pltpu.make_async_copy(sel.at[me], out_ref.at[me], own_sem)
    own.start()
    second = []
    for number, other in enumerate(others):
        copy = pltpu.make_async_remote_copy(
            src_ref=sel.at[other],
            dst_ref=out_ref.at[me],
            send_sem=sem_c.at[number],
            recv_sem=sem_d.at[number],
            device_id=(other, gy),
            device_id_type=MESH,
        )
        copy.start()
        second.append(copy)
    own.wait()
    for copy in second:
        copy.wait()


def route(tab, pieces, offset, per, number):
    rest = pieces.shape[2:]
    return pl.pallas_call(
        functools.partial(route_kernel, offset, per),
        out_shape=jax.ShapeDtypeStruct((NGX, per) + rest, F32),
        in_specs=[pl.BlockSpec(memory_space=SMEM), pl.BlockSpec(memory_space=VMEM)],
        out_specs=pl.BlockSpec(memory_space=VMEM),
        scratch_shapes=[VMEM(pieces.shape, F32), VMEM((NGX, per) + rest, F32)]
        + [pltpu.SemaphoreType.DMA((NGX - 1,))] * 4
        + [pltpu.SemaphoreType.DMA],
        compiler_params=pltpu.CompilerParams(
            collective_id=number, has_side_effects=True, vmem_limit_bytes=LIMIT
        ),
    )(tab, pieces)


def fine_kernel(fine_ref, got, out_ref, rec, buf, state, gp, fx, fy, fz, av, yt, fs, in_sem, out_sem):
    lane = lane_ids()
    sub = lax.broadcasted_iota(I32, (8, 128), 0)
    z = lax.rem(lane, 32)

    def copies_in(s):
        return [
            pltpu.make_async_copy(
                fine_ref.at[s, :, :, :, pl.ds(128 * k, 128)],
                buf.at[s, :, :, pl.ds(8 * k, 8), :],
                in_sem.at[s, k],
            )
            for k in range(8)
        ]

    def copies_out(s):
        return [
            pltpu.make_async_copy(
                buf.at[s, :, :, pl.ds(8 * k, 8), :],
                out_ref.at[s, :, :, :, pl.ds(128 * k, 128)],
                out_sem.at[s, k],
            )
            for k in range(8)
        ]

    for s in range(2):
        for copy in copies_in(s):
            copy.start()

    def y_up(v):
        moved = pltpu.roll(v, 96, axis=1)
        return jnp.where(lane < 96, moved, pltpu.roll(moved, 7, axis=0))

    def y_down(v):
        moved = pltpu.roll(v, 32, axis=1)
        return jnp.where(lane >= 32, moved, pltpu.roll(moved, 1, axis=0))

    def z_up(v):
        return pltpu.roll(v, 127, axis=1)

    def z_down(v):
        return pltpu.roll(v, 1, axis=1)

    y_first = (sub == 0) & (lane < 32)
    y_last = (sub == 7) & (lane >= 96)
    z_first = z == 0
    z_last = z == 31
    y_sign = jnp.where(y_last, 1.0, -1.0).astype(F32)
    z_sign = jnp.where(z_last, 1.0, -1.0).astype(F32)
    y_pick = 32 + jnp.where(lane >= 96, 16, 0) + z // 2
    z_pick = jnp.where(z_first, 64, 80)
    x_pick = z // 2
    left = lane < 64

    def along(mid, pre, normal, up, down, first, last, sign, ghost):
        cell = side(mid, normal, pre)
        shifted = [up(v) for v in mid]
        above = (
            shifted,
            flow(shifted, up(pre[0][normal]), up(pre[1]), normal),
            up(cell[2]),
        )
        inner = twice_flux(cell, above)
        fastest = jnp.maximum(cell[2], ghost[2]) * sign
        edge = [
            (cell[1][f] + ghost[1][f]) - fastest * (ghost[0][f] - mid[f]) for f in range(5)
        ]
        diff = [
            jnp.where(last, edge[f], inner[f]) - jnp.where(first, edge[f], down(inner[f]))
            for f in range(5)
        ]
        return diff, edge

    for s in range(2):
        for copy in copies_in(s):
            copy.wait()
        for x in range(32):
            for f in range(5):
                state[f, 1 + x] = buf[s, f, x // 8, pl.ds(x % 8, 8, stride=8), :]
        lane16 = lane_ids(16)
        quarter = lane16 // 32
        in32 = lax.rem(lane16, 32)

        def row(number):
            return got[pl.ds(s * 8 + number, 16, stride=16), :]

        for f in range(5):
            before = row(f)
            m = 2 * f
            after_x = take(before, 96 + in32)
            source = row(5 + m // 4)
            after_y = take(source, (m % 4) * 32 + in32)
            after_z = take(source, (m % 4 + 1) * 32 + in32)
            after = jnp.where(quarter == 0, after_x, jnp.where(quarter == 1, after_y, after_z))
            gp[0, f] = before
            gp[1, f] = 0.5 * (before + after)

        for step in range(2):
            for f in range(5):
                even = gp[step, f, pl.ds(0, 8, stride=2), :]
                odd = gp[step, f, pl.ds(1, 8, stride=2), :]
                state[f, 0] = jnp.where(left, take(even, x_pick), take(odd, x_pick))
                state[f, 33] = jnp.where(left, take(even, 16 + x_pick), take(odd, 16 + x_pick))
            ghost_low = side([state[f, 0] for f in range(5)], 0)
            plane0 = side([state[f, 1] for f in range(5)], 0)
            low_flux = twice_flux(ghost_low, plane0)
            for f in range(5):
                if step == 0:
                    fx[0, f] = low_flux[f]
                else:
                    fx[0, f] = fx[0, f] + low_flux[f]

            def pair(k, carry):
                below = list(carry)
                ghost_y, ghost_z = [], []
                for f in range(5):
                    line = gp[step, f, pl.ds(k, 1), :]
                    ghost_y.append(take(jnp.broadcast_to(line, (8, 128)), y_pick))
                    even = gp[step, f, pl.ds(0, 8, stride=2), :]
                    odd = gp[step, f, pl.ds(1, 8, stride=2), :]
                    ghost_z.append(jnp.where(left, take(even, z_pick + k), take(odd, z_pick + k)))
                ghost_y = side(ghost_y, 1)
                ghost_z = side(ghost_z, 2)
                mids = [[state[f, 1 + 2 * k + p] for f in range(5)] for p in range(3)]
                pres = [prims(mid) for mid in mids]
                sides = [side(mids[p], 0, pres[p]) for p in range(3)]
                results, edges_y, edges_z = [], [], []
                for p in range(2):
                    above = twice_flux(sides[p], sides[p + 1])
                    diff_y, edge_y = along(
                        mids[p], pres[p], 1, y_up, y_down, y_first, y_last, y_sign, ghost_y
                    )
                    diff_z, edge_z = along(
                        mids[p], pres[p], 2, z_up, z_down, z_first, z_last, z_sign, ghost_z
                    )
                    result = [
                        mids[p][f] - 0.025 * ((above[f] - below[f]) + diff_y[f] + diff_z[f])
                        for f in range(5)
                    ]
                    for f in range(5):
                        state[f, 1 + 2 * k + p] = result[f]
                    below = above
                    results.append(result)
                    edges_y.append(edge_y)
                    edges_z.append(edge_z)
                for f in range(5):
                    sum_y = edges_y[0][f] + edges_y[1][f]
                    sum_z = edges_z[0][f] + edges_z[1][f]
                    if step == 0:
                        fy[f, k] = sum_y
                        fz[f, k] = sum_z
                    else:
                        fy[f, k] = fy[f, k] + sum_y
                        fz[f, k] = fz[f, k] + sum_z
                        mean = results[0][f] + results[1][f]
                        mean = mean + pltpu.roll(mean, 96, axis=1)
                        av[f, k] = 0.125 * (mean + z_up(mean))
                return tuple(below)

            last = lax.fori_loop(0, 16, pair, tuple(low_flux))
            for f in range(5):
                if step == 0:
                    fx[1, f] = last[f]
                else:
                    fx[1, f] = fx[1, f] + last[f]
        for x in range(32):
            for f in range(5):
                buf[s, f, x // 8, pl.ds(x % 8, 8, stride=8), :] = state[f, 1 + x]
        for copy in copies_out(s):
            copy.start()
        slot_of = lax.rem(lane // 32, 2) * 2 + lax.rem(lane, 2)
        for f in range(5):
            for xq in range(4):
                packed = av[f, 4 * xq]
                for j in range(1, 4):
                    moved = pltpu.roll(av[f, 4 * xq + j], (j // 2) * 32 + j % 2, axis=1)
                    packed = jnp.where(slot_of == j, moved, packed)
                v = 4 * f + xq
                rec[pl.ds((v // 2) * 32 + s * 16 + (v % 2) * 8, 8), :] = packed
        is_lo = z < 16
        fold = 2 * lax.rem(lane, 16)
        for f in range(5):
            halves = [None, None]
            for k in range(16):
                v = fz[f, k]
                v = v + pltpu.roll(v, 96, axis=1)
                for h in range(2):
                    picked = take(v, h * 64 + jnp.where(is_lo, 0, 31))
                    halves[h] = (
                        picked if k == 0 else jnp.where(lax.rem(lane, 16) == k, picked, halves[h])
                    )
                v = fy[f, k]
                v = v + z_up(v)
                v = jnp.where(is_lo, take(v, fold), pltpu.roll(take(v, 96 + fold), 1, axis=0))
                yt[f, pl.ds(k, 1), :] = v[0:1]
            ends = []
            for end in range(2):
                v = fx[end, f]
                v = v + pltpu.roll(v, 96, axis=1)
                ends.append(v + z_up(v))
            for h in range(2):
                picked = jnp.where(is_lo, take(ends[0], h * 64 + fold), take(ends[1], h * 64 + fold))
                fs[f, pl.ds(h, 8, stride=2), :] = jnp.where(lane < 32, picked, halves[h])
            whole = jnp.where((lane16 >= 32) & (lane16 < 64), yt[f], fs[f])
            rec[pl.ds((10 + f) * 32 + s * 16, 16), :] = whole * 0.0625
            if f == 0:
                rec[pl.ds(15 * 32 + s * 16, 16), :] = jnp.zeros((16, 128), F32)
    for s in range(2):
        for copy in copies_out(s):
            copy.wait()


def fine_steps(fine, got):
    return pl.pallas_call(
        fine_kernel,
        out_shape=(
            jax.ShapeDtypeStruct((2, 5, 4, 8, 1024), F32),
            jax.ShapeDtypeStruct((512, 128), F32),
        ),
        in_specs=[pl.BlockSpec(memory_space=pl.ANY), pl.BlockSpec(memory_space=VMEM)],
        out_specs=(pl.BlockSpec(memory_space=pl.ANY), pl.BlockSpec(memory_space=VMEM)),
        scratch_shapes=[
            VMEM((2, 5, 4, 64, 128), F32),
            VMEM((5, 34, 8, 128), F32),
            VMEM((2, 5, 16, 128), F32),
            VMEM((2, 5, 8, 128), F32),
            VMEM((5, 16, 8, 128), F32),
            VMEM((5, 16, 8, 128), F32),
            VMEM((5, 16, 8, 128), F32),
            VMEM((5, 16, 128), F32),
            VMEM((5, 16, 128), F32),
            pltpu.SemaphoreType.DMA((2, 8)),
            pltpu.SemaphoreType.DMA((2, 8)),
        ],
        compiler_params=pltpu.CompilerParams(vmem_limit_bytes=LIMIT),
    )(fine, got)


def amounts_kernel(tab, back, fc_ref, am_ref, xs_ref, ys_ref):
    lane16 = lane_ids(16)
    sign = jnp.where(lax.rem(lane16, 32) < 16, -0.05, 0.05).astype(F32)
    xs_ref[...] = jnp.zeros_like(xs_ref)
    ys_ref[...] = jnp.zeros_like(ys_ref)
    count = tab[104]
    for r in range(MOST):

        @pl.when(r < count)
        def _():
            y0 = pl.multiple_of(tab[96 + r], 16)
            z0 = tab[100 + r]
            inside = (lane16 >= z0) & (lane16 < z0 + 16)
            at = lax.rem(lane16 - z0 + 128, 16)
            for f in range(5):
                value = sign * (back[pl.ds((10 + f) * 64 + r * 16, 16), :] - fc_ref[r, f])
                am_ref[r, f] = value
                for end in range(2):
                    picked = jnp.where(inside, take(value, at + 16 * end), 0.0)
                    xs_ref[end, f, pl.ds(y0, 16), :] = xs_ref[end, f, pl.ds(y0, 16), :] + picked
                    picked = jnp.where(inside, take(value, at + 32 + 16 * end), 0.0)
                    which = y0 // 16 + 2 * end
                    ys_ref[which, f] = ys_ref[which, f] + picked


def amounts(tab, back, fc):
    return pl.pallas_call(
        amounts_kernel,
        out_shape=(
            jax.ShapeDtypeStruct((MOST, 5, 16, 128), F32),
            jax.ShapeDtypeStruct((2, 5, 32, 128), F32),
            jax.ShapeDtypeStruct((4, 5, 16, 128), F32),
        ),
        in_specs=[
            pl.BlockSpec(memory_space=SMEM),
            pl.BlockSpec(memory_space=VMEM),
            pl.BlockSpec(memory_space=VMEM),
        ],
        out_specs=(pl.BlockSpec(memory_space=VMEM),) * 3,
        compiler_params=pltpu.CompilerParams(vmem_limit_bytes=LIMIT),
    )(tab, back, fc)


def swap_kernel(xs_ref, ys_ref, xa_ref, ya_ref, send_sem, recv_sem):
    gx, gy, xs, ys = neighbours()
    devices = [(xs[0], gy), (xs[1], gy), (gx, ys[0]), (gx, ys[1])]
    greet(devices)
    pairs = [
        (xs_ref.at[0], xa_ref.at[1]),
        (xs_ref.at[1], xa_ref.at[0]),
        (ys_ref.at[0], ya_ref.at[1]),
        (ys_ref.at[3], ya_ref.at[0]),
    ]
    copies = []
    for number, (src, dst) in enumerate(pairs):
        copy = pltpu.make_async_remote_copy(
            src_ref=src,
            dst_ref=dst,
            send_sem=send_sem.at[number],
            recv_sem=recv_sem.at[number],
            device_id=devices[number],
            device_id_type=MESH,
        )
        copy.start()
        copies.append(copy)
    for copy in copies:
        copy.wait()


def swap(xs, ys):
    return pl.pallas_call(
        swap_kernel,
        out_shape=(
            jax.ShapeDtypeStruct((2, 5, 32, 128), F32),
            jax.ShapeDtypeStruct((2, 5, 16, 128), F32),
        ),
        in_specs=[pl.BlockSpec(memory_space=VMEM)] * 2,
        out_specs=(pl.BlockSpec(memory_space=VMEM),) * 2,
        scratch_shapes=[pltpu.SemaphoreType.DMA((4,)), pltpu.SemaphoreType.DMA((4,))],
        compiler_params=pltpu.CompilerParams(
            collective_id=4, has_side_effects=True, vmem_limit_bytes=LIMIT
        ),
    )(xs, ys)


def final_kernel(tab, new_ref, back, am_ref, ys_ref, xa_ref, ya_ref, out_ref):
    lane = lane_ids()
    lane16 = lane_ids(16)
    out_ref[...] = new_ref[...]
    for f in range(5):
        out_ref[f, pl.ds(0, 32), :] = out_ref[f, pl.ds(0, 32), :] + xa_ref[0, f]
        out_ref[f, pl.ds(480, 32), :] = out_ref[f, pl.ds(480, 32), :] + xa_ref[1, f]
        for y, values in ((0, ya_ref[0, f]), (31, ya_ref[1, f]), (15, ys_ref[1, f]), (16, ys_ref[2, f])):
            out_ref[f, pl.ds(y, 16, stride=32), :] = out_ref[f, pl.ds(y, 16, stride=32), :] + values
    count = tab[104]

    def one_rank(r, carry):
        y0 = pl.multiple_of(tab[96 + r], 16)
        z0 = tab[100 + r]
        low, high = lax.rem(z0 + 127, 128), lax.rem(z0 + 16, 128)
        touched = (lane16 == low) | (lane16 == high)
        at = jnp.where(lane16 == low, 64, 80)
        for f in range(5):
            value = am_ref[r, f]
            for x in range(16):
                rows = pl.ds(32 * x + y0, 16)
                here = out_ref[f, rows, :]
                out_ref[f, rows, :] = jnp.where(touched, here + take(value, at + x), here)
        return carry

    lax.fori_loop(0, count, one_rank, 0)

    def cover(r, carry):
        y0 = pl.multiple_of(tab[96 + r], 16)
        z0 = tab[100 + r]
        inside = (lane >= z0) & (lane < z0 + 16)
        at = 2 * lax.rem(lane - z0 + 128, 16)
        for f in range(5):
            for xq in range(4):
                v = 4 * f + xq
                packed = back[pl.ds((v // 2) * 64 + r * 16 + (v % 2) * 8, 8), :]
                for j in range(4):
                    for h in range(2):
                        rows = pl.ds(32 * (4 * xq + j) + y0 + h, 8, stride=2)
                        picked = take(packed, at + h * 64 + (j // 2) * 32 + j % 2)
                        out_ref[f, rows, :] = jnp.where(inside, picked, out_ref[f, rows, :])
        return carry

    lax.fori_loop(0, count, cover, 0)


def final(tab, new, back, am, ys, xa, ya):
    return pl.pallas_call(
        final_kernel,
        out_shape=jax.ShapeDtypeStruct((5, 512, 128), F32),
        in_specs=[pl.BlockSpec(memory_space=SMEM)] + [pl.BlockSpec(memory_space=VMEM)] * 6,
        out_specs=pl.BlockSpec(memory_space=VMEM),
        compiler_params=pltpu.CompilerParams(vmem_limit_bytes=LIMIT),
    )(tab, new, back, am, ys, xa, ya)


def per_device(coarse_state, fine_state, corners, slot_patch):
    coarse = coarse_state.reshape(5, 512, 128)
    hx, hy, hc = halo(coarse)
    new, pk, fc, tab = coarse_step(corners[0], slot_patch[0], coarse, hx, hy, hc)
    got = route(tab, pk.reshape(NGX, MOST, 8, 128), 0, 2, 2)
    fine_next, rec = fine_steps(fine_state.reshape(2, 5, 4, 8, 1024), got.reshape(256, 128))
    back = route(tab, rec.reshape(NGX, 2, 16, 128), 32, MOST, 3).reshape(1024, 128)
    am, xs, ys = amounts(tab, back, fc)
    xa, ya = swap(xs, ys)
    out = final(tab, new, back, am, ys, xa, ya)
    return out.reshape(coarse_state.shape), fine_next.reshape(fine_state.shape)


def solution(mesh):
    placed = (
        P(None, "gx", "gy", None),
        P("gx", "gy", None, None, None, None),
        P("gy", None, None),
        P("gy", None),
    )
    return jax.shard_map(
        per_device,
        mesh=mesh,
        in_specs=placed,
        out_specs=(P(None, "gx", "gy", None), P("gx", "gy", None, None, None, None)),
        check_vma=False,
    )
```

```python
import functools

import jax
import jax.numpy as jnp
from jax import lax
from jax.experimental import pallas as pl
from jax.experimental.pallas import tpu as pltpu
from jax.sharding import PartitionSpec as P

F32 = jnp.float32
I32 = jnp.int32
MESH = pl.DeviceIdType.MESH
VMEM = pltpu.VMEM
SMEM = pltpu.SMEM
NGX = 16
NGY = 8
MOST = 4
PCOL = 32
YE = 48
XE = 20
LIMIT = 48 * 1024 * 1024


def lane_ids(rows=8):
    return lax.broadcasted_iota(I32, (rows, 128), 1)


def take(values, idx):
    return jnp.take_along_axis(values, idx, axis=1)


def prims(state):
    inv = 1.0 / state[0]
    vel = [state[1] * inv, state[2] * inv, state[3] * inv]
    kinetic = 0.5 * (state[1] * vel[0] + state[2] * vel[1] + state[3] * vel[2])
    pressure = 0.4 * (state[4] - kinetic)
    sound = jnp.sqrt(1.4 * pressure * inv)
    return vel, pressure, sound


def flow(state, vel, pressure, normal):
    out = [state[1 + normal], state[1] * vel, state[2] * vel, state[3] * vel, (state[4] + pressure) * vel]
    out[1 + normal] = out[1 + normal] + pressure
    return out


def side(state, normal, pre=None):
    vel, pressure, sound = prims(state) if pre is None else pre
    return state, flow(state, vel[normal], pressure, normal), jnp.abs(vel[normal]) + sound


def twice_flux(low, high):
    fastest = jnp.maximum(low[2], high[2])
    return [
        (low[1][f] + high[1][f]) - fastest * (high[0][f] - low[0][f]) for f in range(5)
    ]


def neighbours():
    gx, gy = lax.axis_index("gx"), lax.axis_index("gy")
    xs = (lax.rem(gx + NGX - 1, NGX), lax.rem(gx + 1, NGX))
    ys = (lax.rem(gy + NGY - 1, NGY), lax.rem(gy + 1, NGY))
    return gx, gy, xs, ys


def greet(devices):
    barrier = pltpu.get_barrier_semaphore()
    for device in devices:
        pl.semaphore_signal(barrier, inc=1, device_id=device, device_id_type=MESH)
    pl.semaphore_wait(barrier, len(devices))


def halo_kernel(c_ref, hx_ref, hy_ref, hc_ref, y_send, c_send, send_sem, recv_sem):
    gx, gy, xs, ys = neighbours()
    devices = [(xs[0], gy), (xs[1], gy), (gx, ys[0]), (gx, ys[1])]
    devices += [(xs[a], ys[b]) for a in range(2) for b in range(2)]
    greet(devices)
    copies = []

    def send(src, dst, number):
        copy = pltpu.make_async_remote_copy(
            src_ref=src,
            dst_ref=dst,
            send_sem=send_sem.at[number],
            recv_sem=recv_sem.at[number],
            device_id=devices[number],
            device_id_type=MESH,
        )
        copy.start()
        copies.append(copy)

    send(c_ref.at[:, pl.ds(0, 64), :], hx_ref.at[1], 0)
    send(c_ref.at[:, pl.ds(448, 64), :], hx_ref.at[0], 1)
    for end in range(2):
        for f in range(5):
            for r in range(2):
                y_send[end, f, r] = c_ref[f, pl.ds(30 * end + r, 16, stride=32), :]
        send(y_send.at[end], hy_ref.at[1 - end], 2 + end)
    c_send[...] = jnp.zeros_like(c_send)
    for a in range(2):
        for b in range(2):
            k = 2 * a + b
            for f in range(5):
                c_send[k, pl.ds(f, 1), :] = c_ref[f, pl.ds(15 * a * 32 + 31 * b, 1), :]
            send(c_send.at[k], hc_ref.at[3 - k], 4 + k)
    for copy in copies:
        copy.wait()


def halo(coarse):
    return pl.pallas_call(
        halo_kernel,
        out_shape=(
            jax.ShapeDtypeStruct((2, 5, 64, 128), F32),
            jax.ShapeDtypeStruct((2, 5, 2, 16, 128), F32),
            jax.ShapeDtypeStruct((4, 8, 128), F32),
        ),
        in_specs=[pl.BlockSpec(memory_space=VMEM)],
        out_specs=(pl.BlockSpec(memory_space=VMEM),) * 3,
        scratch_shapes=[
            VMEM((2, 5, 2, 16, 128), F32),
            VMEM((4, 8, 128), F32),
            pltpu.SemaphoreType.DMA((8,)),
            pltpu.SemaphoreType.DMA((8,)),
        ],
        compiler_params=pltpu.CompilerParams(
            collective_id=1, has_side_effects=True, vmem_limit_bytes=LIMIT
        ),
    )(coarse)


def coarse_kernel(
    corners, holders, c_ref, hx_ref, hy_ref, hc_ref,
    new_ref, pk_ref, fc_ref, tab,
    old, new, zc, first, copy_sem,
):
    me = lax.axis_index("gx")
    copies = []
    for x in range(16):
        copies.append(
            pltpu.make_async_copy(
                c_ref.at[:, pl.ds(32 * x, 32), :],
                old.at[:, pl.ds((x + 2) * YE + 8, 32), :],
                copy_sem.at[x],
            )
        )
    for number, (end, p, xi) in enumerate(((0, 0, 0), (0, 1, 1), (1, 0, 18), (1, 1, 19))):
        copies.append(
            pltpu.make_async_copy(
                hx_ref.at[end, :, pl.ds(32 * p, 32), :],
                old.at[:, pl.ds(xi * YE + 8, 32), :],
                copy_sem.at[16 + number],
            )
        )
    for copy in copies:
        copy.start()
    for f in range(5):
        for r in range(2):
            old[f, pl.ds(2 * YE + 6 + r, 16, stride=YE), :] = hy_ref[0, f, r]
            old[f, pl.ds(2 * YE + 40 + r, 16, stride=YE), :] = hy_ref[1, f, r]
        for a, xi in ((0, 1), (1, 18)):
            for b, yi in ((0, 7), (1, 40)):
                old[f, pl.ds(xi * YE + yi, 1), :] = hc_ref[2 * a + b, pl.ds(f, 1), :]

    def zero_first(b, carry):
        first[b] = 0
        return carry

    lax.fori_loop(0, NGX + 1, zero_first, 0)

    def count_one(q, carry):
        b = corners[q, 0] // 16
        first[b + 1] = first[b + 1] + 1
        return carry

    lax.fori_loop(0, PCOL, count_one, 0)

    def add_up(b, carry):
        first[b + 1] = first[b + 1] + first[b]
        return carry

    lax.fori_loop(0, NGX, add_up, 0)

    def zero_ret(i, carry):
        tab[i] = 0
        return carry

    lax.fori_loop(32, 128, zero_ret, 0)

    def slot_one(i, carry):
        q = holders[i]
        b = corners[q, 0] // 16
        row = b * MOST + q - first[b]
        tab[i] = row
        tab[32 + row] = i
        return carry

    lax.fori_loop(0, PCOL, slot_one, 0)
    mine = first[me]
    count = first[me + 1] - mine
    for r in range(MOST):
        q = jnp.minimum(mine + r, PCOL - 1)
        tab[96 + r] = lax.rem(corners[q, 1], 32)
        tab[100 + r] = corners[q, 2]
    tab[104] = count

    for copy in copies:
        copy.wait()

    lane = lane_ids()

    def advance(mid, xm, xp, ym, yp):
        pre = prims(mid)
        cx = side(mid, 0, pre)
        diff = twice_flux(cx, side(xp, 0))
        low = twice_flux(side(xm, 0), cx)
        total = [a - b for a, b in zip(diff, low)]
        cy = side(mid, 1, pre)
        up = twice_flux(cy, side(yp, 1))
        low = twice_flux(side(ym, 1), cy)
        total = [t + (a - b) for t, a, b in zip(total, up, low)]
        cz = side(mid, 2, pre)
        next_vel = pltpu.roll(pre[0][2], 127, axis=1)
        next_p = pltpu.roll(pre[1], 127, axis=1)
        next_u = [pltpu.roll(v, 127, axis=1) for v in mid]
        nz = (next_u, flow(next_u, next_vel, next_p, 2), pltpu.roll(cz[2], 127, axis=1))
        up = twice_flux(cz, nz)
        total = [t + (a - pltpu.roll(a, 1, axis=1)) for t, a in zip(total, up)]
        return [u - 0.025 * t for u, t in zip(mid, total)]

    def plane(xi, carry):
        for t in range(4):
            base = xi * YE + 8 + 8 * t

            def rows(start):
                return [old[f, pl.ds(start, 8), :] for f in range(5)]

            result = advance(rows(base), rows(base - YE), rows(base + YE), rows(base - 1), rows(base + 1))
            for f in range(5):
                new[f, pl.ds(base, 8), :] = result[f]
        return carry

    lax.fori_loop(1, 19, plane, 0)
    for yi in (7, 40):
        for half in range(2):
            base = (2 + 8 * half) * YE + yi

            def rows(start):
                return [old[f, pl.ds(start, 8, stride=YE), :] for f in range(5)]

            result = advance(rows(base), rows(base - YE), rows(base + YE), rows(base - 1), rows(base + 1))
            for f in range(5):
                new[f, pl.ds(base, 8, stride=YE), :] = result[f]
    writes = []
    for x in range(16):
        writes.append(
            pltpu.make_async_copy(
                new.at[:, pl.ds((x + 2) * YE + 8, 32), :],
                new_ref.at[:, pl.ds(32 * x, 32), :],
                copy_sem.at[x],
            )
        )
    for copy in writes:
        copy.start()

    zsel = lax.rem(lane_ids(32), 16)
    zpick = 16 * lax.rem(zsel, 8) + 15 * (zsel // 8)
    group = lane_ids(32) // 16
    for when, source in ((0, old), (1, new)):
        for f in range(5):
            for half in range(2):
                acc = None
                for x in range(8):
                    picked = take(source[f, pl.ds((2 + 8 * half + x) * YE + 8, 32), :], zpick)
                    acc = picked if acc is None else jnp.where(group == x, picked, acc)
                zc[when, f, half] = acc

    lane16 = lane_ids(16)
    is_lo = lax.rem(lane16, 32) < 16
    low_half = lax.rem(lane16, 16) < 8
    quarter = lane16 // 32
    sign = jnp.where(is_lo, 1.0, -1.0).astype(F32)

    def one_rank(r, carry):
        y0 = pl.multiple_of(tab[96 + r], 16)
        z0 = tab[100 + r]
        k = z0 // 16
        zidx = z0 + lax.rem(lane16, 16)

        def groups(source, when, outer):
            x_at = (1, 18) if outer else (2, 17)
            y_at = (y0 + 7, y0 + 24) if outer else (y0 + 8, y0 + 23)
            if outer:
                z_at = (8 + lax.rem(k + 7, 8), lax.rem(k + 1, 8))
            else:
                z_at = (k, 8 + k)
            sidx = lax.rem(lane16, 8) * 16 + jnp.where(is_lo, z_at[0], z_at[1])
            found = []
            for f in range(5):
                gx = [take(source[f, pl.ds(xi * YE + 8 + y0, 16), :], zidx) for xi in x_at]
                gy = [take(source[f, pl.ds(2 * YE + yi, 16, stride=YE), :], zidx) for yi in y_at]
                gz = [take(zc[when, f, half, pl.ds(y0, 16), :], sidx) for half in range(2)]
                found.append(
                    (
                        jnp.where(is_lo, gx[0], gx[1]),
                        jnp.where(is_lo, gy[0], gy[1]),
                        jnp.where(low_half, gz[0], gz[1]),
                    )
                )
            return found

        outer_old = groups(old, 0, True)
        outer_new = groups(new, 1, True)
        inner_old = groups(old, 0, False)

        def put(row, value):
            pk_ref[pl.ds(r * 8 + row, 16, stride=32), :] = value

        def by_quarter(a, b, c, d):
            return jnp.where(quarter == 0, a, jnp.where(quarter == 1, b, jnp.where(quarter == 2, c, d)))

        for f in range(5):
            put(f, by_quarter(*outer_old[f], outer_new[f][0]))
        put(5, by_quarter(outer_new[0][1], outer_new[0][2], outer_new[1][1], outer_new[1][2]))
        put(6, by_quarter(outer_new[2][1], outer_new[2][2], outer_new[3][1], outer_new[3][2]))
        put(7, by_quarter(outer_new[4][1], outer_new[4][2], outer_new[4][1], outer_new[4][2]))

        out = [by_quarter(*g, g[2]) for g in outer_old]
        ins = [by_quarter(*g, g[2]) for g in inner_old]

        def normal_side(state):
            vel, pressure, sound = prims(state)
            along = by_quarter(*vel, vel[2])
            flows = [
                by_quarter(state[1], state[2], state[3], state[3]),
                state[1] * along + jnp.where(quarter == 0, pressure, 0.0),
                state[2] * along + jnp.where(quarter == 1, pressure, 0.0),
                state[3] * along + jnp.where(quarter >= 2, pressure, 0.0),
                (state[4] + pressure) * along,
            ]
            return state, flows, jnp.abs(along) + sound

        a, b = normal_side(out), normal_side(ins)
        fastest = jnp.maximum(a[2], b[2]) * sign
        for f in range(5):
            fc_ref[r, f] = 0.5 * ((a[1][f] + b[1][f]) - fastest * (ins[f] - out[f]))
        return carry

    lax.fori_loop(0, MOST, one_rank, 0)
    for copy in writes:
        copy.wait()


def coarse_step(corners, holders, coarse, hx, hy, hc):
    return pl.pallas_call(
        coarse_kernel,
        out_shape=(
            jax.ShapeDtypeStruct((5, 512, 128), F32),
            jax.ShapeDtypeStruct((512, 128), F32),
            jax.ShapeDtypeStruct((MOST, 5, 16, 128), F32),
            jax.ShapeDtypeStruct((128,), I32),
        ),
        in_specs=[
            pl.BlockSpec(memory_space=SMEM),
            pl.BlockSpec(memory_space=SMEM),
            pl.BlockSpec(memory_space=pl.ANY),
            pl.BlockSpec(memory_space=pl.ANY),
            pl.BlockSpec(memory_space=VMEM),
            pl.BlockSpec(memory_space=VMEM),
        ],
        out_specs=(
            pl.BlockSpec(memory_space=pl.ANY),
            pl.BlockSpec(memory_space=VMEM),
            pl.BlockSpec(memory_space=VMEM),
            pl.BlockSpec(memory_space=SMEM),
        ),
        scratch_shapes=[
            VMEM((5, XE * YE, 128), F32),
            VMEM((5, XE * YE, 128), F32),
            VMEM((2, 5, 2, 32, 128), F32),
            SMEM((NGX + 1,), I32),
            pltpu.SemaphoreType.DMA((20,)),
        ],
        compiler_params=pltpu.CompilerParams(vmem_limit_bytes=LIMIT),
    )(corners, holders, coarse, hx, hy, hc)


def route_kernel(offset, per, tab, src_ref, out_ref, mid, sel, sem_a, sem_b, sem_c, sem_d, own_sem):
    me, gy = lax.axis_index("gx"), lax.axis_index("gy")
    others = [lax.rem(me + step, NGX) for step in range(1, NGX)]
    greet([(other, gy) for other in others])
    own = pltpu.make_async_copy(src_ref.at[me], mid.at[me], own_sem)
    own.start()
    first = []
    for number, other in enumerate(others):
        copy = pltpu.make_async_remote_copy(
            src_ref=src_ref.at[other],
            dst_ref=mid.at[me],
            send_sem=sem_a.at[number],
            recv_sem=sem_b.at[number],
            device_id=(other, gy),
            device_id_type=MESH,
        )
        copy.start()
        first.append(copy)
    own.wait()
    for copy in first:
        copy.wait()
    rows = src_ref.shape[1]

    def choose(d, carry):
        for s in range(per):
            at = tab[offset + d * per + s]
            sel[d, s] = mid[at // rows, lax.rem(at, rows)]
        return carry

    lax.fori_loop(0, NGX, choose, 0)
    own = pltpu.make_async_copy(sel.at[me], out_ref.at[me], own_sem)
    own.start()
    second = []
    for number, other in enumerate(others):
        copy = pltpu.make_async_remote_copy(
            src_ref=sel.at[other],
            dst_ref=out_ref.at[me],
            send_sem=sem_c.at[number],
            recv_sem=sem_d.at[number],
            device_id=(other, gy),
            device_id_type=MESH,
        )
        copy.start()
        second.append(copy)
    own.wait()
    for copy in second:
        copy.wait()


def route(tab, pieces, offset, per, number):
    rest = pieces.shape[2:]
    return pl.pallas_call(
        functools.partial(route_kernel, offset, per),
        out_shape=jax.ShapeDtypeStruct((NGX, per) + rest, F32),
        in_specs=[pl.BlockSpec(memory_space=SMEM), pl.BlockSpec(memory_space=VMEM)],
        out_specs=pl.BlockSpec(memory_space=VMEM),
        scratch_shapes=[VMEM(pieces.shape, F32), VMEM((NGX, per) + rest, F32)]
        + [pltpu.SemaphoreType.DMA((NGX - 1,))] * 4
        + [pltpu.SemaphoreType.DMA],
        compiler_params=pltpu.CompilerParams(
            collective_id=number, has_side_effects=True, vmem_limit_bytes=LIMIT
        ),
    )(tab, pieces)


def fine_kernel(fine_ref, got, out_ref, rec, buf, state, gp, gx, gy, gz, fx, fy, fz, fy_low, fy_high, av, fs, in_sem, out_sem):
    lane = lane_ids()
    sub = lax.broadcasted_iota(I32, (8, 128), 0)
    z = lax.rem(lane, 32)

    def copies_in(s):
        return [
            pltpu.make_async_copy(
                fine_ref.at[s, :, :, :, pl.ds(128 * k, 128)],
                buf.at[s, :, :, pl.ds(8 * k, 8), :],
                in_sem.at[s, k],
            )
            for k in range(8)
        ]

    def copies_out(s):
        return [
            pltpu.make_async_copy(
                buf.at[s, :, :, pl.ds(8 * k, 8), :],
                out_ref.at[s, :, :, :, pl.ds(128 * k, 128)],
                out_sem.at[s, k],
            )
            for k in range(8)
        ]

    for s in range(2):
        for copy in copies_in(s):
            copy.start()

    def y_up(v):
        moved = pltpu.roll(v, 96, axis=1)
        return jnp.where(lane < 96, moved, pltpu.roll(moved, 7, axis=0))

    def y_down(v):
        moved = pltpu.roll(v, 32, axis=1)
        return jnp.where(lane >= 32, moved, pltpu.roll(moved, 1, axis=0))

    def z_up(v):
        return pltpu.roll(v, 127, axis=1)

    def z_down(v):
        return pltpu.roll(v, 1, axis=1)

    y_first = (sub == 0) & (lane < 32)
    y_last = (sub == 7) & (lane >= 96)
    z_first = z == 0
    z_last = z == 31
    y_sign = jnp.where(y_last, 1.0, -1.0).astype(F32)
    z_sign = jnp.where(z_last, 1.0, -1.0).astype(F32)
    y_pick = 32 + jnp.where(lane >= 96, 16, 0) + z // 2
    z_pick = jnp.where(z_first, 64, 80)
    x_pick = z // 2
    left = lane < 64

    def along(mid, pre, normal, up, down, first, last, sign, ghost):
        cell = side(mid, normal, pre)
        shifted = [up(v) for v in mid]
        above = (
            shifted,
            flow(shifted, up(pre[0][normal]), up(pre[1]), normal),
            up(cell[2]),
        )
        inner = twice_flux(cell, above)
        fastest = jnp.maximum(cell[2], ghost[2]) * sign
        edge = [
            (cell[1][f] + ghost[1][f]) - fastest * (ghost[0][f] - mid[f]) for f in range(5)
        ]
        diff = [
            jnp.where(last, edge[f], inner[f]) - jnp.where(first, edge[f], down(inner[f]))
            for f in range(5)
        ]
        return diff, edge

    lane16 = lane_ids(16)
    quarter = lane16 // 32
    in32 = lax.rem(lane16, 32)
    for s in range(2):
        rows = [got[pl.ds(s * 8 + number, 16, stride=16), :] for number in range(8)]
        for f in range(5):
            m = 2 * f
            after_x = take(rows[f], 96 + in32)
            source = rows[5 + m // 4]
            after_y = take(source, (m % 4) * 32 + in32)
            after_z = take(source, (m % 4 + 1) * 32 + in32)
            after = jnp.where(quarter == 0, after_x, jnp.where(quarter == 1, after_y, after_z))
            gp[s, 0, f] = rows[f]
            gp[s, 1, f] = 0.5 * (rows[f] + after)
        for step in range(2):
            for f in range(5):
                even = gp[s, step, f, pl.ds(0, 8, stride=2), :]
                odd = gp[s, step, f, pl.ds(1, 8, stride=2), :]
                for end in range(2):
                    picks = [take(v, 16 * end + x_pick) for v in (even, odd)]
                    gx[s, step, f, end] = jnp.where(left, picks[0], picks[1])
                spread = take(gp[s, step, f], jnp.broadcast_to(y_pick[0:1], (16, 128)))
                for k in range(16):
                    picks = [take(v, z_pick + k) for v in (even, odd)]
                    gz[s, step, f, k] = jnp.where(left, picks[0], picks[1])
                    gy[s, step, f, k] = jnp.broadcast_to(spread[k : k + 1], (8, 128))
    for s in range(2):
        for copy in copies_in(s):
            copy.wait()
        for x in range(32):
            for f in range(5):
                state[s, f, x] = buf[s, f, x // 8, pl.ds(x % 8, 8, stride=8), :]

    def one_pair(s, step, k, below):
        ghost_y = [gy[s, step, f, k] for f in range(5)]
        ghost_z = [gz[s, step, f, k] for f in range(5)]
        mids = [[state[s, f, 2 * k + p] for f in range(5)] for p in range(3)]
        old_y = [fy[s, f, k] for f in range(5)] if step else None
        old_z = [fz[s, f, k] for f in range(5)] if step else None
        ghost_y = side(ghost_y, 1)
        ghost_z = side(ghost_z, 2)
        pres = [prims(mid) for mid in mids]
        sides = [side(mids[p], 0, pres[p]) for p in range(3)]
        results, edges_y, edges_z = [], [], []
        for p in range(2):
            above = twice_flux(sides[p], sides[p + 1])
            diff_y, edge_y = along(
                mids[p], pres[p], 1, y_up, y_down, y_first, y_last, y_sign, ghost_y
            )
            diff_z, edge_z = along(
                mids[p], pres[p], 2, z_up, z_down, z_first, z_last, z_sign, ghost_z
            )
            results.append(
                [
                    mids[p][f] - 0.025 * ((above[f] - below[f]) + diff_y[f] + diff_z[f])
                    for f in range(5)
                ]
            )
            below = above
            edges_y.append(edge_y)
            edges_z.append(edge_z)
        sum_y = [edges_y[0][f] + edges_y[1][f] for f in range(5)]
        sum_z = [edges_z[0][f] + edges_z[1][f] for f in range(5)]
        if step == 0:
            return below, results, sum_y, sum_z, None
        sum_y = [a + b for a, b in zip(sum_y, old_y)]
        sum_z = [a + b for a, b in zip(sum_z, old_z)]
        means = []
        for f in range(5):
            mean = results[0][f] + results[1][f]
            mean = mean + pltpu.roll(mean, 96, axis=1)
            means.append(0.125 * (mean + z_up(mean)))
        return below, results, sum_y, sum_z, means

    for step in range(2):
        starts = []
        for s in range(2):
            for f in range(5):
                state[s, f, 32] = gx[s, step, f, 1]
            ghost_low = side([gx[s, step, f, 0] for f in range(5)], 0)
            plane0 = side([state[s, f, 0] for f in range(5)], 0)
            starts.append(twice_flux(ghost_low, plane0))

        def pairs(k, carry):
            found = [one_pair(s, step, k, carry[s]) for s in range(2)]
            for s in range(2):
                below, results, sum_y, sum_z, means = found[s]
                for f in range(5):
                    state[s, f, 2 * k] = results[0][f]
                    state[s, f, 1 + 2 * k] = results[1][f]
                    fy[s, f, k] = sum_y[f]
                    fz[s, f, k] = sum_z[f]
                    if step:
                        av[s, f, k] = means[f]
            return found[0][0], found[1][0]

        ends = lax.fori_loop(0, 16, pairs, tuple(starts), unroll=2)
        for s in range(2):
            for f in range(5):
                if step == 0:
                    fx[s, 0, f] = starts[s][f]
                    fx[s, 1, f] = ends[s][f]
                else:
                    fx[s, 0, f] = fx[s, 0, f] + starts[s][f]
                    fx[s, 1, f] = fx[s, 1, f] + ends[s][f]

    for s in range(2):
        for x in range(32):
            for f in range(5):
                buf[s, f, x // 8, pl.ds(x % 8, 8, stride=8), :] = state[s, f, x]
        for copy in copies_out(s):
            copy.start()
    is_lo = z < 16
    fold = 2 * lax.rem(lane, 16)
    slot_of = lax.rem(lane // 32, 2) * 2 + lax.rem(lane, 2)
    half_lane = lax.rem(lane, 64)
    z_place = jnp.where(half_lane < 31, half_lane, half_lane - 31)
    for s in range(2):
        for f in range(5):
            loaded = [av[s, f, k] for k in range(16)]
            for xq in range(4):
                packed = loaded[4 * xq]
                for j in range(1, 4):
                    moved = pltpu.roll(loaded[4 * xq + j], (j // 2) * 32 + j % 2, axis=1)
                    packed = jnp.where(slot_of == j, moved, packed)
                v = 4 * f + xq
                rec[pl.ds((v // 2) * 32 + s * 16 + (v % 2) * 8, 8), :] = packed
            loaded = [fz[s, f, k] for k in range(16)]
            packed = None
            for k in range(16):
                v = loaded[k] + pltpu.roll(loaded[k], 96, axis=1)
                if k == 0:
                    packed = v
                else:
                    packed = jnp.where(z_place == k, pltpu.roll(v, k, axis=1), packed)
            fz[s, f, 0] = packed
            lows = fy[s, f, :, 0, :]
            highs = fy[s, f, :, 7, :]
            fy_low[s, f] = lows + pltpu.roll(lows, 127, axis=1)
            fy_high[s, f] = highs + pltpu.roll(highs, 127, axis=1)
            for end in range(2):
                v = fx[s, end, f]
                v = v + pltpu.roll(v, 96, axis=1)
                fx[s, end, f] = v + z_up(v)
        rec[pl.ds(15 * 32 + s * 16, 16), :] = jnp.zeros((16, 128), F32)
    fold16 = 2 * lax.rem(lane16, 16)
    for s in range(2):
        for f in range(5):
            y_part = jnp.where(
                in32 < 16, take(fy_low[s, f], fold16), take(fy_high[s, f], 96 + fold16)
            )
            ends = [fx[s, end, f] for end in range(2)]
            packed = fz[s, f, 0]
            for h in range(2):
                picked = jnp.where(is_lo, take(ends[0], h * 64 + fold), take(ends[1], h * 64 + fold))
                z_part = take(packed, h * 64 + jnp.where(is_lo, 0, 31) + lax.rem(lane, 16))
                fs[s, f, pl.ds(h, 8, stride=2), :] = jnp.where(lane < 32, picked, z_part)
            whole = jnp.where((lane16 >= 32) & (lane16 < 64), y_part, fs[s, f])
            rec[pl.ds((10 + f) * 32 + s * 16, 16), :] = whole * 0.0625
    for s in range(2):
        for copy in copies_out(s):
            copy.wait()


def fine_steps(fine, got):
    return pl.pallas_call(
        fine_kernel,
        out_shape=(
            jax.ShapeDtypeStruct((2, 5, 4, 8, 1024), F32),
            jax.ShapeDtypeStruct((512, 128), F32),
        ),
        in_specs=[pl.BlockSpec(memory_space=pl.ANY), pl.BlockSpec(memory_space=VMEM)],
        out_specs=(pl.BlockSpec(memory_space=pl.ANY), pl.BlockSpec(memory_space=VMEM)),
        scratch_shapes=[
            VMEM((2, 5, 4, 64, 128), F32),
            VMEM((2, 5, 33, 8, 128), F32),
            VMEM((2, 2, 5, 16, 128), F32),
            VMEM((2, 2, 5, 2, 8, 128), F32),
            VMEM((2, 2, 5, 16, 8, 128), F32),
            VMEM((2, 2, 5, 16, 8, 128), F32),
            VMEM((2, 2, 5, 8, 128), F32),
            VMEM((2, 5, 16, 8, 128), F32),
            VMEM((2, 5, 16, 8, 128), F32),
            VMEM((2, 5, 16, 128), F32),
            VMEM((2, 5, 16, 128), F32),
            VMEM((2, 5, 16, 8, 128), F32),
            VMEM((2, 5, 16, 128), F32),
            pltpu.SemaphoreType.DMA((2, 8)),
            pltpu.SemaphoreType.DMA((2, 8)),
        ],
        compiler_params=pltpu.CompilerParams(vmem_limit_bytes=LIMIT),
    )(fine, got)


def amounts_kernel(tab, back, fc_ref, am_ref, xs_ref, ys_ref):
    lane16 = lane_ids(16)
    sign = jnp.where(lax.rem(lane16, 32) < 16, -0.05, 0.05).astype(F32)
    xs_ref[...] = jnp.zeros_like(xs_ref)
    ys_ref[...] = jnp.zeros_like(ys_ref)
    count = tab[104]
    for r in range(MOST):

        @pl.when(r < count)
        def _():
            y0 = pl.multiple_of(tab[96 + r], 16)
            z0 = tab[100 + r]
            inside = (lane16 >= z0) & (lane16 < z0 + 16)
            at = lax.rem(lane16 - z0 + 128, 16)
            for f in range(5):
                value = sign * (back[pl.ds((10 + f) * 64 + r * 16, 16), :] - fc_ref[r, f])
                am_ref[r, f] = value
                for end in range(2):
                    picked = jnp.where(inside, take(value, at + 16 * end), 0.0)
                    xs_ref[end, f, pl.ds(y0, 16), :] = xs_ref[end, f, pl.ds(y0, 16), :] + picked
                    picked = jnp.where(inside, take(value, at + 32 + 16 * end), 0.0)
                    which = y0 // 16 + 2 * end
                    ys_ref[which, f] = ys_ref[which, f] + picked


def amounts(tab, back, fc):
    return pl.pallas_call(
        amounts_kernel,
        out_shape=(
            jax.ShapeDtypeStruct((MOST, 5, 16, 128), F32),
            jax.ShapeDtypeStruct((2, 5, 32, 128), F32),
            jax.ShapeDtypeStruct((4, 5, 16, 128), F32),
        ),
        in_specs=[
            pl.BlockSpec(memory_space=SMEM),
            pl.BlockSpec(memory_space=VMEM),
            pl.BlockSpec(memory_space=VMEM),
        ],
        out_specs=(pl.BlockSpec(memory_space=VMEM),) * 3,
        compiler_params=pltpu.CompilerParams(vmem_limit_bytes=LIMIT),
    )(tab, back, fc)


def swap_kernel(xs_ref, ys_ref, xa_ref, ya_ref, send_sem, recv_sem):
    gx, gy, xs, ys = neighbours()
    devices = [(xs[0], gy), (xs[1], gy), (gx, ys[0]), (gx, ys[1])]
    greet(devices)
    pairs = [
        (xs_ref.at[0], xa_ref.at[1]),
        (xs_ref.at[1], xa_ref.at[0]),
        (ys_ref.at[0], ya_ref.at[1]),
        (ys_ref.at[3], ya_ref.at[0]),
    ]
    copies = []
    for number, (src, dst) in enumerate(pairs):
        copy = pltpu.make_async_remote_copy(
            src_ref=src,
            dst_ref=dst,
            send_sem=send_sem.at[number],
            recv_sem=recv_sem.at[number],
            device_id=devices[number],
            device_id_type=MESH,
        )
        copy.start()
        copies.append(copy)
    for copy in copies:
        copy.wait()


def swap(xs, ys):
    return pl.pallas_call(
        swap_kernel,
        out_shape=(
            jax.ShapeDtypeStruct((2, 5, 32, 128), F32),
            jax.ShapeDtypeStruct((2, 5, 16, 128), F32),
        ),
        in_specs=[pl.BlockSpec(memory_space=VMEM)] * 2,
        out_specs=(pl.BlockSpec(memory_space=VMEM),) * 2,
        scratch_shapes=[pltpu.SemaphoreType.DMA((4,)), pltpu.SemaphoreType.DMA((4,))],
        compiler_params=pltpu.CompilerParams(
            collective_id=4, has_side_effects=True, vmem_limit_bytes=LIMIT
        ),
    )(xs, ys)


def final_kernel(tab, new_ref, back, am_ref, ys_ref, xa_ref, ya_ref, out_ref):
    lane = lane_ids()
    lane16 = lane_ids(16)
    out_ref[...] = new_ref[...]
    for f in range(5):
        out_ref[f, pl.ds(0, 32), :] = out_ref[f, pl.ds(0, 32), :] + xa_ref[0, f]
        out_ref[f, pl.ds(480, 32), :] = out_ref[f, pl.ds(480, 32), :] + xa_ref[1, f]
        for y, values in ((0, ya_ref[0, f]), (31, ya_ref[1, f]), (15, ys_ref[1, f]), (16, ys_ref[2, f])):
            out_ref[f, pl.ds(y, 16, stride=32), :] = out_ref[f, pl.ds(y, 16, stride=32), :] + values
    count = tab[104]

    def one_rank(r, carry):
        y0 = pl.multiple_of(tab[96 + r], 16)
        z0 = tab[100 + r]
        low, high = lax.rem(z0 + 127, 128), lax.rem(z0 + 16, 128)
        touched = (lane16 == low) | (lane16 == high)
        at = jnp.where(lane16 == low, 64, 80)
        for f in range(5):
            value = am_ref[r, f]
            for x in range(16):
                rows = pl.ds(32 * x + y0, 16)
                here = out_ref[f, rows, :]
                out_ref[f, rows, :] = jnp.where(touched, here + take(value, at + x), here)
        return carry

    lax.fori_loop(0, count, one_rank, 0)

    def cover(r, carry):
        y0 = pl.multiple_of(tab[96 + r], 16)
        z0 = tab[100 + r]
        inside = (lane >= z0) & (lane < z0 + 16)
        at = 2 * lax.rem(lane - z0 + 128, 16)
        for f in range(5):
            for xq in range(4):
                v = 4 * f + xq
                packed = back[pl.ds((v // 2) * 64 + r * 16 + (v % 2) * 8, 8), :]
                for j in range(4):
                    for h in range(2):
                        rows = pl.ds(32 * (4 * xq + j) + y0 + h, 8, stride=2)
                        picked = take(packed, at + h * 64 + (j // 2) * 32 + j % 2)
                        out_ref[f, rows, :] = jnp.where(inside, picked, out_ref[f, rows, :])
        return carry

    lax.fori_loop(0, count, cover, 0)


def final(tab, new, back, am, ys, xa, ya):
    return pl.pallas_call(
        final_kernel,
        out_shape=jax.ShapeDtypeStruct((5, 512, 128), F32),
        in_specs=[pl.BlockSpec(memory_space=SMEM)] + [pl.BlockSpec(memory_space=VMEM)] * 6,
        out_specs=pl.BlockSpec(memory_space=VMEM),
        compiler_params=pltpu.CompilerParams(vmem_limit_bytes=LIMIT),
    )(tab, new, back, am, ys, xa, ya)


def per_device(coarse_state, fine_state, corners, slot_patch):
    coarse = coarse_state.reshape(5, 512, 128)
    hx, hy, hc = halo(coarse)
    new, pk, fc, tab = coarse_step(corners[0], slot_patch[0], coarse, hx, hy, hc)
    got = route(tab, pk.reshape(NGX, MOST, 8, 128), 0, 2, 2)
    fine_next, rec = fine_steps(fine_state.reshape(2, 5, 4, 8, 1024), got.reshape(256, 128))
    back = route(tab, rec.reshape(NGX, 2, 16, 128), 32, MOST, 3).reshape(1024, 128)
    am, xs, ys = amounts(tab, back, fc)
    xa, ya = swap(xs, ys)
    out = final(tab, new, back, am, ys, xa, ya)
    return out.reshape(coarse_state.shape), fine_next.reshape(fine_state.shape)


def solution(mesh):
    placed = (
        P(None, "gx", "gy", None),
        P("gx", "gy", None, None, None, None),
        P("gy", None, None),
        P("gy", None),
    )
    return jax.shard_map(
        per_device,
        mesh=mesh,
        in_specs=placed,
        out_specs=(P(None, "gx", "gy", None), P("gx", "gy", None, None, None, None)),
        check_vma=False,
    )
```

```python
import jax
import jax.numpy as jnp
from jax import lax
from jax.experimental import pallas as pl
from jax.experimental.pallas import tpu as pltpu
from jax.sharding import PartitionSpec as P

F32 = jnp.float32
I32 = jnp.int32
MESH = pl.DeviceIdType.MESH
VMEM = pltpu.VMEM
SMEM = pltpu.SMEM
NGX = 16
NGY = 8
MOST = 4
PCOL = 32
YE = 48
XE = 20
LIMIT = 48 * 1024 * 1024


def lane_ids(rows=8):
    return lax.broadcasted_iota(I32, (rows, 128), 1)


def take(values, idx):
    return jnp.take_along_axis(values, idx, axis=1)


def prims(state):
    inv = 1.0 / state[0]
    vel = [state[1] * inv, state[2] * inv, state[3] * inv]
    kinetic = 0.5 * (state[1] * vel[0] + state[2] * vel[1] + state[3] * vel[2])
    pressure = 0.4 * (state[4] - kinetic)
    sound = jnp.sqrt(1.4 * pressure * inv)
    return vel, pressure, sound


def flow(state, vel, pressure, normal):
    out = [state[1 + normal], state[1] * vel, state[2] * vel, state[3] * vel, (state[4] + pressure) * vel]
    out[1 + normal] = out[1 + normal] + pressure
    return out


def side(state, normal, pre=None):
    vel, pressure, sound = prims(state) if pre is None else pre
    return state, flow(state, vel[normal], pressure, normal), jnp.abs(vel[normal]) + sound


def twice_flux(low, high):
    fastest = jnp.maximum(low[2], high[2])
    return [
        (low[1][f] + high[1][f]) - fastest * (high[0][f] - low[0][f]) for f in range(5)
    ]


def neighbours():
    gx, gy = lax.axis_index("gx"), lax.axis_index("gy")
    xs = (lax.rem(gx + NGX - 1, NGX), lax.rem(gx + 1, NGX))
    ys = (lax.rem(gy + NGY - 1, NGY), lax.rem(gy + 1, NGY))
    return gx, gy, xs, ys


def greet(devices):
    barrier = pltpu.get_barrier_semaphore()
    for device in devices:
        pl.semaphore_signal(barrier, inc=1, device_id=device, device_id_type=MESH)
    pl.semaphore_wait(barrier, len(devices))


def tables_kernel(corners, holders, tab, first):
    me = lax.axis_index("gx")

    def zero(b, carry):
        first[b] = 0
        return carry

    lax.fori_loop(0, NGX + 1, zero, 0)

    def clear(i, carry):
        tab[i] = 0
        return carry

    lax.fori_loop(32, 96, clear, 0)

    def count_one(q, carry):
        b = corners[q] // 16
        first[b + 1] = first[b + 1] + 1
        return carry

    lax.fori_loop(0, PCOL, count_one, 0)

    def add_up(b, carry):
        first[b + 1] = first[b + 1] + first[b]
        return carry

    lax.fori_loop(0, NGX, add_up, 0)

    def slot_one(i, carry):
        q = holders[i]
        b = corners[q] // 16
        row = b * MOST + q - first[b]
        tab[i] = row
        tab[32 + row] = i
        return carry

    lax.fori_loop(0, PCOL, slot_one, 0)
    mine = first[me]
    for r in range(MOST):
        q = jnp.minimum(mine + r, PCOL - 1)
        tab[96 + r] = lax.rem(corners[PCOL + q], 32)
        tab[100 + r] = corners[2 * PCOL + q]
    tab[104] = first[me + 1] - mine
    for i in range(105, 128):
        tab[i] = 0


def tables(corners, holders):
    return pl.pallas_call(
        tables_kernel,
        out_shape=jax.ShapeDtypeStruct((128,), I32),
        in_specs=[pl.BlockSpec(memory_space=SMEM)] * 2,
        out_specs=pl.BlockSpec(memory_space=SMEM),
        scratch_shapes=[SMEM((NGX + 1,), I32)],
    )(corners, holders)


def front_kernel(
    tab, c_ref, new_ref, got_old, got_new, fc_ref,
    old, new, zc, y_send, c_send, hy, hc, pk, mid_old, mid_new, sel,
    copy_sem, halo_send, halo_recv, sem_a, sem_b, sem_c, sem_d, own_sem,
):
    gx, gy, xs, ys = neighbours()
    me = gx
    others = [lax.rem(me + step, NGX) for step in range(1, NGX)]
    loads = []
    for x in range(16):
        loads.append(
            pltpu.make_async_copy(
                c_ref.at[:, pl.ds(32 * x, 32), :],
                old.at[:, pl.ds((x + 2) * YE + 8, 32), :],
                copy_sem.at[x],
            )
        )
    for copy in loads:
        copy.start()
    around = [(gx, ys[0]), (gx, ys[1])] + [(xs[a], ys[b]) for a in range(2) for b in range(2)]
    barrier = pltpu.get_barrier_semaphore()
    greeted = [(other, gy) for other in others] + around
    for device in greeted:
        pl.semaphore_signal(barrier, inc=1, device_id=device, device_id_type=MESH)
    c_send[...] = jnp.zeros_like(c_send)
    for copy in loads:
        copy.wait()
    for end in range(2):
        for f in range(5):
            for r in range(2):
                y_send[end, f, r] = old[f, pl.ds(2 * YE + 8 + 30 * end + r, 16, stride=YE), :]
    for a in range(2):
        for b in range(2):
            for f in range(5):
                c_send[2 * a + b, pl.ds(f, 1), :] = old[
                    f, pl.ds((2 + 15 * a) * YE + 8 + 31 * b, 1), :
                ]
    pl.semaphore_wait(barrier, len(greeted))
    halos = []

    def send(src, dst, device):
        number = len(halos)
        copy = pltpu.make_async_remote_copy(
            src_ref=src,
            dst_ref=dst,
            send_sem=halo_send.at[number],
            recv_sem=halo_recv.at[number],
            device_id=device,
            device_id_type=MESH,
        )
        copy.start()
        halos.append(copy)

    for plane, xi, where in ((0, 18, 0), (15, 1, 1), (1, 19, 0), (14, 0, 1)):
        send(
            c_ref.at[:, pl.ds(32 * plane, 32), :],
            old.at[:, pl.ds(xi * YE + 8, 32), :],
            (xs[where], gy),
        )
    for end in range(2):
        send(y_send.at[end], hy.at[1 - end], (gx, ys[end]))
    for a in range(2):
        for b in range(2):
            send(c_send.at[2 * a + b], hc.at[3 - 2 * a - b], (xs[a], ys[b]))

    lane16 = lane_ids(16)
    is_lo = lax.rem(lane16, 32) < 16
    quarter = lane16 // 32
    sign = jnp.where(is_lo, 1.0, -1.0).astype(F32)
    in16 = lax.rem(lane_ids(32), 16)
    zpick = (lane_ids(32) - in16 + 15, lane_ids(32) - in16)

    def advance(mid, xm, xp, ym, yp):
        pre = prims(mid)
        cx = side(mid, 0, pre)
        diff = twice_flux(cx, side(xp, 0))
        low = twice_flux(side(xm, 0), cx)
        total = [a - b for a, b in zip(diff, low)]
        cy = side(mid, 1, pre)
        up = twice_flux(cy, side(yp, 1))
        low = twice_flux(side(ym, 1), cy)
        total = [t + (a - b) for t, a, b in zip(total, up, low)]
        cz = side(mid, 2, pre)
        next_vel = pltpu.roll(pre[0][2], 127, axis=1)
        next_p = pltpu.roll(pre[1], 127, axis=1)
        next_u = [pltpu.roll(v, 127, axis=1) for v in mid]
        nz = (next_u, flow(next_u, next_vel, next_p, 2), pltpu.roll(cz[2], 127, axis=1))
        up = twice_flux(cz, nz)
        total = [t + (a - pltpu.roll(a, 1, axis=1)) for t, a in zip(total, up)]
        return [u - 0.025 * t for u, t in zip(mid, total)]

    def tiles(bases, stride=None):
        def rows(start):
            if stride is None:
                return [old[f, pl.ds(start, 8), :] for f in range(5)]
            return [old[f, pl.ds(start, 8, stride=stride), :] for f in range(5)]

        results = [
            advance(rows(base), rows(base - YE), rows(base + YE), rows(base - 1), rows(base + 1))
            for base in bases
        ]
        for base, result in zip(bases, results):
            for f in range(5):
                if stride is None:
                    new[f, pl.ds(base, 8), :] = result[f]
                else:
                    new[f, pl.ds(base, 8, stride=stride), :] = result[f]

    def inner_plane(xi, carry):
        tiles([xi * YE + 16, xi * YE + 24])
        return carry

    def outer_plane(xi, carry):
        tiles([xi * YE + 8, xi * YE + 32])
        return carry

    def compress(when, source):
        def field(f, carry):
            for end in range(2):
                acc = None
                for x in range(16):
                    plane = source[f, pl.ds((2 + x) * YE + 8, 32), :]
                    picked = take(plane, zpick[end])
                    acc = picked if acc is None else jnp.where(in16 == x, picked, acc)
                zc[when, f, end] = acc
            return carry

        lax.fori_loop(0, 5, field, 0)

    lax.fori_loop(3, 17, inner_plane, 0)
    compress(0, old)
    for copy in halos:
        copy.wait()
    for f in range(5):
        for r in range(2):
            old[f, pl.ds(2 * YE + 6 + r, 16, stride=YE), :] = hy[0, f, r]
            old[f, pl.ds(2 * YE + 40 + r, 16, stride=YE), :] = hy[1, f, r]
        for a, xi in ((0, 1), (1, 18)):
            for b, yi in ((0, 7), (1, 40)):
                old[f, pl.ds(xi * YE + yi, 1), :] = hc[2 * a + b, pl.ds(f, 1), :]

    def groups(source, when, outer, y0, z0):
        z0 = jnp.broadcast_to(z0, (16, 128))
        group = (lane16 - z0 + 128) % 128 // 16
        masks = [group == g for g in range(5)]
        bits = [(z0 // (16 << b)) % 2 == 1 for b in range(3)]
        upper = jnp.broadcast_to(y0, (16, 128)) > 0
        x_at = (1, 18) if outer else (2, 17)
        y_at = (7, 24) if outer else (8, 23)
        found = []
        for f in range(5):
            faces = [
                jnp.where(
                    upper,
                    source[f, pl.ds(xi * YE + 24, 16), :],
                    source[f, pl.ds(xi * YE + 8, 16), :],
                )
                for xi in x_at
            ]
            for yi in y_at:
                faces.append(
                    jnp.where(
                        upper,
                        source[f, pl.ds(2 * YE + yi + 16, 16, stride=YE), :],
                        source[f, pl.ds(2 * YE + yi, 16, stride=YE), :],
                    )
                )
            tops, bottoms = (
                jnp.where(upper, zc[when, f, end, pl.ds(16, 16), :], zc[when, f, end, pl.ds(0, 16), :])
                for end in range(2)
            )
            faces += [tops, bottoms] if outer else [bottoms, tops]
            shifts = (0, 16, 32, 48) + ((80, 64) if outer else (64, 80))
            value = pltpu.roll(faces[5], shifts[5], axis=1)
            for g in range(5):
                moved = pltpu.roll(faces[g], shifts[g], axis=1) if shifts[g] else faces[g]
                value = jnp.where(masks[g], moved, value)
            for b in range(3):
                value = jnp.where(bits[b], pltpu.roll(value, 128 - (16 << b), axis=1), value)
            found.append(value)
        return found

    def extract(when, source):
        def one_rank(r, carry):
            y0 = tab[96 + r]
            v = groups(source, when, True, y0, tab[100 + r])
            rows = [
                jnp.where(quarter < 3, v[0], pltpu.roll(v[1], 96, axis=1)),
                jnp.where(quarter < 2, pltpu.roll(v[1], 96, axis=1), pltpu.roll(v[2], 64, axis=1)),
                jnp.where(quarter < 1, pltpu.roll(v[2], 64, axis=1), pltpu.roll(v[3], 32, axis=1)),
                v[4],
            ]
            for i in range(4):
                pk[when, pl.ds(r * 4 + i, 16, stride=16), :] = rows[i]
            return carry

        lax.fori_loop(0, MOST, one_rank, 0)

    mids = (mid_old, mid_new)

    def scatter(when):
        own = pltpu.make_async_copy(
            pk.at[when, pl.ds(16 * me, 16), :], mids[when].at[pl.ds(16 * me, 16), :], own_sem.at[when]
        )
        own.start()
        copies = [own]
        for number, other in enumerate(others):
            copy = pltpu.make_async_remote_copy(
                src_ref=pk.at[when, pl.ds(16 * other, 16), :],
                dst_ref=mids[when].at[pl.ds(16 * me, 16), :],
                send_sem=sem_a.at[when, number],
                recv_sem=sem_b.at[when, number],
                device_id=(other, gy),
                device_id_type=MESH,
            )
            copy.start()
            copies.append(copy)
        return copies

    def forward(when, out_ref):
        def choose(d, carry):
            for s in range(2):
                at = tab[2 * d + s]
                sel[when, pl.ds(8 * d + 4 * s, 4), :] = mids[when][pl.ds(4 * at, 4), :]
            return carry

        lax.fori_loop(0, NGX, choose, 0)
        own = pltpu.make_async_copy(
            sel.at[when, pl.ds(8 * me, 8), :], out_ref.at[pl.ds(8 * me, 8), :], own_sem.at[2 + when]
        )
        own.start()
        copies = [own]
        for number, other in enumerate(others):
            copy = pltpu.make_async_remote_copy(
                src_ref=sel.at[when, pl.ds(8 * other, 8), :],
                dst_ref=out_ref.at[pl.ds(8 * me, 8), :],
                send_sem=sem_c.at[when, number],
                recv_sem=sem_d.at[when, number],
                device_id=(other, gy),
                device_id_type=MESH,
            )
            copy.start()
            copies.append(copy)
        return copies

    extract(0, old)
    old_first = scatter(0)
    lax.fori_loop(3, 17, outer_plane, 0)
    for xi in (1, 2, 17, 18):
        tiles([xi * YE + 8, xi * YE + 16])
        tiles([xi * YE + 24, xi * YE + 32])
    for yi in (7, 40):
        tiles([2 * YE + yi, 10 * YE + yi], YE)
    writes = []
    for x in range(16):
        writes.append(
            pltpu.make_async_copy(
                new.at[:, pl.ds((x + 2) * YE + 8, 32), :],
                new_ref.at[:, pl.ds(32 * x, 32), :],
                copy_sem.at[x],
            )
        )
    compress(1, new)
    extract(1, new)
    new_first = scatter(1)
    for copy in old_first:
        copy.wait()
    old_second = forward(0, got_old)
    for copy in writes:
        copy.start()

    def by_normal(a, b, c):
        return jnp.where(quarter == 0, a, jnp.where(quarter == 1, b, c))

    def normal_side(state):
        vel, pressure, sound = prims(state)
        along = by_normal(*vel)
        flows = [
            by_normal(state[1], state[2], state[3]),
            state[1] * along + jnp.where(quarter == 0, pressure, 0.0),
            state[2] * along + jnp.where(quarter == 1, pressure, 0.0),
            state[3] * along + jnp.where(quarter >= 2, pressure, 0.0),
            (state[4] + pressure) * along,
        ]
        return state, flows, jnp.abs(along) + sound

    def face_flux(r, carry):
        y0 = tab[96 + r]
        out = groups(old, 0, True, y0, tab[100 + r])
        ins = groups(old, 0, False, y0, tab[100 + r])
        a, b = normal_side(out), normal_side(ins)
        fastest = jnp.maximum(a[2], b[2]) * sign
        for f in range(5):
            fc_ref[r, f] = 0.5 * ((a[1][f] + b[1][f]) - fastest * (ins[f] - out[f]))
        return carry

    for copy in new_first:
        copy.wait()
    new_second = forward(1, got_new)
    lax.fori_loop(0, MOST, face_flux, 0)

    for copy in old_second + new_second + writes:
        copy.wait()


def front(tab, coarse):
    dma = pltpu.SemaphoreType.DMA
    return pl.pallas_call(
        front_kernel,
        out_shape=(
            jax.ShapeDtypeStruct((5, 512, 128), F32),
            jax.ShapeDtypeStruct((128, 128), F32),
            jax.ShapeDtypeStruct((128, 128), F32),
            jax.ShapeDtypeStruct((MOST, 5, 16, 128), F32),
        ),
        in_specs=[pl.BlockSpec(memory_space=SMEM), pl.BlockSpec(memory_space=pl.ANY)],
        out_specs=(
            pl.BlockSpec(memory_space=pl.ANY),
            pl.BlockSpec(memory_space=VMEM),
            pl.BlockSpec(memory_space=VMEM),
            pl.BlockSpec(memory_space=VMEM),
        ),
        scratch_shapes=[
            VMEM((5, XE * YE, 128), F32),
            VMEM((5, XE * YE, 128), F32),
            VMEM((2, 5, 2, 32, 128), F32),
            VMEM((2, 5, 2, 16, 128), F32),
            VMEM((4, 8, 128), F32),
            VMEM((2, 5, 2, 16, 128), F32),
            VMEM((4, 8, 128), F32),
            VMEM((2, 256, 128), F32),
            VMEM((256, 128), F32),
            VMEM((256, 128), F32),
            VMEM((2, 128, 128), F32),
            dma((16,)),
            dma((10,)),
            dma((10,)),
            dma((2, NGX - 1)),
            dma((2, NGX - 1)),
            dma((2, NGX - 1)),
            dma((2, NGX - 1)),
            dma((4,)),
        ],
        compiler_params=pltpu.CompilerParams(
            collective_id=1, has_side_effects=True, vmem_limit_bytes=LIMIT
        ),
    )(tab, coarse)


def fine_kernel(fine_ref, got_old, got_new, out_ref, rec, buf, state, gp, gx, gy, gz, fx, fy, fz, fy_low, fy_high, av, fs, in_sem, out_sem):
    lane = lane_ids()
    sub = lax.broadcasted_iota(I32, (8, 128), 0)
    z = lax.rem(lane, 32)

    def copies_in(s):
        return [
            pltpu.make_async_copy(
                fine_ref.at[s, :, :, :, pl.ds(128 * k, 128)],
                buf.at[s, :, :, pl.ds(8 * k, 8), :],
                in_sem.at[s, k],
            )
            for k in range(8)
        ]

    def copies_out(s):
        return [
            pltpu.make_async_copy(
                buf.at[s, :, :, pl.ds(8 * k, 8), :],
                out_ref.at[s, :, :, :, pl.ds(128 * k, 128)],
                out_sem.at[s, k],
            )
            for k in range(8)
        ]

    for s in range(2):
        for copy in copies_in(s):
            copy.start()

    def y_up(v):
        moved = pltpu.roll(v, 96, axis=1)
        return jnp.where(lane < 96, moved, pltpu.roll(moved, 7, axis=0))

    def y_down(v):
        moved = pltpu.roll(v, 32, axis=1)
        return jnp.where(lane >= 32, moved, pltpu.roll(moved, 1, axis=0))

    def z_up(v):
        return pltpu.roll(v, 127, axis=1)

    def z_down(v):
        return pltpu.roll(v, 1, axis=1)

    y_first = (sub == 0) & (lane < 32)
    y_last = (sub == 7) & (lane >= 96)
    z_first = z == 0
    z_last = z == 31
    y_sign = jnp.where(y_last, 1.0, -1.0).astype(F32)
    z_sign = jnp.where(z_last, 1.0, -1.0).astype(F32)
    y_pick = 32 + jnp.where(lane >= 96, 16, 0) + z // 2
    z_pick = jnp.where(z_first, 64, 80)
    x_pick = z // 2
    left = lane < 64

    def along(mid, pre, normal, up, down, first, last, sign, ghost):
        cell = side(mid, normal, pre)
        shifted = [up(v) for v in mid]
        above = (
            shifted,
            flow(shifted, up(pre[0][normal]), up(pre[1]), normal),
            up(cell[2]),
        )
        inner = twice_flux(cell, above)
        fastest = jnp.maximum(cell[2], ghost[2]) * sign
        edge = [
            (cell[1][f] + ghost[1][f]) - fastest * (ghost[0][f] - mid[f]) for f in range(5)
        ]
        diff = [
            jnp.where(last, edge[f], inner[f]) - jnp.where(first, edge[f], down(inner[f]))
            for f in range(5)
        ]
        return diff, edge

    lane16 = lane_ids(16)
    quarter = lane16 // 32
    in32 = lax.rem(lane16, 32)
    for s in range(2):
        rows = [
            [got[pl.ds(s * 4 + i, 16, stride=8), :] for i in range(4)] for got in (got_old, got_new)
        ]
        for f in range(5):
            both = []
            for when in range(2):
                parts = []
                for g in range(3):
                    c = 3 * f + g
                    parts.append(take(rows[when][c // 4], (c % 4) * 32 + in32))
                both.append(
                    jnp.where(quarter == 0, parts[0], jnp.where(quarter == 1, parts[1], parts[2]))
                )
            gp[s, 0, f] = both[0]
            gp[s, 1, f] = 0.5 * (both[0] + both[1])
        for step in range(2):
            for f in range(5):
                even = gp[s, step, f, pl.ds(0, 8, stride=2), :]
                odd = gp[s, step, f, pl.ds(1, 8, stride=2), :]
                for end in range(2):
                    picks = [take(v, 16 * end + x_pick) for v in (even, odd)]
                    gx[s, step, f, end] = jnp.where(left, picks[0], picks[1])
                spread = take(gp[s, step, f], jnp.broadcast_to(y_pick[0:1], (16, 128)))
                for k in range(16):
                    picks = [take(v, z_pick + k) for v in (even, odd)]
                    gz[s, step, f, k] = jnp.where(left, picks[0], picks[1])
                    gy[s, step, f, k] = jnp.broadcast_to(spread[k : k + 1], (8, 128))
    for s in range(2):
        for copy in copies_in(s):
            copy.wait()
        for x in range(32):
            for f in range(5):
                state[s, f, x] = buf[s, f, x // 8, pl.ds(x % 8, 8, stride=8), :]

    def one_pair(s, step, k, below):
        ghost_y = [gy[s, step, f, k] for f in range(5)]
        ghost_z = [gz[s, step, f, k] for f in range(5)]
        mids = [[state[s, f, 2 * k + p] for f in range(5)] for p in range(3)]
        old_y = [fy[s, f, k] for f in range(5)] if step else None
        old_z = [fz[s, f, k] for f in range(5)] if step else None
        ghost_y = side(ghost_y, 1)
        ghost_z = side(ghost_z, 2)
        pres = [prims(mid) for mid in mids]
        sides = [side(mids[p], 0, pres[p]) for p in range(3)]
        results, edges_y, edges_z = [], [], []
        for p in range(2):
            above = twice_flux(sides[p], sides[p + 1])
            diff_y, edge_y = along(
                mids[p], pres[p], 1, y_up, y_down, y_first, y_last, y_sign, ghost_y
            )
            diff_z, edge_z = along(
                mids[p], pres[p], 2, z_up, z_down, z_first, z_last, z_sign, ghost_z
            )
            results.append(
                [
                    mids[p][f] - 0.025 * ((above[f] - below[f]) + diff_y[f] + diff_z[f])
                    for f in range(5)
                ]
            )
            below = above
            edges_y.append(edge_y)
            edges_z.append(edge_z)
        sum_y = [edges_y[0][f] + edges_y[1][f] for f in range(5)]
        sum_z = [edges_z[0][f] + edges_z[1][f] for f in range(5)]
        if step == 0:
            return below, results, sum_y, sum_z, None
        sum_y = [a + b for a, b in zip(sum_y, old_y)]
        sum_z = [a + b for a, b in zip(sum_z, old_z)]
        means = []
        for f in range(5):
            mean = results[0][f] + results[1][f]
            mean = mean + pltpu.roll(mean, 96, axis=1)
            means.append(0.125 * (mean + z_up(mean)))
        return below, results, sum_y, sum_z, means

    for step in range(2):
        starts = []
        for s in range(2):
            for f in range(5):
                state[s, f, 32] = gx[s, step, f, 1]
            ghost_low = side([gx[s, step, f, 0] for f in range(5)], 0)
            plane0 = side([state[s, f, 0] for f in range(5)], 0)
            starts.append(twice_flux(ghost_low, plane0))

        def pairs(k, carry):
            found = [one_pair(s, step, k, carry[s]) for s in range(2)]
            for s in range(2):
                below, results, sum_y, sum_z, means = found[s]
                for f in range(5):
                    state[s, f, 2 * k] = results[0][f]
                    state[s, f, 1 + 2 * k] = results[1][f]
                    fy[s, f, k] = sum_y[f]
                    fz[s, f, k] = sum_z[f]
                    if step:
                        av[s, f, k] = means[f]
            return found[0][0], found[1][0]

        ends = lax.fori_loop(0, 16, pairs, tuple(starts), unroll=2)
        for s in range(2):
            for f in range(5):
                if step == 0:
                    fx[s, 0, f] = starts[s][f]
                    fx[s, 1, f] = ends[s][f]
                else:
                    fx[s, 0, f] = fx[s, 0, f] + starts[s][f]
                    fx[s, 1, f] = fx[s, 1, f] + ends[s][f]

    for s in range(2):
        for x in range(32):
            for f in range(5):
                buf[s, f, x // 8, pl.ds(x % 8, 8, stride=8), :] = state[s, f, x]
        for copy in copies_out(s):
            copy.start()
    is_lo = z < 16
    fold = 2 * lax.rem(lane, 16)
    slot_of = lax.rem(lane // 32, 2) * 2 + lax.rem(lane, 2)
    half_lane = lax.rem(lane, 64)
    z_place = jnp.where(half_lane < 31, half_lane, half_lane - 31)
    for s in range(2):
        for f in range(5):
            loaded = [av[s, f, k] for k in range(16)]
            for xq in range(4):
                packed = loaded[4 * xq]
                for j in range(1, 4):
                    moved = pltpu.roll(loaded[4 * xq + j], (j // 2) * 32 + j % 2, axis=1)
                    packed = jnp.where(slot_of == j, moved, packed)
                v = 4 * f + xq
                rec[pl.ds((v // 2) * 32 + s * 16 + (v % 2) * 8, 8), :] = packed
            loaded = [fz[s, f, k] for k in range(16)]
            packed = None
            for k in range(16):
                v = loaded[k] + pltpu.roll(loaded[k], 96, axis=1)
                if k == 0:
                    packed = v
                else:
                    packed = jnp.where(z_place == k, pltpu.roll(v, k, axis=1), packed)
            fz[s, f, 0] = packed
            lows = fy[s, f, :, 0, :]
            highs = fy[s, f, :, 7, :]
            fy_low[s, f] = lows + pltpu.roll(lows, 127, axis=1)
            fy_high[s, f] = highs + pltpu.roll(highs, 127, axis=1)
            for end in range(2):
                v = fx[s, end, f]
                v = v + pltpu.roll(v, 96, axis=1)
                fx[s, end, f] = v + z_up(v)
        rec[pl.ds(15 * 32 + s * 16, 16), :] = jnp.zeros((16, 128), F32)
    fold16 = 2 * lax.rem(lane16, 16)
    for s in range(2):
        for f in range(5):
            y_part = jnp.where(
                in32 < 16, take(fy_low[s, f], fold16), take(fy_high[s, f], 96 + fold16)
            )
            ends = [fx[s, end, f] for end in range(2)]
            packed = fz[s, f, 0]
            for h in range(2):
                picked = jnp.where(is_lo, take(ends[0], h * 64 + fold), take(ends[1], h * 64 + fold))
                z_part = take(packed, h * 64 + jnp.where(is_lo, 0, 31) + lax.rem(lane, 16))
                fs[s, f, pl.ds(h, 8, stride=2), :] = jnp.where(lane < 32, picked, z_part)
            whole = jnp.where((lane16 >= 32) & (lane16 < 64), y_part, fs[s, f])
            rec[pl.ds((10 + f) * 32 + s * 16, 16), :] = whole * 0.0625
    for s in range(2):
        for copy in copies_out(s):
            copy.wait()


def fine_steps(fine, got_old, got_new):
    return pl.pallas_call(
        fine_kernel,
        out_shape=(
            jax.ShapeDtypeStruct((2, 5, 4, 8, 1024), F32),
            jax.ShapeDtypeStruct((512, 128), F32),
        ),
        in_specs=[pl.BlockSpec(memory_space=pl.ANY)] + [pl.BlockSpec(memory_space=VMEM)] * 2,
        out_specs=(pl.BlockSpec(memory_space=pl.ANY), pl.BlockSpec(memory_space=VMEM)),
        scratch_shapes=[
            VMEM((2, 5, 4, 64, 128), F32),
            VMEM((2, 5, 33, 8, 128), F32),
            VMEM((2, 2, 5, 16, 128), F32),
            VMEM((2, 2, 5, 2, 8, 128), F32),
            VMEM((2, 2, 5, 16, 8, 128), F32),
            VMEM((2, 2, 5, 16, 8, 128), F32),
            VMEM((2, 2, 5, 8, 128), F32),
            VMEM((2, 5, 16, 8, 128), F32),
            VMEM((2, 5, 16, 8, 128), F32),
            VMEM((2, 5, 16, 128), F32),
            VMEM((2, 5, 16, 128), F32),
            VMEM((2, 5, 16, 8, 128), F32),
            VMEM((2, 5, 16, 128), F32),
            pltpu.SemaphoreType.DMA((2, 8)),
            pltpu.SemaphoreType.DMA((2, 8)),
        ],
        compiler_params=pltpu.CompilerParams(vmem_limit_bytes=LIMIT),
    )(fine, got_old, got_new)


def back_kernel(
    tab, rec, fc_ref, new_ref, out_ref,
    mid, sel, back, zs_buf, xs_buf, ys_buf, xa, ya,
    new_sem, sem_a, sem_b, sem_c, sem_d, own_sem, swap_send, swap_recv,
):
    gx, gy, xs, ys = neighbours()
    me = gx
    others = [lax.rem(me + step, NGX) for step in range(1, NGX)]
    load = pltpu.make_async_copy(new_ref, out_ref, new_sem)
    load.start()
    greet([(other, gy) for other in others] + [(gx, ys[0]), (gx, ys[1])])

    def exchange(src, dst, size, sem_s, sem_r, own_at):
        own = pltpu.make_async_copy(
            src.at[pl.ds(size * me, size), :], dst.at[pl.ds(size * me, size), :], own_sem.at[own_at]
        )
        own.start()
        copies = [own]
        for number, other in enumerate(others):
            copy = pltpu.make_async_remote_copy(
                src_ref=src.at[pl.ds(size * other, size), :],
                dst_ref=dst.at[pl.ds(size * me, size), :],
                send_sem=sem_s.at[number],
                recv_sem=sem_r.at[number],
                device_id=(other, gy),
                device_id_type=MESH,
            )
            copy.start()
            copies.append(copy)
        for copy in copies:
            copy.wait()

    exchange(rec, mid, 32, sem_a, sem_b, 0)

    def choose(i, carry):
        sel[pl.ds(16 * i, 16), :] = mid[pl.ds(16 * tab[32 + i], 16), :]
        return carry

    lax.fori_loop(0, NGX * MOST, choose, 0)
    exchange(sel, back, 64, sem_c, sem_d, 1)

    lane = lane_ids()
    lane16 = lane_ids(16)
    sign = jnp.where(lax.rem(lane16, 32) < 16, -0.05, 0.05).astype(F32)
    count = tab[104]
    y0s = [jnp.where(r < count, tab[96 + r], -1) for r in range(MOST)]
    z0s = [tab[100 + r] for r in range(MOST)]

    rest16 = lax.rem(lane16, 16)
    wanted = [
        [
            (lane16 >= z0s[r]) & (lane16 < z0s[r] + 16) & (jnp.broadcast_to(y0s[r], (16, 128)) == 16 * half)
            for half in range(2)
        ]
        for r in range(MOST)
    ]

    def correct(f, carry):
        values = [
            sign * (back[pl.ds((10 + f) * 64 + r * 16, 16), :] - fc_ref[r, f]) for r in range(MOST)
        ]
        for face in range(6):
            picks = [take(value, rest16 + 16 * face) for value in values]
            for half in range(2):
                total = jnp.zeros((16, 128), F32)
                for r in range(MOST):
                    total = jnp.where(wanted[r][half], picks[r], total)
                if face < 2:
                    xs_buf[face, f, pl.ds(16 * half, 16), :] = total
                elif face < 4:
                    ys_buf[half + 2 * (face - 2), f] = total
                else:
                    zs_buf[face - 4, f, pl.ds(16 * half, 16), :] = total
        return carry

    lax.fori_loop(0, 5, correct, 0)
    swaps = []
    for number, (src, dst, device) in enumerate(
        (
            (xs_buf.at[0], xa.at[1], (xs[0], gy)),
            (xs_buf.at[1], xa.at[0], (xs[1], gy)),
            (ys_buf.at[0], ya.at[1], (gx, ys[0])),
            (ys_buf.at[3], ya.at[0], (gx, ys[1])),
        )
    ):
        copy = pltpu.make_async_remote_copy(
            src_ref=src,
            dst_ref=dst,
            send_sem=swap_send.at[number],
            recv_sem=swap_recv.at[number],
            device_id=device,
            device_id_type=MESH,
        )
        copy.start()
        swaps.append(copy)
    load.wait()

    rest = lax.rem(lane, 16)
    insides = [[wanted[r][half][0:8] for r in range(MOST)] for half in range(2)]

    def assemble(i, carry):
        f, xq = i // 4, lax.rem(i, 4)
        packed = [
            back[pl.ds((i // 2) * 64 + r * 16 + lax.rem(i, 2) * 8, 8), :] for r in range(MOST)
        ]
        for h in range(2):
            faces = [
                [zs_buf[end, f, pl.ds(16 * half + h, 8, stride=2), :] for end in range(2)]
                for half in range(2)
            ]
            for j in range(4):
                x = 4 * xq + j
                pick = 2 * rest + (h * 64 + (j // 2) * 32 + j % 2)
                picks = [take(packed[r], pick) for r in range(MOST)]
                low_at = (lane + 1 + x) % 128
                high_at = (lane + 112 + x) % 128
                for half in range(2):
                    rows = pl.ds(32 * x + 16 * half + h, 8, stride=2)
                    value = out_ref[f, rows, :]
                    low = take(faces[half][0], low_at)
                    high = take(faces[half][1], high_at)
                    value = value + jnp.where(rest == 15, low, jnp.where(rest == 0, high, 0.0))
                    for r in range(MOST):
                        value = jnp.where(insides[half][r], picks[r], value)
                    out_ref[f, rows, :] = value
        return carry

    lax.fori_loop(0, 20, assemble, 0)
    covered = []
    for half in range(2):
        mask = wanted[0][half]
        for r in range(1, MOST):
            mask = mask | wanted[r][half]
        covered.append(mask)
    for copy in swaps:
        copy.wait()
    for f in range(5):
        for end in range(2):
            for half in range(2):
                rows = pl.ds(480 * end + 16 * half, 16)
                out_ref[f, rows, :] = out_ref[f, rows, :] + jnp.where(
                    covered[half], 0.0, xa[end, f, pl.ds(16 * half, 16), :]
                )
        for y, values in ((0, ya[0, f]), (31, ya[1, f]), (15, ys_buf[1, f]), (16, ys_buf[2, f])):
            rows = pl.ds(y, 16, stride=32)
            out_ref[f, rows, :] = out_ref[f, rows, :] + jnp.where(covered[y // 16], 0.0, values)


def assemble_all(tab, rec, fc, new):
    dma = pltpu.SemaphoreType.DMA
    return pl.pallas_call(
        back_kernel,
        out_shape=jax.ShapeDtypeStruct((5, 512, 128), F32),
        in_specs=[
            pl.BlockSpec(memory_space=SMEM),
            pl.BlockSpec(memory_space=VMEM),
            pl.BlockSpec(memory_space=VMEM),
            pl.BlockSpec(memory_space=pl.ANY),
        ],
        out_specs=pl.BlockSpec(memory_space=VMEM),
        scratch_shapes=[
            VMEM((512, 128), F32),
            VMEM((1024, 128), F32),
            VMEM((1024, 128), F32),
            VMEM((2, 5, 32, 128), F32),
            VMEM((2, 5, 32, 128), F32),
            VMEM((4, 5, 16, 128), F32),
            VMEM((2, 5, 32, 128), F32),
            VMEM((2, 5, 16, 128), F32),
            dma,
            dma((NGX - 1,)),
            dma((NGX - 1,)),
            dma((NGX - 1,)),
            dma((NGX - 1,)),
            dma((2,)),
            dma((4,)),
            dma((4,)),
        ],
        compiler_params=pltpu.CompilerParams(
            collective_id=2, has_side_effects=True, vmem_limit_bytes=LIMIT
        ),
    )(tab, rec, fc, new)


def per_device(coarse_state, fine_state, corners, slot_patch):
    coarse = coarse_state.reshape(5, 512, 128)
    table = corners[0].T.reshape(3 * PCOL)
    tab = tables(table, slot_patch[0])
    new, got_old, got_new, fc = front(tab, coarse)
    fine_next, rec = fine_steps(fine_state.reshape(2, 5, 4, 8, 1024), got_old, got_new)
    out = assemble_all(tab, rec, fc, new)
    return out.reshape(coarse_state.shape), fine_next.reshape(fine_state.shape)


def solution(mesh):
    placed = (
        P(None, "gx", "gy", None),
        P("gx", "gy", None, None, None, None),
        P("gy", None, None),
        P("gy", None),
    )
    return jax.shard_map(
        per_device,
        mesh=mesh,
        in_specs=placed,
        out_specs=(P(None, "gx", "gy", None), P("gx", "gy", None, None, None, None)),
        check_vma=False,
    )
```

```python
import jax
import jax.numpy as jnp
from jax import lax
from jax.experimental import pallas as pl
from jax.experimental.pallas import tpu as pltpu
from jax.sharding import PartitionSpec as P

F32 = jnp.float32
I32 = jnp.int32
MESH = pl.DeviceIdType.MESH
VMEM = pltpu.VMEM
SMEM = pltpu.SMEM
NGX = 16
NGY = 8
MOST = 4
PCOL = 32
YE = 48
XE = 20
LIMIT = 48 * 1024 * 1024


def lane_ids(rows=8):
    return lax.broadcasted_iota(I32, (rows, 128), 1)


def take(values, idx):
    return jnp.take_along_axis(values, idx, axis=1)


def prims(state):
    inv = 1.0 / state[0]
    vel = [state[1] * inv, state[2] * inv, state[3] * inv]
    kinetic = 0.5 * (state[1] * vel[0] + state[2] * vel[1] + state[3] * vel[2])
    pressure = 0.4 * (state[4] - kinetic)
    sound = jnp.sqrt(1.4 * pressure * inv)
    return vel, pressure, sound


def flow(state, vel, pressure, normal):
    out = [state[1 + normal], state[1] * vel, state[2] * vel, state[3] * vel, (state[4] + pressure) * vel]
    out[1 + normal] = out[1 + normal] + pressure
    return out


def side(state, normal, pre=None):
    vel, pressure, sound = prims(state) if pre is None else pre
    return state, flow(state, vel[normal], pressure, normal), jnp.abs(vel[normal]) + sound


def twice_flux(low, high):
    fastest = jnp.maximum(low[2], high[2])
    return [
        (low[1][f] + high[1][f]) - fastest * (high[0][f] - low[0][f]) for f in range(5)
    ]


def neighbours():
    gx, gy = lax.axis_index("gx"), lax.axis_index("gy")
    xs = (lax.rem(gx + NGX - 1, NGX), lax.rem(gx + 1, NGX))
    ys = (lax.rem(gy + NGY - 1, NGY), lax.rem(gy + 1, NGY))
    return gx, gy, xs, ys


def greet(devices):
    barrier = pltpu.get_barrier_semaphore()
    for device in devices:
        pl.semaphore_signal(barrier, inc=1, device_id=device, device_id_type=MESH)
    pl.semaphore_wait(barrier, len(devices))


def tables_kernel(corners, holders, tab, rows):
    me = lax.axis_index("gx")
    for i in range(NGX * MOST):
        tab[32 + i] = 0
    for i in range(105, 128):
        tab[i] = 0
    mine, count, last, rank = 0, 0, -1, 0
    for q in range(PCOL):
        b = corners[0, 0, q] // 16
        rank = jnp.where(b == last, rank + 1, 0)
        last = b
        rows[q] = b * MOST + rank
        mine = mine + jnp.where(b < me, 1, 0)
        count = count + jnp.where(b == me, 1, 0)
    found = [rows[holders[0, i]] for i in range(PCOL)]
    for i in range(PCOL):
        tab[i] = found[i]
        tab[32 + found[i]] = i
    for r in range(MOST):
        q = jnp.minimum(mine + r, PCOL - 1)
        tab[96 + r] = lax.rem(corners[1, 0, q], 32)
        tab[100 + r] = corners[2, 0, q]
    tab[104] = count


def tables(corners, holders):
    return pl.pallas_call(
        tables_kernel,
        out_shape=jax.ShapeDtypeStruct((128,), I32),
        in_specs=[pl.BlockSpec(memory_space=SMEM)] * 2,
        out_specs=pl.BlockSpec(memory_space=SMEM),
        scratch_shapes=[SMEM((PCOL,), I32)],
    )(corners, holders)


def y_up(v):
    moved = pltpu.roll(v, 96, axis=1)
    return jnp.where(lane_ids() < 96, moved, pltpu.roll(moved, 7, axis=0))


def y_down(v):
    moved = pltpu.roll(v, 32, axis=1)
    return jnp.where(lane_ids() >= 32, moved, pltpu.roll(moved, 1, axis=0))


def z_up(v):
    return pltpu.roll(v, 127, axis=1)


def z_down(v):
    return pltpu.roll(v, 1, axis=1)


def along(mid, pre, normal, up, down, first, last, sign, ghost):
    cell = side(mid, normal, pre)
    shifted = [up(v) for v in mid]
    above = (shifted, flow(shifted, up(pre[0][normal]), up(pre[1]), normal), up(cell[2]))
    inner = twice_flux(cell, above)
    fastest = jnp.maximum(cell[2], ghost[2]) * sign
    edge = [(cell[1][f] + ghost[1][f]) - fastest * (ghost[0][f] - mid[f]) for f in range(5)]
    diff = [
        jnp.where(last, edge[f], inner[f]) - jnp.where(first, edge[f], down(inner[f]))
        for f in range(5)
    ]
    return diff, edge


def unpack_ghosts(got, s):
    lane16 = lane_ids(16)
    quarter = lane16 // 32
    rows = [got[pl.ds(s * 4 + i, 16, stride=8), :] for i in range(4)]
    found = []
    for f in range(5):
        parts = []
        for g in range(3):
            c = 3 * f + g
            shift = (g - c) % 4 * 32
            parts.append(pltpu.roll(rows[c // 4], shift, axis=1) if shift else rows[c // 4])
        found.append(jnp.where(quarter == 0, parts[0], jnp.where(quarter == 1, parts[1], parts[2])))
    return found


def spread_ghosts(s, faces, gp, gx, gy, gz):
    lane = lane_ids()
    z = lax.rem(lane, 32)
    left = lane < 64
    lane16 = lane_ids(16)
    y_pick = 32 + jnp.where(lane16 >= 96, 16, 0) + lax.rem(lane16, 32) // 2
    z_pick = jnp.where(z == 0, 64, 80)
    for f in range(5):
        gp[s, f] = faces[f]
    for f in range(5):
        even = gp[s, f, pl.ds(0, 8, stride=2), :]
        odd = gp[s, f, pl.ds(1, 8, stride=2), :]
        for end in range(2):
            picks = [take(v, 16 * end + z // 2) for v in (even, odd)]
            gx[s, f, end] = jnp.where(left, picks[0], picks[1])
        lines = take(faces[f], y_pick)
        for k in range(16):
            picks = [take(v, z_pick + k) for v in (even, odd)]
            gz[s, f, k] = jnp.where(left, picks[0], picks[1])
            gy[s, f, k] = jnp.broadcast_to(lines[k : k + 1], (8, 128))


def fine_pass(state, gx, gy, gz, put, put_sums):
    lane = lane_ids()
    sub = lax.broadcasted_iota(I32, (8, 128), 0)
    z = lax.rem(lane, 32)
    y_first = (sub == 0) & (lane < 32)
    y_last = (sub == 7) & (lane >= 96)
    z_first = z == 0
    z_last = z == 31
    y_sign = jnp.where(y_last, 1.0, -1.0).astype(F32)
    z_sign = jnp.where(z_last, 1.0, -1.0).astype(F32)

    def one_pair(s, k, below):
        ghost_y = [gy[s, f, k] for f in range(5)]
        ghost_z = [gz[s, f, k] for f in range(5)]
        mids = [[state[s, f, 2 * k + p] for f in range(5)] for p in range(2)]
        at_end = jnp.broadcast_to(k, (8, 128)) == 15
        mids.append(
            [
                jnp.where(at_end, gx[s, f, 1], state[s, f, 2 * k + 2 - 2 * (k // 15)])
                for f in range(5)
            ]
        )
        ghost_y = side(ghost_y, 1)
        ghost_z = side(ghost_z, 2)
        pres = [prims(mid) for mid in mids]
        sides = [side(mids[p], 0, pres[p]) for p in range(3)]
        results, edges_y, edges_z = [], [], []
        for p in range(2):
            above = twice_flux(sides[p], sides[p + 1])
            diff_y, edge_y = along(mids[p], pres[p], 1, y_up, y_down, y_first, y_last, y_sign, ghost_y)
            diff_z, edge_z = along(mids[p], pres[p], 2, z_up, z_down, z_first, z_last, z_sign, ghost_z)
            results.append(
                [
                    mids[p][f] - 0.025 * ((above[f] - below[f]) + diff_y[f] + diff_z[f])
                    for f in range(5)
                ]
            )
            below = above
            edges_y.append(edge_y)
            edges_z.append(edge_z)
        sum_y = [edges_y[0][f] + edges_y[1][f] for f in range(5)]
        sum_z = [edges_z[0][f] + edges_z[1][f] for f in range(5)]
        return below, results, sum_y, sum_z

    starts = []
    for s in range(2):
        ghost_low = side([gx[s, f, 0] for f in range(5)], 0)
        plane0 = side([state[s, f, 0] for f in range(5)], 0)
        starts.append(twice_flux(ghost_low, plane0))

    def pairs(k, carry):
        found = [one_pair(s, k, carry[s]) for s in range(2)]
        for s in range(2):
            put(s, k, found[s][1])
            put_sums(s, k, found[s][2], found[s][3])
        return tuple(found[0][0]), tuple(found[1][0])

    ends = lax.fori_loop(0, 16, pairs, (tuple(starts[0]), tuple(starts[1])), unroll=2)
    return starts, ends


def front_kernel(
    tab, c_ref, fine_ref, new_ref, got_old, got_new, fc_ref, state, fx, fy, fz,
    buf, gp, gx_old, gy_old, gz_old, fine_sem,
    old, new, zc, y_send, c_send, hy, hc, pk, mid_old, mid_new, sel,
    copy_sem, halo_send, halo_recv, sem_a, sem_b, sem_c, sem_d, own_sem,
):
    gx, gy, xs, ys = neighbours()
    me = gx
    others = [lax.rem(me + step, NGX) for step in range(1, NGX)]
    loads = []
    for x in range(16):
        loads.append(
            pltpu.make_async_copy(
                c_ref.at[:, pl.ds(32 * x, 32), :],
                old.at[:, pl.ds((x + 2) * YE + 8, 32), :],
                copy_sem.at[x],
            )
        )
    for copy in loads:
        copy.start()
    fine_loads = [
        pltpu.make_async_copy(
            fine_ref.at[s, :, :, :, pl.ds(128 * k, 128)],
            buf.at[s, :, :, pl.ds(8 * k, 8), :],
            fine_sem.at[s, k],
        )
        for s in range(2)
        for k in range(8)
    ]
    for copy in fine_loads:
        copy.start()
    around = [(gx, ys[0]), (gx, ys[1])] + [(xs[a], ys[b]) for a in range(2) for b in range(2)]
    barrier = pltpu.get_barrier_semaphore()
    greeted = [(other, gy) for other in others] + around
    for device in greeted:
        pl.semaphore_signal(barrier, inc=1, device_id=device, device_id_type=MESH)
    c_send[...] = jnp.zeros_like(c_send)
    for copy in loads:
        copy.wait()
    for end in range(2):
        for f in range(5):
            for r in range(2):
                y_send[end, f, r] = old[f, pl.ds(2 * YE + 8 + 30 * end + r, 16, stride=YE), :]
    for a in range(2):
        for b in range(2):
            for f in range(5):
                c_send[2 * a + b, pl.ds(f, 1), :] = old[
                    f, pl.ds((2 + 15 * a) * YE + 8 + 31 * b, 1), :
                ]
    pl.semaphore_wait(barrier, len(greeted))
    halos = []

    def send(src, dst, device):
        number = len(halos)
        copy = pltpu.make_async_remote_copy(
            src_ref=src,
            dst_ref=dst,
            send_sem=halo_send.at[number],
            recv_sem=halo_recv.at[number],
            device_id=device,
            device_id_type=MESH,
        )
        copy.start()
        halos.append(copy)

    for plane, xi, where in ((0, 18, 0), (15, 1, 1), (1, 19, 0), (14, 0, 1)):
        send(
            c_ref.at[:, pl.ds(32 * plane, 32), :],
            old.at[:, pl.ds(xi * YE + 8, 32), :],
            (xs[where], gy),
        )
    for end in range(2):
        send(y_send.at[end], hy.at[1 - end], (gx, ys[end]))
    for a in range(2):
        for b in range(2):
            send(c_send.at[2 * a + b], hc.at[3 - 2 * a - b], (xs[a], ys[b]))

    lane16 = lane_ids(16)
    is_lo = lax.rem(lane16, 32) < 16
    quarter = lane16 // 32
    sign = jnp.where(is_lo, 1.0, -1.0).astype(F32)
    in16 = lax.rem(lane_ids(32), 16)
    zpick = (lane_ids(32) - in16 + 15, lane_ids(32) - in16)

    def advance(mid, xm, xp, ym, yp):
        pre = prims(mid)
        cx = side(mid, 0, pre)
        diff = twice_flux(cx, side(xp, 0))
        low = twice_flux(side(xm, 0), cx)
        total = [a - b for a, b in zip(diff, low)]
        cy = side(mid, 1, pre)
        up = twice_flux(cy, side(yp, 1))
        low = twice_flux(side(ym, 1), cy)
        total = [t + (a - b) for t, a, b in zip(total, up, low)]
        cz = side(mid, 2, pre)
        next_vel = pltpu.roll(pre[0][2], 127, axis=1)
        next_p = pltpu.roll(pre[1], 127, axis=1)
        next_u = [pltpu.roll(v, 127, axis=1) for v in mid]
        nz = (next_u, flow(next_u, next_vel, next_p, 2), pltpu.roll(cz[2], 127, axis=1))
        up = twice_flux(cz, nz)
        total = [t + (a - pltpu.roll(a, 1, axis=1)) for t, a in zip(total, up)]
        return [u - 0.025 * t for u, t in zip(mid, total)]

    def tiles(bases, stride=None):
        def rows(start):
            if stride is None:
                return [old[f, pl.ds(start, 8), :] for f in range(5)]
            return [old[f, pl.ds(start, 8, stride=stride), :] for f in range(5)]

        results = [
            advance(rows(base), rows(base - YE), rows(base + YE), rows(base - 1), rows(base + 1))
            for base in bases
        ]
        for base, result in zip(bases, results):
            for f in range(5):
                if stride is None:
                    new[f, pl.ds(base, 8), :] = result[f]
                else:
                    new[f, pl.ds(base, 8, stride=stride), :] = result[f]

    def inner_plane(xi, carry):
        tiles([xi * YE + 16, xi * YE + 24])
        return carry

    def outer_plane(xi, carry):
        tiles([xi * YE + 8, xi * YE + 32])
        return carry

    def compress(when, source):
        def field(f, carry):
            for end in range(2):
                acc = None
                for x in range(16):
                    plane = source[f, pl.ds((2 + x) * YE + 8, 32), :]
                    picked = take(plane, zpick[end])
                    acc = picked if acc is None else jnp.where(in16 == x, picked, acc)
                zc[when, f, end] = acc
            return carry

        lax.fori_loop(0, 5, field, 0)

    lax.fori_loop(3, 17, inner_plane, 0)
    compress(0, old)
    for copy in halos:
        copy.wait()
    for f in range(5):
        for r in range(2):
            old[f, pl.ds(2 * YE + 6 + r, 16, stride=YE), :] = hy[0, f, r]
            old[f, pl.ds(2 * YE + 40 + r, 16, stride=YE), :] = hy[1, f, r]
        for a, xi in ((0, 1), (1, 18)):
            for b, yi in ((0, 7), (1, 40)):
                old[f, pl.ds(xi * YE + yi, 1), :] = hc[2 * a + b, pl.ds(f, 1), :]

    def groups(source, when, outer, y0, z0):
        z0 = jnp.broadcast_to(z0, (16, 128))
        group = (lane16 - z0 + 128) % 128 // 16
        masks = [group == g for g in range(5)]
        bits = [(z0 // (16 << b)) % 2 == 1 for b in range(3)]
        upper = jnp.broadcast_to(y0, (16, 128)) > 0
        x_at = (1, 18) if outer else (2, 17)
        y_at = (7, 24) if outer else (8, 23)
        found = []
        for f in range(5):
            faces = [
                jnp.where(
                    upper,
                    source[f, pl.ds(xi * YE + 24, 16), :],
                    source[f, pl.ds(xi * YE + 8, 16), :],
                )
                for xi in x_at
            ]
            for yi in y_at:
                faces.append(
                    jnp.where(
                        upper,
                        source[f, pl.ds(2 * YE + yi + 16, 16, stride=YE), :],
                        source[f, pl.ds(2 * YE + yi, 16, stride=YE), :],
                    )
                )
            tops, bottoms = (
                jnp.where(upper, zc[when, f, end, pl.ds(16, 16), :], zc[when, f, end, pl.ds(0, 16), :])
                for end in range(2)
            )
            faces += [tops, bottoms] if outer else [bottoms, tops]
            shifts = (0, 16, 32, 48) + ((80, 64) if outer else (64, 80))
            value = pltpu.roll(faces[5], shifts[5], axis=1)
            for g in range(5):
                moved = pltpu.roll(faces[g], shifts[g], axis=1) if shifts[g] else faces[g]
                value = jnp.where(masks[g], moved, value)
            for b in range(3):
                value = jnp.where(bits[b], pltpu.roll(value, 128 - (16 << b), axis=1), value)
            found.append(value)
        return found

    def extract(when, source):
        def one_rank(r, carry):
            y0 = tab[96 + r]
            v = groups(source, when, True, y0, tab[100 + r])
            rows = [
                jnp.where(quarter < 3, v[0], pltpu.roll(v[1], 96, axis=1)),
                jnp.where(quarter < 2, pltpu.roll(v[1], 96, axis=1), pltpu.roll(v[2], 64, axis=1)),
                jnp.where(quarter < 1, pltpu.roll(v[2], 64, axis=1), pltpu.roll(v[3], 32, axis=1)),
                v[4],
            ]
            for i in range(4):
                pk[when, pl.ds(r * 4 + i, 16, stride=16), :] = rows[i]
            return carry

        lax.fori_loop(0, MOST, one_rank, 0)

    mids = (mid_old, mid_new)

    def scatter(when):
        own = pltpu.make_async_copy(
            pk.at[when, pl.ds(16 * me, 16), :], mids[when].at[pl.ds(16 * me, 16), :], own_sem.at[when]
        )
        own.start()
        copies = [own]
        for number, other in enumerate(others):
            copy = pltpu.make_async_remote_copy(
                src_ref=pk.at[when, pl.ds(16 * other, 16), :],
                dst_ref=mids[when].at[pl.ds(16 * me, 16), :],
                send_sem=sem_a.at[when, number],
                recv_sem=sem_b.at[when, number],
                device_id=(other, gy),
                device_id_type=MESH,
            )
            copy.start()
            copies.append(copy)
        return copies

    def forward(when, out_ref):
        def choose(d, carry):
            for s in range(2):
                at = tab[2 * d + s]
                sel[when, pl.ds(8 * d + 4 * s, 4), :] = mids[when][pl.ds(4 * at, 4), :]
            return carry

        lax.fori_loop(0, NGX, choose, 0)
        own = pltpu.make_async_copy(
            sel.at[when, pl.ds(8 * me, 8), :], out_ref.at[pl.ds(8 * me, 8), :], own_sem.at[2 + when]
        )
        own.start()
        copies = [own]
        for number, other in enumerate(others):
            copy = pltpu.make_async_remote_copy(
                src_ref=sel.at[when, pl.ds(8 * other, 8), :],
                dst_ref=out_ref.at[pl.ds(8 * me, 8), :],
                send_sem=sem_c.at[when, number],
                recv_sem=sem_d.at[when, number],
                device_id=(other, gy),
                device_id_type=MESH,
            )
            copy.start()
            copies.append(copy)
        return copies

    extract(0, old)
    old_first = scatter(0)
    lax.fori_loop(3, 17, outer_plane, 0)
    for xi in (1, 2, 17, 18):
        tiles([xi * YE + 8, xi * YE + 16])
        tiles([xi * YE + 24, xi * YE + 32])
    for yi in (7, 40):
        tiles([2 * YE + yi, 10 * YE + yi], YE)
    writes = []
    for x in range(16):
        writes.append(
            pltpu.make_async_copy(
                new.at[:, pl.ds((x + 2) * YE + 8, 32), :],
                new_ref.at[:, pl.ds(32 * x, 32), :],
                copy_sem.at[x],
            )
        )
    compress(1, new)
    extract(1, new)
    new_first = scatter(1)
    for copy in old_first:
        copy.wait()
    old_second = forward(0, got_old)
    for copy in writes:
        copy.start()

    def by_normal(a, b, c):
        return jnp.where(quarter == 0, a, jnp.where(quarter == 1, b, c))

    def normal_side(state):
        vel, pressure, sound = prims(state)
        along = by_normal(*vel)
        flows = [
            by_normal(state[1], state[2], state[3]),
            state[1] * along + jnp.where(quarter == 0, pressure, 0.0),
            state[2] * along + jnp.where(quarter == 1, pressure, 0.0),
            state[3] * along + jnp.where(quarter >= 2, pressure, 0.0),
            (state[4] + pressure) * along,
        ]
        return state, flows, jnp.abs(along) + sound

    def face_flux(r, carry):
        y0 = tab[96 + r]
        out = groups(old, 0, True, y0, tab[100 + r])
        ins = groups(old, 0, False, y0, tab[100 + r])
        a, b = normal_side(out), normal_side(ins)
        fastest = jnp.maximum(a[2], b[2]) * sign
        for f in range(5):
            fc_ref[r, f] = 0.5 * ((a[1][f] + b[1][f]) - fastest * (ins[f] - out[f]))
        return carry

    lax.fori_loop(0, MOST, face_flux, 0)
    for copy in fine_loads:
        copy.wait()
    for s in range(2):
        for x in range(32):
            for f in range(5):
                state[s, f, x] = buf[s, f, x // 8, pl.ds(x % 8, 8, stride=8), :]
    for copy in new_first:
        copy.wait()
    new_second = forward(1, got_new)
    for copy in old_second:
        copy.wait()
    for s in range(2):
        spread_ghosts(s, unpack_ghosts(got_old, s), gp, gx_old, gy_old, gz_old)

    def put(s, k, results):
        for f in range(5):
            for p in range(2):
                state[s, f, 2 * k + p] = results[p][f]

    def put_sums(s, k, sum_y, sum_z):
        for f in range(5):
            fy[s, f, k] = sum_y[f]
            fz[s, f, k] = sum_z[f]

    starts, ends = fine_pass(state, gx_old, gy_old, gz_old, put, put_sums)
    for s in range(2):
        for f in range(5):
            fx[s, 0, f] = starts[s][f]
            fx[s, 1, f] = ends[s][f]
    for copy in new_second + writes:
        copy.wait()


def front(tab, coarse, fine):
    dma = pltpu.SemaphoreType.DMA
    return pl.pallas_call(
        front_kernel,
        out_shape=(
            jax.ShapeDtypeStruct((5, 512, 128), F32),
            jax.ShapeDtypeStruct((128, 128), F32),
            jax.ShapeDtypeStruct((128, 128), F32),
            jax.ShapeDtypeStruct((MOST, 5, 16, 128), F32),
            jax.ShapeDtypeStruct((2, 5, 32, 8, 128), F32),
            jax.ShapeDtypeStruct((2, 2, 5, 8, 128), F32),
            jax.ShapeDtypeStruct((2, 5, 16, 8, 128), F32),
            jax.ShapeDtypeStruct((2, 5, 16, 8, 128), F32),
        ),
        in_specs=[
            pl.BlockSpec(memory_space=SMEM),
            pl.BlockSpec(memory_space=pltpu.HBM),
            pl.BlockSpec(memory_space=pltpu.HBM),
        ],
        out_specs=(pl.BlockSpec(memory_space=pl.ANY),) + (pl.BlockSpec(memory_space=VMEM),) * 7,
        scratch_shapes=[
            VMEM((2, 5, 4, 64, 128), F32),
            VMEM((2, 5, 16, 128), F32),
            VMEM((2, 5, 2, 8, 128), F32),
            VMEM((2, 5, 16, 8, 128), F32),
            VMEM((2, 5, 16, 8, 128), F32),
            dma((2, 8)),
            VMEM((5, XE * YE, 128), F32),
            VMEM((5, XE * YE, 128), F32),
            VMEM((2, 5, 2, 32, 128), F32),
            VMEM((2, 5, 2, 16, 128), F32),
            VMEM((4, 8, 128), F32),
            VMEM((2, 5, 2, 16, 128), F32),
            VMEM((4, 8, 128), F32),
            VMEM((2, 256, 128), F32),
            VMEM((256, 128), F32),
            VMEM((256, 128), F32),
            VMEM((2, 128, 128), F32),
            dma((16,)),
            dma((10,)),
            dma((10,)),
            dma((2, NGX - 1)),
            dma((2, NGX - 1)),
            dma((2, NGX - 1)),
            dma((2, NGX - 1)),
            dma((4,)),
        ],
        compiler_params=pltpu.CompilerParams(
            collective_id=1, has_side_effects=True, vmem_limit_bytes=LIMIT
        ),
    )(tab, coarse, fine)


def fine_kernel(
    state, got_old, got_new, fx_in, fy_in, fz_in, out_ref, rec,
    buf, gp, gx, gy, gz, fx, fy, fz, fy_low, fy_high, av, fs, out_sem,
):
    lane = lane_ids()
    z = lax.rem(lane, 32)
    lane16 = lane_ids(16)
    in32 = lax.rem(lane16, 32)
    for s in range(2):
        before, after = unpack_ghosts(got_old, s), unpack_ghosts(got_new, s)
        spread_ghosts(s, [0.5 * (a + b) for a, b in zip(before, after)], gp, gx, gy, gz)

    def put(s, k, results):
        for f in range(5):
            for p in range(2):
                x = 2 * k + p
                buf[s, f, x // 8, pl.ds(lax.rem(x, 8), 8, stride=8), :] = results[p][f]
            av[s, f, k] = results[0][f] + results[1][f]

    def put_sums(s, k, sum_y, sum_z):
        for f in range(5):
            fy[s, f, k] = sum_y[f]
            fz[s, f, k] = sum_z[f]

    starts, ends = fine_pass(state, gx, gy, gz, put, put_sums)
    copies = [
        pltpu.make_async_copy(
            buf.at[s, :, :, pl.ds(8 * k, 8), :],
            out_ref.at[s, :, :, :, pl.ds(128 * k, 128)],
            out_sem.at[s, k],
        )
        for s in range(2)
        for k in range(8)
    ]
    for copy in copies:
        copy.start()
    is_lo = z < 16
    fold = 2 * lax.rem(lane, 16)
    slot_of = lax.rem(lane // 32, 2) * 2 + lax.rem(lane, 2)
    half_lane = lax.rem(lane, 64)
    z_place = jnp.where(half_lane < 31, half_lane, half_lane - 31)
    for s in range(2):
        for f in range(5):
            loaded = [av[s, f, k] for k in range(16)]
            loaded = [v + pltpu.roll(v, 96, axis=1) for v in loaded]
            loaded = [0.125 * (v + z_up(v)) for v in loaded]
            for xq in range(4):
                packed = loaded[4 * xq]
                for j in range(1, 4):
                    moved = pltpu.roll(loaded[4 * xq + j], (j // 2) * 32 + j % 2, axis=1)
                    packed = jnp.where(slot_of == j, moved, packed)
                v = 4 * f + xq
                rec[pl.ds((v // 2) * 32 + s * 16 + (v % 2) * 8, 8), :] = packed
            loaded = [fz[s, f, k] + fz_in[s, f, k] for k in range(16)]
            packed = None
            for k in range(16):
                v = loaded[k] + pltpu.roll(loaded[k], 96, axis=1)
                if k == 0:
                    packed = v
                else:
                    packed = jnp.where(z_place == k, pltpu.roll(v, k, axis=1), packed)
            fz[s, f, 0] = packed
            lows = fy[s, f, :, 0, :] + fy_in[s, f, :, 0, :]
            highs = fy[s, f, :, 7, :] + fy_in[s, f, :, 7, :]
            fy_low[s, f] = lows + pltpu.roll(lows, 127, axis=1)
            fy_high[s, f] = highs + pltpu.roll(highs, 127, axis=1)
            for end, added in enumerate((starts, ends)):
                v = fx_in[s, end, f] + added[s][f]
                v = v + pltpu.roll(v, 96, axis=1)
                fx[s, end, f] = v + z_up(v)
        rec[pl.ds(15 * 32 + s * 16, 16), :] = jnp.zeros((16, 128), F32)
    fold16 = 2 * lax.rem(lane16, 16)
    for s in range(2):
        for f in range(5):
            y_part = jnp.where(
                in32 < 16, take(fy_low[s, f], fold16), take(fy_high[s, f], 96 + fold16)
            )
            outer = [fx[s, end, f] for end in range(2)]
            packed = fz[s, f, 0]
            for h in range(2):
                picked = jnp.where(is_lo, take(outer[0], h * 64 + fold), take(outer[1], h * 64 + fold))
                z_part = take(packed, h * 64 + jnp.where(is_lo, 0, 31) + lax.rem(lane, 16))
                fs[s, f, pl.ds(h, 8, stride=2), :] = jnp.where(lane < 32, picked, z_part)
            whole = jnp.where((lane16 >= 32) & (lane16 < 64), y_part, fs[s, f])
            rec[pl.ds((10 + f) * 32 + s * 16, 16), :] = whole * 0.0625
    for copy in copies:
        copy.wait()


def second_step(state, got_old, got_new, fx, fy, fz):
    return pl.pallas_call(
        fine_kernel,
        out_shape=(
            jax.ShapeDtypeStruct((2, 5, 4, 8, 1024), F32),
            jax.ShapeDtypeStruct((512, 128), F32),
        ),
        in_specs=[pl.BlockSpec(memory_space=VMEM)] * 6,
        out_specs=(pl.BlockSpec(memory_space=pl.ANY), pl.BlockSpec(memory_space=VMEM)),
        scratch_shapes=[
            VMEM((2, 5, 4, 64, 128), F32),
            VMEM((2, 5, 16, 128), F32),
            VMEM((2, 5, 2, 8, 128), F32),
            VMEM((2, 5, 16, 8, 128), F32),
            VMEM((2, 5, 16, 8, 128), F32),
            VMEM((2, 2, 5, 8, 128), F32),
            VMEM((2, 5, 16, 8, 128), F32),
            VMEM((2, 5, 16, 8, 128), F32),
            VMEM((2, 5, 16, 128), F32),
            VMEM((2, 5, 16, 128), F32),
            VMEM((2, 5, 16, 8, 128), F32),
            VMEM((2, 5, 16, 128), F32),
            pltpu.SemaphoreType.DMA((2, 8)),
        ],
        compiler_params=pltpu.CompilerParams(vmem_limit_bytes=LIMIT),
    )(state, got_old, got_new, fx, fy, fz)


def back_kernel(
    tab, rec, fc_ref, new_ref, out_ref,
    mid, sel, back, zs_buf, xs_buf, ys_buf, xa, ya,
    new_sem, sem_a, sem_b, sem_c, sem_d, own_sem, swap_send, swap_recv,
):
    gx, gy, xs, ys = neighbours()
    me = gx
    others = [lax.rem(me + step, NGX) for step in range(1, NGX)]
    load = pltpu.make_async_copy(new_ref, out_ref, new_sem)
    load.start()
    greet([(other, gy) for other in others] + [(gx, ys[0]), (gx, ys[1])])

    def exchange(src, dst, size, sem_s, sem_r, own_at):
        own = pltpu.make_async_copy(
            src.at[pl.ds(size * me, size), :], dst.at[pl.ds(size * me, size), :], own_sem.at[own_at]
        )
        own.start()
        copies = [own]
        for number, other in enumerate(others):
            copy = pltpu.make_async_remote_copy(
                src_ref=src.at[pl.ds(size * other, size), :],
                dst_ref=dst.at[pl.ds(size * me, size), :],
                send_sem=sem_s.at[number],
                recv_sem=sem_r.at[number],
                device_id=(other, gy),
                device_id_type=MESH,
            )
            copy.start()
            copies.append(copy)
        for copy in copies:
            copy.wait()

    exchange(rec, mid, 32, sem_a, sem_b, 0)

    def choose(i, carry):
        sel[pl.ds(16 * i, 16), :] = mid[pl.ds(16 * tab[32 + i], 16), :]
        return carry

    lax.fori_loop(0, NGX * MOST, choose, 0)
    exchange(sel, back, 64, sem_c, sem_d, 1)

    lane = lane_ids()
    lane16 = lane_ids(16)
    sign = jnp.where(lax.rem(lane16, 32) < 16, -0.05, 0.05).astype(F32)
    count = tab[104]
    y0s = [jnp.where(r < count, tab[96 + r], -1) for r in range(MOST)]
    z0s = [tab[100 + r] for r in range(MOST)]

    rest16 = lax.rem(lane16, 16)
    wanted = [
        [
            (lane16 >= z0s[r]) & (lane16 < z0s[r] + 16) & (jnp.broadcast_to(y0s[r], (16, 128)) == 16 * half)
            for half in range(2)
        ]
        for r in range(MOST)
    ]

    def correct(f, carry):
        values = [
            sign * (back[pl.ds((10 + f) * 64 + r * 16, 16), :] - fc_ref[r, f]) for r in range(MOST)
        ]
        for face in range(6):
            picks = [take(value, rest16 + 16 * face) for value in values]
            for half in range(2):
                total = jnp.zeros((16, 128), F32)
                for r in range(MOST):
                    total = jnp.where(wanted[r][half], picks[r], total)
                if face < 2:
                    xs_buf[face, f, pl.ds(16 * half, 16), :] = total
                elif face < 4:
                    ys_buf[half + 2 * (face - 2), f] = total
                else:
                    zs_buf[face - 4, f, pl.ds(16 * half, 16), :] = total
        return carry

    lax.fori_loop(0, 5, correct, 0)
    swaps = []
    for number, (src, dst, device) in enumerate(
        (
            (xs_buf.at[0], xa.at[1], (xs[0], gy)),
            (xs_buf.at[1], xa.at[0], (xs[1], gy)),
            (ys_buf.at[0], ya.at[1], (gx, ys[0])),
            (ys_buf.at[3], ya.at[0], (gx, ys[1])),
        )
    ):
        copy = pltpu.make_async_remote_copy(
            src_ref=src,
            dst_ref=dst,
            send_sem=swap_send.at[number],
            recv_sem=swap_recv.at[number],
            device_id=device,
            device_id_type=MESH,
        )
        copy.start()
        swaps.append(copy)
    load.wait()

    rest = lax.rem(lane, 16)
    insides = [[wanted[r][half][0:8] for r in range(MOST)] for half in range(2)]

    def assemble(i, carry):
        f, xq = i // 4, lax.rem(i, 4)
        packed = [
            back[pl.ds((i // 2) * 64 + r * 16 + lax.rem(i, 2) * 8, 8), :] for r in range(MOST)
        ]
        for h in range(2):
            faces = [
                [zs_buf[end, f, pl.ds(16 * half + h, 8, stride=2), :] for end in range(2)]
                for half in range(2)
            ]
            for j in range(4):
                x = 4 * xq + j
                pick = 2 * rest + (h * 64 + (j // 2) * 32 + j % 2)
                picks = [take(packed[r], pick) for r in range(MOST)]
                low_at = (lane + 1 + x) % 128
                high_at = (lane + 112 + x) % 128
                for half in range(2):
                    rows = pl.ds(32 * x + 16 * half + h, 8, stride=2)
                    value = out_ref[f, rows, :]
                    low = take(faces[half][0], low_at)
                    high = take(faces[half][1], high_at)
                    value = value + jnp.where(rest == 15, low, jnp.where(rest == 0, high, 0.0))
                    for r in range(MOST):
                        value = jnp.where(insides[half][r], picks[r], value)
                    out_ref[f, rows, :] = value
        return carry

    lax.fori_loop(0, 20, assemble, 0)
    covered = []
    for half in range(2):
        mask = wanted[0][half]
        for r in range(1, MOST):
            mask = mask | wanted[r][half]
        covered.append(mask)
    for copy in swaps:
        copy.wait()
    for f in range(5):
        for end in range(2):
            for half in range(2):
                rows = pl.ds(480 * end + 16 * half, 16)
                out_ref[f, rows, :] = out_ref[f, rows, :] + jnp.where(
                    covered[half], 0.0, xa[end, f, pl.ds(16 * half, 16), :]
                )
        for y, values in ((0, ya[0, f]), (31, ya[1, f]), (15, ys_buf[1, f]), (16, ys_buf[2, f])):
            rows = pl.ds(y, 16, stride=32)
            out_ref[f, rows, :] = out_ref[f, rows, :] + jnp.where(covered[y // 16], 0.0, values)


def assemble_all(tab, rec, fc, new):
    dma = pltpu.SemaphoreType.DMA
    return pl.pallas_call(
        back_kernel,
        out_shape=jax.ShapeDtypeStruct((5, 512, 128), F32),
        in_specs=[
            pl.BlockSpec(memory_space=SMEM),
            pl.BlockSpec(memory_space=VMEM),
            pl.BlockSpec(memory_space=VMEM),
            pl.BlockSpec(memory_space=pl.ANY),
        ],
        out_specs=pl.BlockSpec(memory_space=VMEM),
        scratch_shapes=[
            VMEM((512, 128), F32),
            VMEM((1024, 128), F32),
            VMEM((1024, 128), F32),
            VMEM((2, 5, 32, 128), F32),
            VMEM((2, 5, 32, 128), F32),
            VMEM((4, 5, 16, 128), F32),
            VMEM((2, 5, 32, 128), F32),
            VMEM((2, 5, 16, 128), F32),
            dma,
            dma((NGX - 1,)),
            dma((NGX - 1,)),
            dma((NGX - 1,)),
            dma((NGX - 1,)),
            dma((2,)),
            dma((4,)),
            dma((4,)),
        ],
        compiler_params=pltpu.CompilerParams(
            collective_id=2, has_side_effects=True, vmem_limit_bytes=LIMIT
        ),
    )(tab, rec, fc, new)


def per_device(coarse_state, fine_state, corners, slot_patch):
    coarse = coarse_state.reshape(5, 512, 128)
    tab = tables(jnp.transpose(corners, (2, 0, 1)), slot_patch)
    new, got_old, got_new, fc, state, fx, fy, fz = front(
        tab, coarse, fine_state.reshape(2, 5, 4, 8, 1024)
    )
    fine_next, rec = second_step(state, got_old, got_new, fx, fy, fz)
    out = assemble_all(tab, rec, fc, new)
    return out.reshape(coarse_state.shape), fine_next.reshape(fine_state.shape)


def solution(mesh):
    placed = (
        P(None, "gx", "gy", None),
        P("gx", "gy", None, None, None, None),
        P("gy", None, None),
        P("gy", None),
    )
    return jax.shard_map(
        per_device,
        mesh=mesh,
        in_specs=placed,
        out_specs=(P(None, "gx", "gy", None), P("gx", "gy", None, None, None, None)),
        check_vma=False,
    )
```

```python
import jax
import jax.numpy as jnp
from jax import lax
from jax.experimental import pallas as pl
from jax.experimental.pallas import tpu as pltpu
from jax.sharding import PartitionSpec as P

F32 = jnp.float32
I32 = jnp.int32
MESH = pl.DeviceIdType.MESH
VMEM = pltpu.VMEM
SMEM = pltpu.SMEM
NGX = 16
NGY = 8
MOST = 4
PCOL = 32
YE = 48
XE = 20
LIMIT = 48 * 1024 * 1024


def lane_ids(rows=8):
    return lax.broadcasted_iota(I32, (rows, 128), 1)


def take(values, idx):
    return jnp.take_along_axis(values, idx, axis=1)


def prims(state):
    inv = 1.0 / state[0]
    vel = [state[1] * inv, state[2] * inv, state[3] * inv]
    kinetic = 0.5 * (state[1] * vel[0] + state[2] * vel[1] + state[3] * vel[2])
    pressure = 0.4 * (state[4] - kinetic)
    sound = jnp.sqrt(1.4 * pressure * inv)
    return vel, pressure, sound


def flow(state, vel, pressure, normal):
    out = [state[1 + normal], state[1] * vel, state[2] * vel, state[3] * vel, (state[4] + pressure) * vel]
    out[1 + normal] = out[1 + normal] + pressure
    return out


def side(state, normal, pre=None):
    vel, pressure, sound = prims(state) if pre is None else pre
    return state, flow(state, vel[normal], pressure, normal), jnp.abs(vel[normal]) + sound


def twice_flux(low, high):
    fastest = jnp.maximum(low[2], high[2])
    return [
        (low[1][f] + high[1][f]) - fastest * (high[0][f] - low[0][f]) for f in range(5)
    ]


def neighbours():
    gx, gy = lax.axis_index("gx"), lax.axis_index("gy")
    xs = (lax.rem(gx + NGX - 1, NGX), lax.rem(gx + 1, NGX))
    ys = (lax.rem(gy + NGY - 1, NGY), lax.rem(gy + 1, NGY))
    return gx, gy, xs, ys


def greet(devices):
    barrier = pltpu.get_barrier_semaphore()
    for device in devices:
        pl.semaphore_signal(barrier, inc=1, device_id=device, device_id_type=MESH)
    pl.semaphore_wait(barrier, len(devices))


def tables_kernel(corners, holders, tab, rows):
    me = lax.axis_index("gx")
    for i in range(NGX * MOST):
        tab[32 + i] = 0
    for i in range(105, 128):
        tab[i] = 0
    mine, count, last, rank = 0, 0, -1, 0
    for q in range(PCOL):
        b = corners[0, 0, q] // 16
        rank = jnp.where(b == last, rank + 1, 0)
        last = b
        rows[q] = b * MOST + rank
        mine = mine + jnp.where(b < me, 1, 0)
        count = count + jnp.where(b == me, 1, 0)
    found = [rows[holders[0, i]] for i in range(PCOL)]
    for i in range(PCOL):
        tab[i] = found[i]
        tab[32 + found[i]] = i
    for r in range(MOST):
        q = jnp.minimum(mine + r, PCOL - 1)
        tab[96 + r] = lax.rem(corners[1, 0, q], 32)
        tab[100 + r] = corners[2, 0, q]
    tab[104] = count


def tables(corners, holders):
    return pl.pallas_call(
        tables_kernel,
        out_shape=jax.ShapeDtypeStruct((128,), I32),
        in_specs=[pl.BlockSpec(memory_space=SMEM)] * 2,
        out_specs=pl.BlockSpec(memory_space=SMEM),
        scratch_shapes=[SMEM((PCOL,), I32)],
    )(corners, holders)


def y_up(v):
    moved = pltpu.roll(v, 96, axis=1)
    return jnp.where(lane_ids() < 96, moved, pltpu.roll(moved, 7, axis=0))


def y_down(v):
    moved = pltpu.roll(v, 32, axis=1)
    return jnp.where(lane_ids() >= 32, moved, pltpu.roll(moved, 1, axis=0))


def z_up(v):
    return pltpu.roll(v, 127, axis=1)


def z_down(v):
    return pltpu.roll(v, 1, axis=1)


def along(mid, pre, normal, up, down, first, last, sign, ghost):
    cell = side(mid, normal, pre)
    shifted = [up(v) for v in mid]
    above = (shifted, flow(shifted, up(pre[0][normal]), up(pre[1]), normal), up(cell[2]))
    inner = twice_flux(cell, above)
    fastest = jnp.maximum(cell[2], ghost[2]) * sign
    edge = [(cell[1][f] + ghost[1][f]) - fastest * (ghost[0][f] - mid[f]) for f in range(5)]
    diff = [
        jnp.where(last, edge[f], inner[f]) - jnp.where(first, edge[f], down(inner[f]))
        for f in range(5)
    ]
    return diff, edge


def pack_rows(v):
    quarter = lane_ids(16) // 32
    return [
        jnp.where(quarter < 3, v[0], pltpu.roll(v[1], 96, axis=1)),
        jnp.where(quarter < 2, pltpu.roll(v[1], 96, axis=1), pltpu.roll(v[2], 64, axis=1)),
        jnp.where(quarter < 1, pltpu.roll(v[2], 64, axis=1), pltpu.roll(v[3], 32, axis=1)),
        v[4],
    ]


def unpack_rows(got, first, stride):
    quarter = lane_ids(16) // 32
    rows = [got[pl.ds(first + i, 16, stride=stride), :] for i in range(4)]
    found = []
    for f in range(5):
        parts = []
        for g in range(3):
            c = 3 * f + g
            shift = (g - c) % 4 * 32
            parts.append(pltpu.roll(rows[c // 4], shift, axis=1) if shift else rows[c // 4])
        found.append(jnp.where(quarter == 0, parts[0], jnp.where(quarter == 1, parts[1], parts[2])))
    return found


def spread_ghosts(s, faces, gp, gx, gy, gz):
    lane = lane_ids()
    z = lax.rem(lane, 32)
    left = lane < 64
    lane16 = lane_ids(16)
    y_pick = 32 + jnp.where(lane16 >= 96, 16, 0) + lax.rem(lane16, 32) // 2
    z_pick = jnp.where(z == 0, 64, 80)
    for f in range(5):
        gp[s, f] = faces[f]
    for f in range(5):
        even = gp[s, f, pl.ds(0, 8, stride=2), :]
        odd = gp[s, f, pl.ds(1, 8, stride=2), :]
        for end in range(2):
            picks = [take(v, 16 * end + z // 2) for v in (even, odd)]
            gx[s, f, end] = jnp.where(left, picks[0], picks[1])
        lines = take(faces[f], y_pick)
        for k in range(16):
            picks = [take(v, z_pick + k) for v in (even, odd)]
            gz[s, f, k] = jnp.where(left, picks[0], picks[1])
            gy[s, f, k] = jnp.broadcast_to(lines[k : k + 1], (8, 128))


def fine_pass(state, gx, gy, gz, put, put_sums):
    lane = lane_ids()
    sub = lax.broadcasted_iota(I32, (8, 128), 0)
    z = lax.rem(lane, 32)
    y_first = (sub == 0) & (lane < 32)
    y_last = (sub == 7) & (lane >= 96)
    z_first = z == 0
    z_last = z == 31
    y_sign = jnp.where(y_last, 1.0, -1.0).astype(F32)
    z_sign = jnp.where(z_last, 1.0, -1.0).astype(F32)

    def one_pair(s, k, below):
        ghost_y = [gy[s, f, k] for f in range(5)]
        ghost_z = [gz[s, f, k] for f in range(5)]
        mids = [[state[s, f, 2 * k + p] for f in range(5)] for p in range(2)]
        at_end = jnp.broadcast_to(k, (8, 128)) == 15
        mids.append(
            [
                jnp.where(at_end, gx[s, f, 1], state[s, f, 2 * k + 2 - 2 * (k // 15)])
                for f in range(5)
            ]
        )
        ghost_y = side(ghost_y, 1)
        ghost_z = side(ghost_z, 2)
        pres = [prims(mid) for mid in mids]
        sides = [side(mids[p], 0, pres[p]) for p in range(3)]
        results, edges_y, edges_z = [], [], []
        for p in range(2):
            above = twice_flux(sides[p], sides[p + 1])
            diff_y, edge_y = along(mids[p], pres[p], 1, y_up, y_down, y_first, y_last, y_sign, ghost_y)
            diff_z, edge_z = along(mids[p], pres[p], 2, z_up, z_down, z_first, z_last, z_sign, ghost_z)
            results.append(
                [
                    mids[p][f] - 0.025 * ((above[f] - below[f]) + diff_y[f] + diff_z[f])
                    for f in range(5)
                ]
            )
            below = above
            edges_y.append(edge_y)
            edges_z.append(edge_z)
        sum_y = [edges_y[0][f] + edges_y[1][f] for f in range(5)]
        sum_z = [edges_z[0][f] + edges_z[1][f] for f in range(5)]
        return below, results, sum_y, sum_z

    starts = []
    for s in range(2):
        ghost_low = side([gx[s, f, 0] for f in range(5)], 0)
        plane0 = side([state[s, f, 0] for f in range(5)], 0)
        starts.append(twice_flux(ghost_low, plane0))

    def pairs(k, carry):
        found = [one_pair(s, k, carry[s]) for s in range(2)]
        for s in range(2):
            put(s, k, found[s][1])
            put_sums(s, k, found[s][2], found[s][3])
        return tuple(found[0][0]), tuple(found[1][0])

    ends = lax.fori_loop(0, 16, pairs, (tuple(starts[0]), tuple(starts[1])), unroll=2)
    return starts, ends


def step_kernel(
    tab, c_ref, fine_ref, out_ref, fine_out,
    old, new, zc, y_send, c_send, hy, hc, pk, mid_old, mid_new, sel, got_old, got_new, fc_ref,
    buf, state, result, gp, gx_at, gy_at, gz_at, fx, fy, fz, fx2, fy2, fz2, fy_low, fy_high, av, fs,
    rec_f, mid_f, sel_f, back_f, rec_a, mid_a, sel_a, back_a, back_s,
    xs_buf, ys_buf, zs_buf, xa, ya,
    copy_sem, fine_sem, out_sem, halo_send, halo_recv, col_send, col_recv, own_sem, swap_send, swap_recv,
):
    gx, gy, xs, ys = neighbours()
    me = gx
    others = [lax.rem(me + step, NGX) for step in range(1, NGX)]
    loads = []
    for x in range(16):
        loads.append(
            pltpu.make_async_copy(
                c_ref.at[:, pl.ds(32 * x, 32), :],
                old.at[:, pl.ds((x + 2) * YE + 8, 32), :],
                copy_sem.at[x],
            )
        )
    for copy in loads:
        copy.start()
    fine_loads = [
        pltpu.make_async_copy(
            fine_ref.at[s, :, :, :, pl.ds(128 * k, 128)],
            buf.at[s, :, :, pl.ds(8 * k, 8), :],
            fine_sem.at[s, k],
        )
        for s in range(2)
        for k in range(8)
    ]
    for copy in fine_loads:
        copy.start()
    around = [(gx, ys[0]), (gx, ys[1])] + [(xs[a], ys[b]) for a in range(2) for b in range(2)]
    barrier = pltpu.get_barrier_semaphore()
    greeted = [(other, gy) for other in others] + around
    for device in greeted:
        pl.semaphore_signal(barrier, inc=1, device_id=device, device_id_type=MESH)
    c_send[...] = jnp.zeros_like(c_send)
    rec_a[...] = jnp.zeros_like(rec_a)
    for copy in loads:
        copy.wait()
    for end in range(2):
        for f in range(5):
            for r in range(2):
                y_send[end, f, r] = old[f, pl.ds(2 * YE + 8 + 30 * end + r, 16, stride=YE), :]
    for a in range(2):
        for b in range(2):
            for f in range(5):
                c_send[2 * a + b, pl.ds(f, 1), :] = old[
                    f, pl.ds((2 + 15 * a) * YE + 8 + 31 * b, 1), :
                ]
    pl.semaphore_wait(barrier, len(greeted))
    halos = []

    def send(src, dst, device):
        number = len(halos)
        copy = pltpu.make_async_remote_copy(
            src_ref=src,
            dst_ref=dst,
            send_sem=halo_send.at[number],
            recv_sem=halo_recv.at[number],
            device_id=device,
            device_id_type=MESH,
        )
        copy.start()
        halos.append(copy)

    def send_planes(planes):
        for plane, xi, where in planes:
            send(
                c_ref.at[:, pl.ds(32 * plane, 32), :],
                old.at[:, pl.ds(xi * YE + 8, 32), :],
                (xs[where], gy),
            )

    send_planes(((0, 18, 0), (15, 1, 1)))
    for end in range(2):
        send(y_send.at[end], hy.at[1 - end], (gx, ys[end]))
    for a in range(2):
        for b in range(2):
            send(c_send.at[2 * a + b], hc.at[3 - 2 * a - b], (xs[a], ys[b]))
    near = list(halos)
    send_planes(((1, 19, 0), (14, 0, 1)))
    far = halos[len(near) :]

    lane16 = lane_ids(16)
    is_lo = lax.rem(lane16, 32) < 16
    quarter = lane16 // 32
    sign = jnp.where(is_lo, 1.0, -1.0).astype(F32)
    in16 = lax.rem(lane_ids(32), 16)
    zpick = (lane_ids(32) - in16 + 15, lane_ids(32) - in16)

    def advance(mid, xm, xp, ym, yp):
        pre = prims(mid)
        cx = side(mid, 0, pre)
        diff = twice_flux(cx, side(xp, 0))
        low = twice_flux(side(xm, 0), cx)
        total = [a - b for a, b in zip(diff, low)]
        cy = side(mid, 1, pre)
        up = twice_flux(cy, side(yp, 1))
        low = twice_flux(side(ym, 1), cy)
        total = [t + (a - b) for t, a, b in zip(total, up, low)]
        cz = side(mid, 2, pre)
        next_vel = pltpu.roll(pre[0][2], 127, axis=1)
        next_p = pltpu.roll(pre[1], 127, axis=1)
        next_u = [pltpu.roll(v, 127, axis=1) for v in mid]
        nz = (next_u, flow(next_u, next_vel, next_p, 2), pltpu.roll(cz[2], 127, axis=1))
        up = twice_flux(cz, nz)
        total = [t + (a - pltpu.roll(a, 1, axis=1)) for t, a in zip(total, up)]
        return [u - 0.025 * t for u, t in zip(mid, total)]

    def tiles(bases, stride=None):
        def rows(start):
            if stride is None:
                return [old[f, pl.ds(start, 8), :] for f in range(5)]
            return [old[f, pl.ds(start, 8, stride=stride), :] for f in range(5)]

        results = [
            advance(rows(base), rows(base - YE), rows(base + YE), rows(base - 1), rows(base + 1))
            for base in bases
        ]
        for base, result in zip(bases, results):
            for f in range(5):
                if stride is None:
                    new[f, pl.ds(base, 8), :] = result[f]
                else:
                    new[f, pl.ds(base, 8, stride=stride), :] = result[f]

    def inner_plane(xi, carry):
        tiles([xi * YE + 16, xi * YE + 24])
        return carry

    def outer_plane(xi, carry):
        tiles([xi * YE + 8, xi * YE + 32])
        return carry

    def compress(when, source):
        def field(f, carry):
            for end in range(2):
                acc = None
                for x in range(16):
                    plane = source[f, pl.ds((2 + x) * YE + 8, 32), :]
                    picked = take(plane, zpick[end])
                    acc = picked if acc is None else jnp.where(in16 == x, picked, acc)
                zc[when, f, end] = acc
            return carry

        lax.fori_loop(0, 5, field, 0)

    lax.fori_loop(3, 17, inner_plane, 0)
    compress(0, old)
    for copy in near:
        copy.wait()
    for f in range(5):
        for r in range(2):
            old[f, pl.ds(2 * YE + 6 + r, 16, stride=YE), :] = hy[0, f, r]
            old[f, pl.ds(2 * YE + 40 + r, 16, stride=YE), :] = hy[1, f, r]
        for a, xi in ((0, 1), (1, 18)):
            for b, yi in ((0, 7), (1, 40)):
                old[f, pl.ds(xi * YE + yi, 1), :] = hc[2 * a + b, pl.ds(f, 1), :]

    def groups(source, when, outer, y0, z0):
        z0 = jnp.broadcast_to(z0, (16, 128))
        group = (lane16 - z0 + 128) % 128 // 16
        masks = [group == g for g in range(5)]
        bits = [(z0 // (16 << b)) % 2 == 1 for b in range(3)]
        upper = jnp.broadcast_to(y0, (16, 128)) > 0
        x_at = (1, 18) if outer else (2, 17)
        y_at = (7, 24) if outer else (8, 23)
        found = []
        for f in range(5):
            faces = [
                jnp.where(
                    upper,
                    source[f, pl.ds(xi * YE + 24, 16), :],
                    source[f, pl.ds(xi * YE + 8, 16), :],
                )
                for xi in x_at
            ]
            for yi in y_at:
                faces.append(
                    jnp.where(
                        upper,
                        source[f, pl.ds(2 * YE + yi + 16, 16, stride=YE), :],
                        source[f, pl.ds(2 * YE + yi, 16, stride=YE), :],
                    )
                )
            tops, bottoms = (
                jnp.where(upper, zc[when, f, end, pl.ds(16, 16), :], zc[when, f, end, pl.ds(0, 16), :])
                for end in range(2)
            )
            faces += [tops, bottoms] if outer else [bottoms, tops]
            shifts = (0, 16, 32, 48) + ((80, 64) if outer else (64, 80))
            value = pltpu.roll(faces[5], shifts[5], axis=1)
            for g in range(5):
                moved = pltpu.roll(faces[g], shifts[g], axis=1) if shifts[g] else faces[g]
                value = jnp.where(masks[g], moved, value)
            for b in range(3):
                value = jnp.where(bits[b], pltpu.roll(value, 128 - (16 << b), axis=1), value)
            found.append(value)
        return found

    def extract(when, source):
        def one_rank(r, carry):
            y0 = tab[96 + r]
            v = groups(source, when, True, y0, tab[100 + r])
            rows = pack_rows(v)
            for i in range(4):
                pk[when, pl.ds(r * 4 + i, 16, stride=16), :] = rows[i]
            return carry

        lax.fori_loop(0, MOST, one_rank, 0)

    mids = (mid_old, mid_new)

    def exchange(src, dst, size, number):
        own = pltpu.make_async_copy(
            src.at[pl.ds(size * me, size), :], dst.at[pl.ds(size * me, size), :], own_sem.at[number]
        )
        own.start()
        copies = [own]
        for at, other in enumerate(others):
            copy = pltpu.make_async_remote_copy(
                src_ref=src.at[pl.ds(size * other, size), :],
                dst_ref=dst.at[pl.ds(size * me, size), :],
                send_sem=col_send.at[number, at],
                recv_sem=col_recv.at[number, at],
                device_id=(other, gy),
                device_id_type=MESH,
            )
            copy.start()
            copies.append(copy)
        return copies

    def scatter(when):
        return exchange(pk.at[when], mids[when], 16, when)

    def forward(when, got):
        def choose(d, carry):
            for s in range(2):
                at = tab[2 * d + s]
                sel[when, pl.ds(8 * d + 4 * s, 4), :] = mids[when][pl.ds(4 * at, 4), :]
            return carry

        lax.fori_loop(0, NGX, choose, 0)
        return exchange(sel.at[when], got, 8, 2 + when)

    extract(0, old)
    old_first = scatter(0)
    lax.fori_loop(3, 17, outer_plane, 0)
    for copy in far:
        copy.wait()
    for xi in (1, 2, 17, 18):
        tiles([xi * YE + 8, xi * YE + 16])
        tiles([xi * YE + 24, xi * YE + 32])
    for yi in (7, 40):
        tiles([2 * YE + yi, 10 * YE + yi], YE)
    writes = []
    for x in range(16):
        writes.append(
            pltpu.make_async_copy(
                new.at[:, pl.ds((x + 2) * YE + 8, 32), :],
                out_ref.at[:, pl.ds(32 * x, 32), :],
                copy_sem.at[x],
            )
        )
    compress(1, new)
    extract(1, new)
    new_first = scatter(1)
    for copy in old_first:
        copy.wait()
    old_second = forward(0, got_old)
    for copy in writes:
        copy.start()

    def by_normal(a, b, c):
        return jnp.where(quarter == 0, a, jnp.where(quarter == 1, b, c))

    def normal_side(state):
        vel, pressure, sound = prims(state)
        along = by_normal(*vel)
        flows = [
            by_normal(state[1], state[2], state[3]),
            state[1] * along + jnp.where(quarter == 0, pressure, 0.0),
            state[2] * along + jnp.where(quarter == 1, pressure, 0.0),
            state[3] * along + jnp.where(quarter >= 2, pressure, 0.0),
            (state[4] + pressure) * along,
        ]
        return state, flows, jnp.abs(along) + sound

    def face_flux(r, carry):
        y0 = tab[96 + r]
        out = groups(old, 0, True, y0, tab[100 + r])
        ins = groups(old, 0, False, y0, tab[100 + r])
        a, b = normal_side(out), normal_side(ins)
        fastest = jnp.maximum(a[2], b[2]) * sign
        for f in range(5):
            fc_ref[r, f] = 0.5 * ((a[1][f] + b[1][f]) - fastest * (ins[f] - out[f]))
        return carry

    lax.fori_loop(0, MOST, face_flux, 0)
    for copy in fine_loads:
        copy.wait()
    for s in range(2):
        for x in range(32):
            for f in range(5):
                state[s, f, x] = buf[s, f, x // 8, pl.ds(x % 8, 8, stride=8), :]
    for copy in new_first:
        copy.wait()
    new_second = forward(1, got_new)
    for copy in old_second:
        copy.wait()
    for s in range(2):
        spread_ghosts(s, unpack_rows(got_old, 4 * s, 8), gp, gx_at, gy_at, gz_at)

    def put(s, k, results):
        for f in range(5):
            for p in range(2):
                state[s, f, 2 * k + p] = results[p][f]

    def put_sums(s, k, sum_y, sum_z):
        for f in range(5):
            fy[s, f, k] = sum_y[f]
            fz[s, f, k] = sum_z[f]

    starts, ends = fine_pass(state, gx_at, gy_at, gz_at, put, put_sums)
    for s in range(2):
        for f in range(5):
            fx[s, 0, f] = starts[s][f]
            fx[s, 1, f] = ends[s][f]
    for copy in new_second:
        copy.wait()
    for s in range(2):
        before, after = unpack_rows(got_old, 4 * s, 8), unpack_rows(got_new, 4 * s, 8)
        spread_ghosts(s, [0.5 * (a + b) for a, b in zip(before, after)], gp, gx_at, gy_at, gz_at)

    def put_last(s, k, results):
        for f in range(5):
            for p in range(2):
                result[s, f, 2 * k + p] = results[p][f]
            av[s, f, k] = results[0][f] + results[1][f]

    def put_last_sums(s, k, sum_y, sum_z):
        for f in range(5):
            fy2[s, f, k] = sum_y[f]
            fz2[s, f, k] = sum_z[f]

    starts, ends = fine_pass(state, gx_at, gy_at, gz_at, put_last, put_last_sums)

    lane = lane_ids()
    z = lax.rem(lane, 32)
    in32 = lax.rem(lane16, 32)
    z_is_lo = z < 16
    fold = 2 * lax.rem(lane, 16)
    fold16 = 2 * lax.rem(lane16, 16)
    half_lane = lax.rem(lane, 64)
    z_place = jnp.where(half_lane < 31, half_lane, half_lane - 31)
    for s in range(2):
        for f in range(5):
            loaded = [fz2[s, f, k] + fz[s, f, k] for k in range(16)]
            packed = None
            for k in range(16):
                v = loaded[k] + pltpu.roll(loaded[k], 96, axis=1)
                if k == 0:
                    packed = v
                else:
                    packed = jnp.where(z_place == k, pltpu.roll(v, k, axis=1), packed)
            fz2[s, f, 0] = packed
            lows = fy2[s, f, :, 0, :] + fy[s, f, :, 0, :]
            highs = fy2[s, f, :, 7, :] + fy[s, f, :, 7, :]
            fy_low[s, f] = lows + pltpu.roll(lows, 127, axis=1)
            fy_high[s, f] = highs + pltpu.roll(highs, 127, axis=1)
            for end, added in enumerate((starts, ends)):
                v = fx[s, end, f] + added[s][f]
                v = v + pltpu.roll(v, 96, axis=1)
                fx2[s, end, f] = v + z_up(v)
    for s in range(2):
        means = []
        for f in range(5):
            y_part = jnp.where(
                in32 < 16, take(fy_low[s, f], fold16), take(fy_high[s, f], 96 + fold16)
            )
            packed = fz2[s, f, 0]
            for h in range(2):
                picked = jnp.where(
                    z_is_lo,
                    take(fx2[s, 0, f], h * 64 + fold),
                    take(fx2[s, 1, f], h * 64 + fold),
                )
                z_part = take(packed, h * 64 + jnp.where(z_is_lo, 0, 31) + lax.rem(lane, 16))
                fs[s, f, pl.ds(h, 8, stride=2), :] = jnp.where(lane < 32, picked, z_part)
            whole = jnp.where((lane16 >= 32) & (lane16 < 64), y_part, fs[s, f])
            means.append(whole * 0.0625)
        rows = pack_rows(means)
        for i in range(4):
            rec_f[pl.ds(4 * s + i, 16, stride=8), :] = rows[i]
    flux_first = exchange(rec_f, mid_f, 8, 4)

    slot_of = lax.rem(lane // 32, 2) * 2 + lax.rem(lane, 2)
    for s in range(2):
        for f in range(5):
            loaded = [av[s, f, k] for k in range(16)]
            loaded = [v + pltpu.roll(v, 96, axis=1) for v in loaded]
            loaded = [0.125 * (v + z_up(v)) for v in loaded]
            for xq in range(4):
                packed = loaded[4 * xq]
                for j in range(1, 4):
                    moved = pltpu.roll(loaded[4 * xq + j], (j // 2) * 32 + j % 2, axis=1)
                    packed = jnp.where(slot_of == j, moved, packed)
                v = 4 * f + xq
                if v < 16:
                    rec_a[pl.ds(24 * v + 8 * s, 8), :] = packed
                else:
                    for c in range(4):
                        at = 24 * (4 * (v - 16) + c) + 16 + 2 * s
                        rec_a[pl.ds(at, 2), :] = packed[2 * c : 2 * c + 2]
    average_first = exchange(rec_a, mid_a, 24, 5)
    for s in range(2):
        for x in range(32):
            for f in range(5):
                buf[s, f, x // 8, pl.ds(x % 8, 8, stride=8), :] = result[s, f, x]
    fine_writes = [
        pltpu.make_async_copy(
            buf.at[s, :, :, pl.ds(8 * k, 8), :],
            fine_out.at[s, :, :, :, pl.ds(128 * k, 128)],
            out_sem.at[s, k],
        )
        for s in range(2)
        for k in range(8)
    ]
    for copy in fine_writes:
        copy.start()

    for copy in flux_first:
        copy.wait()

    def choose_flux(i, carry):
        sel_f[pl.ds(4 * i, 4), :] = mid_f[pl.ds(4 * tab[32 + i], 4), :]
        return carry

    lax.fori_loop(0, NGX * MOST, choose_flux, 0)
    flux_second = exchange(sel_f, back_f, 16, 6)
    for copy in average_first:
        copy.wait()

    def choose_average(b, carry):
        for r in range(MOST):
            at = tab[32 + MOST * b + r]
            sel_a[pl.ds(40 * b + 8 * r, 8), :] = mid_a[pl.ds(24 * (at // 2) + 8 * (at % 2), 8), :]
            sel_a[pl.ds(40 * b + 32 + 2 * r, 2), :] = mid_a[
                pl.ds(24 * (at // 2) + 16 + 2 * (at % 2), 2), :
            ]
        return carry

    lax.fori_loop(0, NGX, choose_average, 0)
    average_second = exchange(sel_a, back_a, 40, 7)

    amount_sign = jnp.where(in32 < 16, -0.05, 0.05).astype(F32)
    count = tab[104]
    y0s = [jnp.where(r < count, tab[96 + r], -1) for r in range(MOST)]
    z0s = [tab[100 + r] for r in range(MOST)]
    rest16 = lax.rem(lane16, 16)
    wanted = [
        [
            (lane16 >= z0s[r])
            & (lane16 < z0s[r] + 16)
            & (jnp.broadcast_to(y0s[r], (16, 128)) == 16 * half)
            for half in range(2)
        ]
        for r in range(MOST)
    ]
    covered = []
    for half in range(2):
        mask = wanted[0][half]
        for r in range(1, MOST):
            mask = mask | wanted[r][half]
        covered.append(mask)
    for copy in flux_second:
        copy.wait()
    means = [unpack_rows(back_f, 4 * r, 16) for r in range(MOST)]
    for f in range(5):
        values = [amount_sign * (means[r][f] - fc_ref[r, f]) for r in range(MOST)]
        for face in range(6):
            picks = [take(value, rest16 + 16 * face) for value in values]
            for half in range(2):
                total = jnp.zeros((16, 128), F32)
                for r in range(MOST):
                    total = jnp.where(wanted[r][half], picks[r], total)
                if face < 2:
                    xs_buf[face, f, pl.ds(16 * half, 16), :] = total
                elif face < 4:
                    ys_buf[half + 2 * (face - 2), f] = total
                else:
                    zs_buf[face - 4, f, pl.ds(16 * half, 16), :] = total
    swaps = []
    for number, (src, dst, device) in enumerate(
        (
            (xs_buf.at[0], xa.at[1], (xs[0], gy)),
            (xs_buf.at[1], xa.at[0], (xs[1], gy)),
            (ys_buf.at[0], ya.at[1], (gx, ys[0])),
            (ys_buf.at[3], ya.at[0], (gx, ys[1])),
        )
    ):
        copy = pltpu.make_async_remote_copy(
            src_ref=src,
            dst_ref=dst,
            send_sem=swap_send.at[number],
            recv_sem=swap_recv.at[number],
            device_id=device,
            device_id_type=MESH,
        )
        copy.start()
        swaps.append(copy)
    for copy in writes + average_second:
        copy.wait()
    for c in range(16):
        for r in range(MOST):
            back_s[pl.ds(((c // 4) * 4 + r) * 8 + 2 * (c % 4), 2), :] = back_a[
                pl.ds(40 * c + 32 + 2 * r, 2), :
            ]

    rest = lax.rem(lane, 16)
    insides = [[wanted[r][half][0:8] for r in range(MOST)] for half in range(2)]

    def assemble(f, xq, packed):
        for h in range(2):
            faces = [
                [zs_buf[end, f, pl.ds(16 * half + h, 8, stride=2), :] for end in range(2)]
                for half in range(2)
            ]
            for j in range(4):
                x = 4 * xq + j
                pick = 2 * rest + (h * 64 + (j // 2) * 32 + j % 2)
                picks = [take(packed[r], pick) for r in range(MOST)]
                low_at = (lane + 1 + x) % 128
                high_at = (lane + 112 + x) % 128
                for half in range(2):
                    rows = pl.ds(32 * x + 16 * half + h, 8, stride=2)
                    value = out_ref[f, rows, :]
                    low = take(faces[half][0], low_at)
                    high = take(faces[half][1], high_at)
                    value = value + jnp.where(rest == 15, low, jnp.where(rest == 0, high, 0.0))
                    for r in range(MOST):
                        value = jnp.where(insides[half][r], picks[r], value)
                    out_ref[f, rows, :] = value

    def assemble_piece(i, carry):
        assemble(i // 4, i % 4, [back_a[pl.ds(40 * i + 8 * r, 8), :] for r in range(MOST)])
        return carry

    def assemble_rest(i, carry):
        assemble(4, i, [back_s[pl.ds(32 * i + 8 * r, 8), :] for r in range(MOST)])
        return carry

    lax.fori_loop(0, 16, assemble_piece, 0)
    lax.fori_loop(0, 4, assemble_rest, 0)
    for copy in swaps:
        copy.wait()
    for f in range(5):
        for end in range(2):
            for half in range(2):
                rows = pl.ds(480 * end + 16 * half, 16)
                out_ref[f, rows, :] = out_ref[f, rows, :] + jnp.where(
                    covered[half], 0.0, xa[end, f, pl.ds(16 * half, 16), :]
                )
        for y, values in ((0, ya[0, f]), (31, ya[1, f]), (15, ys_buf[1, f]), (16, ys_buf[2, f])):
            rows = pl.ds(y, 16, stride=32)
            out_ref[f, rows, :] = out_ref[f, rows, :] + jnp.where(covered[y // 16], 0.0, values)
    for copy in fine_writes:
        copy.wait()


def whole_step(tab, coarse, fine):
    dma = pltpu.SemaphoreType.DMA

    def array(*shape):
        return VMEM(shape, F32)

    return pl.pallas_call(
        step_kernel,
        out_shape=(
            jax.ShapeDtypeStruct((5, 512, 128), F32),
            jax.ShapeDtypeStruct((2, 5, 4, 8, 1024), F32),
        ),
        in_specs=[
            pl.BlockSpec(memory_space=SMEM),
            pl.BlockSpec(memory_space=pltpu.HBM),
            pl.BlockSpec(memory_space=pltpu.HBM),
        ],
        out_specs=(pl.BlockSpec(memory_space=VMEM), pl.BlockSpec(memory_space=pl.ANY)),
        scratch_shapes=[
            array(5, XE * YE, 128),
            array(5, XE * YE, 128),
            array(2, 5, 2, 32, 128),
            array(2, 5, 2, 16, 128),
            array(4, 8, 128),
            array(2, 5, 2, 16, 128),
            array(4, 8, 128),
            array(2, 256, 128),
            array(256, 128),
            array(256, 128),
            array(2, 128, 128),
            array(128, 128),
            array(128, 128),
            array(MOST, 5, 16, 128),
            array(2, 5, 4, 64, 128),
            array(2, 5, 32, 8, 128),
            array(2, 5, 32, 8, 128),
            array(2, 5, 16, 128),
            array(2, 5, 2, 8, 128),
            array(2, 5, 16, 8, 128),
            array(2, 5, 16, 8, 128),
            array(2, 2, 5, 8, 128),
            array(2, 5, 16, 8, 128),
            array(2, 5, 16, 8, 128),
            array(2, 2, 5, 8, 128),
            array(2, 5, 16, 8, 128),
            array(2, 5, 16, 8, 128),
            array(2, 5, 16, 128),
            array(2, 5, 16, 128),
            array(2, 5, 16, 8, 128),
            array(2, 5, 16, 128),
            array(128, 128),
            array(128, 128),
            array(256, 128),
            array(256, 128),
            array(384, 128),
            array(384, 128),
            array(640, 128),
            array(640, 128),
            array(128, 128),
            array(2, 5, 32, 128),
            array(4, 5, 16, 128),
            array(2, 5, 32, 128),
            array(2, 5, 32, 128),
            array(2, 5, 16, 128),
            dma((16,)),
            dma((2, 8)),
            dma((2, 8)),
            dma((10,)),
            dma((10,)),
            dma((8, NGX - 1)),
            dma((8, NGX - 1)),
            dma((8,)),
            dma((4,)),
            dma((4,)),
        ],
        compiler_params=pltpu.CompilerParams(
            collective_id=1, has_side_effects=True, vmem_limit_bytes=LIMIT
        ),
    )(tab, coarse, fine)


def per_device(coarse_state, fine_state, corners, slot_patch):
    coarse = coarse_state.reshape(5, 512, 128)
    tab = tables(jnp.transpose(corners, (2, 0, 1)), slot_patch)
    out, fine_next = whole_step(tab, coarse, fine_state.reshape(2, 5, 4, 8, 1024))
    return out.reshape(coarse_state.shape), fine_next.reshape(fine_state.shape)


def solution(mesh):
    placed = (
        P(None, "gx", "gy", None),
        P("gx", "gy", None, None, None, None),
        P("gy", None, None),
        P("gy", None),
    )
    return jax.shard_map(
        per_device,
        mesh=mesh,
        in_specs=placed,
        out_specs=(P(None, "gx", "gy", None), P("gx", "gy", None, None, None, None)),
        check_vma=False,
    )
```

```python
import jax
import jax.numpy as jnp
from jax import lax
from jax.experimental import pallas as pl
from jax.experimental.pallas import tpu as pltpu
from jax.sharding import PartitionSpec as P

F32 = jnp.float32
I32 = jnp.int32
MESH = pl.DeviceIdType.MESH
VMEM = pltpu.VMEM
SMEM = pltpu.SMEM
NGX = 16
NGY = 8
MOST = 4
PCOL = 32
YE = 48
XE = 20
LIMIT = 56 * 1024 * 1024
PLACE_LIMIT = 4 * 1024 * 1024


def lane_ids(rows=8):
    return lax.broadcasted_iota(I32, (rows, 128), 1)


def take(values, idx):
    return jnp.take_along_axis(values, idx, axis=1)


def prims(state):
    inv = 1.0 / state[0]
    vel = [state[1] * inv, state[2] * inv, state[3] * inv]
    kinetic = 0.5 * (state[1] * vel[0] + state[2] * vel[1] + state[3] * vel[2])
    pressure = 0.4 * (state[4] - kinetic)
    sound = jnp.sqrt(1.4 * pressure * inv)
    return vel, pressure, sound


def flow(state, vel, pressure, normal):
    out = [state[1 + normal], state[1] * vel, state[2] * vel, state[3] * vel, (state[4] + pressure) * vel]
    out[1 + normal] = out[1 + normal] + pressure
    return out


def side(state, normal, pre=None):
    vel, pressure, sound = prims(state) if pre is None else pre
    return state, flow(state, vel[normal], pressure, normal), jnp.abs(vel[normal]) + sound


def twice_flux(low, high):
    fastest = jnp.maximum(low[2], high[2])
    return [
        (low[1][f] + high[1][f]) - fastest * (high[0][f] - low[0][f]) for f in range(5)
    ]


def neighbours():
    gx, gy = lax.axis_index("gx"), lax.axis_index("gy")
    xs = (lax.rem(gx + NGX - 1, NGX), lax.rem(gx + 1, NGX))
    ys = (lax.rem(gy + NGY - 1, NGY), lax.rem(gy + 1, NGY))
    return gx, gy, xs, ys


def greet(devices):
    barrier = pltpu.get_barrier_semaphore()
    for device in devices:
        pl.semaphore_signal(barrier, inc=1, device_id=device, device_id_type=MESH)
    pl.semaphore_wait(barrier, len(devices))


def tables_kernel(corners, holders, tab, rows):
    me = lax.axis_index("gx")
    for i in range(NGX * MOST):
        tab[32 + i] = 0
    for i in range(105, 128):
        tab[i] = 0
    mine, count, last, rank = 0, 0, -1, 0
    for q in range(PCOL):
        b = corners[0, 0, q] // 16
        rank = jnp.where(b == last, rank + 1, 0)
        last = b
        rows[q] = b * MOST + rank
        mine = mine + jnp.where(b < me, 1, 0)
        count = count + jnp.where(b == me, 1, 0)
    found = [rows[holders[0, i]] for i in range(PCOL)]
    for i in range(PCOL):
        tab[i] = found[i]
        tab[32 + found[i]] = i
    for r in range(MOST):
        q = jnp.minimum(mine + r, PCOL - 1)
        tab[96 + r] = lax.rem(corners[1, 0, q], 32)
        tab[100 + r] = corners[2, 0, q]
    tab[104] = count


def tables(corners, holders):
    return pl.pallas_call(
        tables_kernel,
        out_shape=jax.ShapeDtypeStruct((128,), I32),
        in_specs=[pl.BlockSpec(memory_space=SMEM)] * 2,
        out_specs=pl.BlockSpec(memory_space=SMEM),
        scratch_shapes=[SMEM((PCOL,), I32)],
    )(corners, holders)


def y_up(v):
    moved = pltpu.roll(v, 96, axis=1)
    return jnp.where(lane_ids() < 96, moved, pltpu.roll(moved, 7, axis=0))


def y_down(v):
    moved = pltpu.roll(v, 32, axis=1)
    return jnp.where(lane_ids() >= 32, moved, pltpu.roll(moved, 1, axis=0))


def z_up(v):
    return pltpu.roll(v, 127, axis=1)


def z_down(v):
    return pltpu.roll(v, 1, axis=1)


def along(mid, pre, normal, up, down, first, last, sign, ghost):
    cell = side(mid, normal, pre)
    shifted = [up(v) for v in mid]
    above = (shifted, flow(shifted, up(pre[0][normal]), up(pre[1]), normal), up(cell[2]))
    inner = twice_flux(cell, above)
    fastest = jnp.maximum(cell[2], ghost[2]) * sign
    edge = [(cell[1][f] + ghost[1][f]) - fastest * (ghost[0][f] - mid[f]) for f in range(5)]
    diff = [
        jnp.where(last, edge[f], inner[f]) - jnp.where(first, edge[f], down(inner[f]))
        for f in range(5)
    ]
    return diff, edge


def pack_rows(v):
    quarter = lane_ids(16) // 32
    return [
        jnp.where(quarter < 3, v[0], pltpu.roll(v[1], 96, axis=1)),
        jnp.where(quarter < 2, pltpu.roll(v[1], 96, axis=1), pltpu.roll(v[2], 64, axis=1)),
        jnp.where(quarter < 1, pltpu.roll(v[2], 64, axis=1), pltpu.roll(v[3], 32, axis=1)),
        v[4],
    ]


def unpack_rows(got, first, stride):
    quarter = lane_ids(16) // 32
    rows = [got[pl.ds(first + i, 16, stride=stride), :] for i in range(4)]
    found = []
    for f in range(5):
        parts = []
        for g in range(3):
            c = 3 * f + g
            shift = (g - c) % 4 * 32
            parts.append(pltpu.roll(rows[c // 4], shift, axis=1) if shift else rows[c // 4])
        found.append(jnp.where(quarter == 0, parts[0], jnp.where(quarter == 1, parts[1], parts[2])))
    return found


def spread_ghosts(s, faces, gp, gx, gy, gz):
    lane = lane_ids()
    z = lax.rem(lane, 32)
    left = lane < 64
    lane16 = lane_ids(16)
    y_pick = 32 + jnp.where(lane16 >= 96, 16, 0) + lax.rem(lane16, 32) // 2
    z_pick = jnp.where(z == 0, 64, 80)
    for f in range(5):
        gp[s, f] = faces[f]
    for f in range(5):
        even = gp[s, f, pl.ds(0, 8, stride=2), :]
        odd = gp[s, f, pl.ds(1, 8, stride=2), :]
        for end in range(2):
            picks = [take(v, 16 * end + z // 2) for v in (even, odd)]
            gx[s, f, end] = jnp.where(left, picks[0], picks[1])
        lines = take(faces[f], y_pick)
        for k in range(16):
            picks = [take(v, z_pick + k) for v in (even, odd)]
            gz[s, f, k] = jnp.where(left, picks[0], picks[1])
            gy[s, f, k] = jnp.broadcast_to(lines[k : k + 1], (8, 128))


def fine_pass(state, gx, gy, gz, put, put_sums):
    lane = lane_ids()
    sub = lax.broadcasted_iota(I32, (8, 128), 0)
    z = lax.rem(lane, 32)
    y_first = (sub == 0) & (lane < 32)
    y_last = (sub == 7) & (lane >= 96)
    z_first = z == 0
    z_last = z == 31
    y_sign = jnp.where(y_last, 1.0, -1.0).astype(F32)
    z_sign = jnp.where(z_last, 1.0, -1.0).astype(F32)

    def one_pair(s, k, below):
        ghost_y = [gy[s, f, k] for f in range(5)]
        ghost_z = [gz[s, f, k] for f in range(5)]
        mids = [[state[s, f, 2 * k + p] for f in range(5)] for p in range(2)]
        at_end = jnp.broadcast_to(k, (8, 128)) == 15
        mids.append(
            [
                jnp.where(at_end, gx[s, f, 1], state[s, f, 2 * k + 2 - 2 * (k // 15)])
                for f in range(5)
            ]
        )
        ghost_y = side(ghost_y, 1)
        ghost_z = side(ghost_z, 2)
        pres = [prims(mid) for mid in mids]
        sides = [side(mids[p], 0, pres[p]) for p in range(3)]
        results, edges_y, edges_z = [], [], []
        for p in range(2):
            above = twice_flux(sides[p], sides[p + 1])
            diff_y, edge_y = along(mids[p], pres[p], 1, y_up, y_down, y_first, y_last, y_sign, ghost_y)
            diff_z, edge_z = along(mids[p], pres[p], 2, z_up, z_down, z_first, z_last, z_sign, ghost_z)
            results.append(
                [
                    mids[p][f] - 0.025 * ((above[f] - below[f]) + diff_y[f] + diff_z[f])
                    for f in range(5)
                ]
            )
            below = above
            edges_y.append(edge_y)
            edges_z.append(edge_z)
        sum_y = [edges_y[0][f] + edges_y[1][f] for f in range(5)]
        sum_z = [edges_z[0][f] + edges_z[1][f] for f in range(5)]
        return below, results, sum_y, sum_z

    starts = []
    for s in range(2):
        ghost_low = side([gx[s, f, 0] for f in range(5)], 0)
        plane0 = side([state[s, f, 0] for f in range(5)], 0)
        starts.append(twice_flux(ghost_low, plane0))

    def pairs(k, carry):
        found = [one_pair(s, k, carry[s]) for s in range(2)]
        for s in range(2):
            put(s, k, found[s][1])
            put_sums(s, k, found[s][2], found[s][3])
        return tuple(found[0][0]), tuple(found[1][0])

    ends = lax.fori_loop(0, 16, pairs, (tuple(starts[0]), tuple(starts[1])))
    return starts, ends


def step_kernel(
    tab, c_ref, fine_ref, out_ref, fine_out,
    old, new, zc, y_send, c_send, hy, hc, pk, mid_old, mid_new, sel, got_old, got_new, fc_ref,
    buf, state, result, gp, gx_at, gy_at, gz_at, fx, fy, fz, fx2, fy2, fz2, fy_low, fy_high, av, fs,
    rec_f, mid_f, sel_f, back_f, rec_a, mid_a, sel_a, back_a, back_s,
    xs_buf, ys_buf, zs_buf, xa, ya,
    copy_sem, fine_sem, out_sem, halo_send, halo_recv, col_send, col_recv, own_sem, swap_send, swap_recv,
):
    gx, gy, xs, ys = neighbours()
    me = gx
    others = [lax.rem(me + step, NGX) for step in range(1, NGX)]
    loads = []
    for x in range(16):
        loads.append(
            pltpu.make_async_copy(
                c_ref.at[:, pl.ds(32 * x, 32), :],
                old.at[:, pl.ds((x + 2) * YE + 8, 32), :],
                copy_sem.at[x],
            )
        )
    for copy in loads:
        copy.start()
    fine_loads = [
        pltpu.make_async_copy(
            fine_ref.at[s, :, :, :, pl.ds(128 * k, 128)],
            buf.at[s, :, :, pl.ds(8 * k, 8), :],
            fine_sem.at[s, k],
        )
        for s in range(2)
        for k in range(8)
    ]
    for copy in fine_loads:
        copy.start()
    around = [(gx, ys[0]), (gx, ys[1])] + [(xs[a], ys[b]) for a in range(2) for b in range(2)]
    barrier = pltpu.get_barrier_semaphore()
    greeted = [(other, gy) for other in others] + around
    for device in greeted:
        pl.semaphore_signal(barrier, inc=1, device_id=device, device_id_type=MESH)
    c_send[...] = jnp.zeros_like(c_send)
    rec_a[...] = jnp.zeros_like(rec_a)
    for copy in loads:
        copy.wait()
    for end in range(2):
        for f in range(5):
            for r in range(2):
                y_send[end, f, r] = old[f, pl.ds(2 * YE + 8 + 30 * end + r, 16, stride=YE), :]
    for a in range(2):
        for b in range(2):
            for f in range(5):
                c_send[2 * a + b, pl.ds(f, 1), :] = old[
                    f, pl.ds((2 + 15 * a) * YE + 8 + 31 * b, 1), :
                ]
    pl.semaphore_wait(barrier, len(greeted))
    halos = []

    def send(src, dst, device):
        number = len(halos)
        copy = pltpu.make_async_remote_copy(
            src_ref=src,
            dst_ref=dst,
            send_sem=halo_send.at[number],
            recv_sem=halo_recv.at[number],
            device_id=device,
            device_id_type=MESH,
        )
        copy.start()
        halos.append(copy)

    def send_planes(planes):
        for plane, xi, where in planes:
            send(
                c_ref.at[:, pl.ds(32 * plane, 32), :],
                old.at[:, pl.ds(xi * YE + 8, 32), :],
                (xs[where], gy),
            )

    send_planes(((0, 18, 0), (15, 1, 1)))
    for end in range(2):
        send(y_send.at[end], hy.at[1 - end], (gx, ys[end]))
    for a in range(2):
        for b in range(2):
            send(c_send.at[2 * a + b], hc.at[3 - 2 * a - b], (xs[a], ys[b]))
    near = list(halos)
    send_planes(((1, 19, 0), (14, 0, 1)))
    far = halos[len(near) :]

    lane16 = lane_ids(16)
    is_lo = lax.rem(lane16, 32) < 16
    quarter = lane16 // 32
    sign = jnp.where(is_lo, 1.0, -1.0).astype(F32)
    in16 = lax.rem(lane_ids(32), 16)
    zpick = 16 * (in16 % 8) + jnp.where(in16 < 8, 15, 0)
    zorder = 16 * (in16 % 8) + lane_ids(32) // 16
    group = lane_ids(32) // 16

    def advance(mid, xm, xp, ym, yp):
        pre = prims(mid)
        cx = side(mid, 0, pre)
        diff = twice_flux(cx, side(xp, 0))
        low = twice_flux(side(xm, 0), cx)
        total = [a - b for a, b in zip(diff, low)]
        cy = side(mid, 1, pre)
        up = twice_flux(cy, side(yp, 1))
        low = twice_flux(side(ym, 1), cy)
        total = [t + (a - b) for t, a, b in zip(total, up, low)]
        cz = side(mid, 2, pre)
        next_vel = pltpu.roll(pre[0][2], 127, axis=1)
        next_p = pltpu.roll(pre[1], 127, axis=1)
        next_u = [pltpu.roll(v, 127, axis=1) for v in mid]
        nz = (next_u, flow(next_u, next_vel, next_p, 2), pltpu.roll(cz[2], 127, axis=1))
        up = twice_flux(cz, nz)
        total = [t + (a - pltpu.roll(a, 1, axis=1)) for t, a in zip(total, up)]
        return [u - 0.025 * t for u, t in zip(mid, total)]

    def tiles(bases, stride=None):
        def rows(start):
            if stride is None:
                return [old[f, pl.ds(start, 8), :] for f in range(5)]
            return [old[f, pl.ds(start, 8, stride=stride), :] for f in range(5)]

        results = [
            advance(rows(base), rows(base - YE), rows(base + YE), rows(base - 1), rows(base + 1))
            for base in bases
        ]
        for base, result in zip(bases, results):
            for f in range(5):
                if stride is None:
                    new[f, pl.ds(base, 8), :] = result[f]
                else:
                    new[f, pl.ds(base, 8, stride=stride), :] = result[f]

    def inner_plane(xi, carry):
        tiles([xi * YE + 16, xi * YE + 24])
        return carry

    def outer_plane(xi, carry):
        tiles([xi * YE + 8, xi * YE + 32])
        return carry

    def compress(when, source):
        def field(f, carry):
            halves = []
            for half in range(2):
                acc = None
                for x in range(8):
                    plane = source[f, pl.ds((2 + 8 * half + x) * YE + 8, 32), :]
                    picked = take(plane, zpick)
                    acc = picked if acc is None else jnp.where(group == x, picked, acc)
                halves.append(acc)
            for end in range(2):
                parts = [take(acc, zorder + 8 * end) for acc in halves]
                zc[when, f, end] = jnp.where(in16 < 8, parts[0], parts[1])
            return carry

        lax.fori_loop(0, 5, field, 0)

    lax.fori_loop(3, 17, inner_plane, 0)
    compress(0, old)
    for copy in near:
        copy.wait()
    for f in range(5):
        for r in range(2):
            old[f, pl.ds(2 * YE + 6 + r, 16, stride=YE), :] = hy[0, f, r]
            old[f, pl.ds(2 * YE + 40 + r, 16, stride=YE), :] = hy[1, f, r]
        for a, xi in ((0, 1), (1, 18)):
            for b, yi in ((0, 7), (1, 40)):
                old[f, pl.ds(xi * YE + yi, 1), :] = hc[2 * a + b, pl.ds(f, 1), :]

    def groups(source, when, outer, y0, z0):
        z0 = jnp.broadcast_to(z0, (16, 128))
        group = (lane16 - z0 + 128) % 128 // 16
        masks = [group == g for g in range(5)]
        bits = [(z0 // (16 << b)) % 2 == 1 for b in range(3)]
        upper = jnp.broadcast_to(y0, (16, 128)) > 0
        x_at = (1, 18) if outer else (2, 17)
        y_at = (7, 24) if outer else (8, 23)
        found = []
        for f in range(5):
            faces = [
                jnp.where(
                    upper,
                    source[f, pl.ds(xi * YE + 24, 16), :],
                    source[f, pl.ds(xi * YE + 8, 16), :],
                )
                for xi in x_at
            ]
            for yi in y_at:
                faces.append(
                    jnp.where(
                        upper,
                        source[f, pl.ds(2 * YE + yi + 16, 16, stride=YE), :],
                        source[f, pl.ds(2 * YE + yi, 16, stride=YE), :],
                    )
                )
            tops, bottoms = (
                jnp.where(upper, zc[when, f, end, pl.ds(16, 16), :], zc[when, f, end, pl.ds(0, 16), :])
                for end in range(2)
            )
            faces += [tops, bottoms] if outer else [bottoms, tops]
            shifts = (0, 16, 32, 48) + ((80, 64) if outer else (64, 80))
            value = pltpu.roll(faces[5], shifts[5], axis=1)
            for g in range(5):
                moved = pltpu.roll(faces[g], shifts[g], axis=1) if shifts[g] else faces[g]
                value = jnp.where(masks[g], moved, value)
            for b in range(3):
                value = jnp.where(bits[b], pltpu.roll(value, 128 - (16 << b), axis=1), value)
            found.append(value)
        return found

    def extract(when, source):
        def one_rank(r, carry):
            y0 = tab[96 + r]
            v = groups(source, when, True, y0, tab[100 + r])
            rows = pack_rows(v)
            for i in range(4):
                pk[when, pl.ds(r * 4 + i, 16, stride=16), :] = rows[i]
            return carry

        lax.fori_loop(0, MOST, one_rank, 0)

    mids = (mid_old, mid_new)

    def exchange(src, dst, size, number):
        own = pltpu.make_async_copy(
            src.at[pl.ds(size * me, size), :], dst.at[pl.ds(size * me, size), :], own_sem.at[number]
        )
        own.start()
        copies = [own]
        for at, other in enumerate(others):
            copy = pltpu.make_async_remote_copy(
                src_ref=src.at[pl.ds(size * other, size), :],
                dst_ref=dst.at[pl.ds(size * me, size), :],
                send_sem=col_send.at[number, at],
                recv_sem=col_recv.at[number, at],
                device_id=(other, gy),
                device_id_type=MESH,
            )
            copy.start()
            copies.append(copy)
        return copies

    def scatter(when):
        return exchange(pk.at[when], mids[when], 16, when)

    def forward(when, got):
        def choose(d, carry):
            for s in range(2):
                at = tab[2 * d + s]
                sel[when, pl.ds(8 * d + 4 * s, 4), :] = mids[when][pl.ds(4 * at, 4), :]
            return carry

        lax.fori_loop(0, NGX, choose, 0)
        return exchange(sel.at[when], got, 8, 2 + when)

    extract(0, old)
    old_first = scatter(0)
    lax.fori_loop(3, 17, outer_plane, 0)
    for copy in far:
        copy.wait()
    for xi in (1, 2, 17, 18):
        tiles([xi * YE + 8, xi * YE + 16])
        tiles([xi * YE + 24, xi * YE + 32])
    for yi in (7, 40):
        tiles([2 * YE + yi, 10 * YE + yi], YE)
    writes = []
    for x in range(16):
        writes.append(
            pltpu.make_async_copy(
                new.at[:, pl.ds((x + 2) * YE + 8, 32), :],
                out_ref.at[:, pl.ds(32 * x, 32), :],
                copy_sem.at[x],
            )
        )
    compress(1, new)
    extract(1, new)
    new_first = scatter(1)
    for copy in old_first:
        copy.wait()
    old_second = forward(0, got_old)
    for copy in writes:
        copy.start()

    def by_normal(a, b, c):
        return jnp.where(quarter == 0, a, jnp.where(quarter == 1, b, c))

    def normal_side(state):
        vel, pressure, sound = prims(state)
        along = by_normal(*vel)
        flows = [
            by_normal(state[1], state[2], state[3]),
            state[1] * along + jnp.where(quarter == 0, pressure, 0.0),
            state[2] * along + jnp.where(quarter == 1, pressure, 0.0),
            state[3] * along + jnp.where(quarter >= 2, pressure, 0.0),
            (state[4] + pressure) * along,
        ]
        return state, flows, jnp.abs(along) + sound

    def face_flux(r, carry):
        y0 = tab[96 + r]
        out = groups(old, 0, True, y0, tab[100 + r])
        ins = groups(old, 0, False, y0, tab[100 + r])
        a, b = normal_side(out), normal_side(ins)
        fastest = jnp.maximum(a[2], b[2]) * sign
        for f in range(5):
            fc_ref[r, f] = 0.5 * ((a[1][f] + b[1][f]) - fastest * (ins[f] - out[f]))
        return carry

    lax.fori_loop(0, MOST, face_flux, 0)
    for copy in fine_loads:
        copy.wait()
    for s in range(2):
        for x in range(32):
            for f in range(5):
                state[s, f, x] = buf[s, f, x // 8, pl.ds(x % 8, 8, stride=8), :]
    for copy in new_first:
        copy.wait()
    new_second = forward(1, got_new)
    for copy in old_second:
        copy.wait()
    for s in range(2):
        spread_ghosts(s, unpack_rows(got_old, 4 * s, 8), gp, gx_at, gy_at, gz_at)

    def put(s, k, results):
        for f in range(5):
            for p in range(2):
                state[s, f, 2 * k + p] = results[p][f]

    def put_sums(s, k, sum_y, sum_z):
        for f in range(5):
            fy[s, f, k] = sum_y[f]
            fz[s, f, k] = sum_z[f]

    starts, ends = fine_pass(state, gx_at, gy_at, gz_at, put, put_sums)
    for s in range(2):
        for f in range(5):
            fx[s, 0, f] = starts[s][f]
            fx[s, 1, f] = ends[s][f]
    for copy in new_second:
        copy.wait()
    for s in range(2):
        before, after = unpack_rows(got_old, 4 * s, 8), unpack_rows(got_new, 4 * s, 8)
        spread_ghosts(s, [0.5 * (a + b) for a, b in zip(before, after)], gp, gx_at, gy_at, gz_at)

    def put_last(s, k, results):
        for f in range(5):
            for p in range(2):
                result[s, f, 2 * k + p] = results[p][f]
            av[s, f, k] = results[0][f] + results[1][f]

    def put_last_sums(s, k, sum_y, sum_z):
        for f in range(5):
            fy2[s, f, k] = sum_y[f]
            fz2[s, f, k] = sum_z[f]

    starts, ends = fine_pass(state, gx_at, gy_at, gz_at, put_last, put_last_sums)

    lane = lane_ids()
    z = lax.rem(lane, 32)
    in32 = lax.rem(lane16, 32)
    z_is_lo = z < 16
    fold = 2 * lax.rem(lane, 16)
    fold16 = 2 * lax.rem(lane16, 16)
    half_lane = lax.rem(lane, 64)
    z_place = jnp.where(half_lane < 31, half_lane, half_lane - 31)
    for s in range(2):
        for f in range(5):
            loaded = [fz2[s, f, k] + fz[s, f, k] for k in range(16)]
            packed = None
            for k in range(16):
                v = loaded[k] + pltpu.roll(loaded[k], 96, axis=1)
                if k == 0:
                    packed = v
                else:
                    packed = jnp.where(z_place == k, pltpu.roll(v, k, axis=1), packed)
            fz2[s, f, 0] = packed
            lows = fy2[s, f, :, 0, :] + fy[s, f, :, 0, :]
            highs = fy2[s, f, :, 7, :] + fy[s, f, :, 7, :]
            fy_low[s, f] = lows + pltpu.roll(lows, 127, axis=1)
            fy_high[s, f] = highs + pltpu.roll(highs, 127, axis=1)
            for end, added in enumerate((starts, ends)):
                v = fx[s, end, f] + added[s][f]
                v = v + pltpu.roll(v, 96, axis=1)
                fx2[s, end, f] = v + z_up(v)
    for s in range(2):
        means = []
        for f in range(5):
            y_part = jnp.where(
                in32 < 16, take(fy_low[s, f], fold16), take(fy_high[s, f], 96 + fold16)
            )
            packed = fz2[s, f, 0]
            for h in range(2):
                picked = jnp.where(
                    z_is_lo,
                    take(fx2[s, 0, f], h * 64 + fold),
                    take(fx2[s, 1, f], h * 64 + fold),
                )
                z_part = take(packed, h * 64 + jnp.where(z_is_lo, 0, 31) + lax.rem(lane, 16))
                fs[s, f, pl.ds(h, 8, stride=2), :] = jnp.where(lane < 32, picked, z_part)
            whole = jnp.where((lane16 >= 32) & (lane16 < 64), y_part, fs[s, f])
            means.append(whole * 0.0625)
        rows = pack_rows(means)
        for i in range(4):
            rec_f[pl.ds(4 * s + i, 16, stride=8), :] = rows[i]
    flux_first = exchange(rec_f, mid_f, 8, 4)

    slot_of = lax.rem(lane // 32, 2) * 2 + lax.rem(lane, 2)
    for s in range(2):
        for f in range(5):
            loaded = [av[s, f, k] for k in range(16)]
            loaded = [v + pltpu.roll(v, 96, axis=1) for v in loaded]
            loaded = [0.125 * (v + z_up(v)) for v in loaded]
            for xq in range(4):
                packed = loaded[4 * xq]
                for j in range(1, 4):
                    moved = pltpu.roll(loaded[4 * xq + j], (j // 2) * 32 + j % 2, axis=1)
                    packed = jnp.where(slot_of == j, moved, packed)
                v = 4 * f + xq
                if v < 16:
                    rec_a[pl.ds(24 * v + 8 * s, 8), :] = packed
                else:
                    for c in range(4):
                        at = 24 * (4 * (v - 16) + c) + 16 + 2 * s
                        rec_a[pl.ds(at, 2), :] = packed[2 * c : 2 * c + 2]
    average_first = exchange(rec_a, mid_a, 24, 5)
    for s in range(2):
        for x in range(32):
            for f in range(5):
                buf[s, f, x // 8, pl.ds(x % 8, 8, stride=8), :] = result[s, f, x]
    fine_writes = [
        pltpu.make_async_copy(
            buf.at[s, :, :, pl.ds(8 * k, 8), :],
            fine_out.at[s, :, :, :, pl.ds(128 * k, 128)],
            out_sem.at[s, k],
        )
        for s in range(2)
        for k in range(8)
    ]
    for copy in fine_writes:
        copy.start()

    for copy in flux_first:
        copy.wait()

    def choose_flux(i, carry):
        sel_f[pl.ds(4 * i, 4), :] = mid_f[pl.ds(4 * tab[32 + i], 4), :]
        return carry

    lax.fori_loop(0, NGX * MOST, choose_flux, 0)
    flux_second = exchange(sel_f, back_f, 16, 6)
    for copy in average_first:
        copy.wait()

    def choose_average(b, carry):
        for r in range(MOST):
            at = tab[32 + MOST * b + r]
            sel_a[pl.ds(40 * b + 8 * r, 8), :] = mid_a[pl.ds(24 * (at // 2) + 8 * (at % 2), 8), :]
            sel_a[pl.ds(40 * b + 32 + 2 * r, 2), :] = mid_a[
                pl.ds(24 * (at // 2) + 16 + 2 * (at % 2), 2), :
            ]
        return carry

    lax.fori_loop(0, NGX, choose_average, 0)
    average_second = exchange(sel_a, back_a, 40, 7)

    amount_sign = jnp.where(in32 < 16, -0.05, 0.05).astype(F32)
    count = tab[104]
    y0s = [jnp.where(r < count, tab[96 + r], -1) for r in range(MOST)]
    z0s = [tab[100 + r] for r in range(MOST)]
    rest16 = lax.rem(lane16, 16)
    wanted = [
        [
            (lane16 >= z0s[r])
            & (lane16 < z0s[r] + 16)
            & (jnp.broadcast_to(y0s[r], (16, 128)) == 16 * half)
            for half in range(2)
        ]
        for r in range(MOST)
    ]
    covered = []
    for half in range(2):
        mask = wanted[0][half]
        for r in range(1, MOST):
            mask = mask | wanted[r][half]
        covered.append(mask)
    for copy in flux_second:
        copy.wait()
    means = [unpack_rows(back_f, 4 * r, 16) for r in range(MOST)]
    for f in range(5):
        values = [amount_sign * (means[r][f] - fc_ref[r, f]) for r in range(MOST)]
        for face in range(6):
            picks = [take(value, rest16 + 16 * face) for value in values]
            for half in range(2):
                total = jnp.zeros((16, 128), F32)
                for r in range(MOST):
                    total = jnp.where(wanted[r][half], picks[r], total)
                if face < 2:
                    xs_buf[face, f, pl.ds(16 * half, 16), :] = total
                elif face < 4:
                    ys_buf[half + 2 * (face - 2), f] = total
                else:
                    zs_buf[face - 4, f, pl.ds(16 * half, 16), :] = total
    swaps = []
    for number, (src, dst, device) in enumerate(
        (
            (xs_buf.at[0], xa.at[1], (xs[0], gy)),
            (xs_buf.at[1], xa.at[0], (xs[1], gy)),
            (ys_buf.at[0], ya.at[1], (gx, ys[0])),
            (ys_buf.at[3], ya.at[0], (gx, ys[1])),
        )
    ):
        copy = pltpu.make_async_remote_copy(
            src_ref=src,
            dst_ref=dst,
            send_sem=swap_send.at[number],
            recv_sem=swap_recv.at[number],
            device_id=device,
            device_id_type=MESH,
        )
        copy.start()
        swaps.append(copy)
    for copy in writes + average_second:
        copy.wait()
    for c in range(16):
        for r in range(MOST):
            back_s[pl.ds(((c // 4) * 4 + r) * 8 + 2 * (c % 4), 2), :] = back_a[
                pl.ds(40 * c + 32 + 2 * r, 2), :
            ]

    rest = lax.rem(lane, 16)
    insides = [[wanted[r][half][0:8] for r in range(MOST)] for half in range(2)]

    def assemble(f, xq, packed):
        for h in range(2):
            faces = [
                [zs_buf[end, f, pl.ds(16 * half + h, 8, stride=2), :] for end in range(2)]
                for half in range(2)
            ]
            for j in range(4):
                x = 4 * xq + j
                pick = 2 * rest + (h * 64 + (j // 2) * 32 + j % 2)
                picks = [take(packed[r], pick) for r in range(MOST)]
                low_at = (lane + 1 + x) % 128
                high_at = (lane + 112 + x) % 128
                for half in range(2):
                    rows = pl.ds(32 * x + 16 * half + h, 8, stride=2)
                    value = out_ref[f, rows, :]
                    low = take(faces[half][0], low_at)
                    high = take(faces[half][1], high_at)
                    value = value + jnp.where(rest == 15, low, jnp.where(rest == 0, high, 0.0))
                    for r in range(MOST):
                        value = jnp.where(insides[half][r], picks[r], value)
                    out_ref[f, rows, :] = value

    def assemble_piece(i, carry):
        assemble(i // 4, i % 4, [back_a[pl.ds(40 * i + 8 * r, 8), :] for r in range(MOST)])
        return carry

    def assemble_rest(i, carry):
        assemble(4, i, [back_s[pl.ds(32 * i + 8 * r, 8), :] for r in range(MOST)])
        return carry

    lax.fori_loop(0, 16, assemble_piece, 0)
    lax.fori_loop(0, 4, assemble_rest, 0)
    for copy in swaps:
        copy.wait()
    for f in range(5):
        for end in range(2):
            for half in range(2):
                rows = pl.ds(480 * end + 16 * half, 16)
                out_ref[f, rows, :] = out_ref[f, rows, :] + jnp.where(
                    covered[half], 0.0, xa[end, f, pl.ds(16 * half, 16), :]
                )
        for y, values in ((0, ya[0, f]), (31, ya[1, f]), (15, ys_buf[1, f]), (16, ys_buf[2, f])):
            rows = pl.ds(y, 16, stride=32)
            out_ref[f, rows, :] = out_ref[f, rows, :] + jnp.where(covered[y // 16], 0.0, values)
    for copy in fine_writes:
        copy.wait()


def whole_step(tab, coarse, fine):
    dma = pltpu.SemaphoreType.DMA

    def array(*shape):
        return VMEM(shape, F32)

    return pl.pallas_call(
        step_kernel,
        out_shape=(
            VMEM((5, 512, 128), F32),
            VMEM((2, 5, 4, 8, 1024), F32),
        ),
        in_specs=[
            pl.BlockSpec(memory_space=SMEM),
            pl.BlockSpec(memory_space=pltpu.HBM),
            pl.BlockSpec(memory_space=pltpu.HBM),
        ],
        out_specs=(pl.BlockSpec(memory_space=VMEM), pl.BlockSpec(memory_space=VMEM)),
        scratch_shapes=[
            array(5, XE * YE, 128),
            array(5, XE * YE, 128),
            array(2, 5, 2, 32, 128),
            array(2, 5, 2, 16, 128),
            array(4, 8, 128),
            array(2, 5, 2, 16, 128),
            array(4, 8, 128),
            array(2, 256, 128),
            array(256, 128),
            array(256, 128),
            array(2, 128, 128),
            array(128, 128),
            array(128, 128),
            array(MOST, 5, 16, 128),
            array(2, 5, 4, 64, 128),
            array(2, 5, 32, 8, 128),
            array(2, 5, 32, 8, 128),
            array(2, 5, 16, 128),
            array(2, 5, 2, 8, 128),
            array(2, 5, 16, 8, 128),
            array(2, 5, 16, 8, 128),
            array(2, 2, 5, 8, 128),
            array(2, 5, 16, 8, 128),
            array(2, 5, 16, 8, 128),
            array(2, 2, 5, 8, 128),
            array(2, 5, 16, 8, 128),
            array(2, 5, 16, 8, 128),
            array(2, 5, 16, 128),
            array(2, 5, 16, 128),
            array(2, 5, 16, 8, 128),
            array(2, 5, 16, 128),
            array(128, 128),
            array(128, 128),
            array(256, 128),
            array(256, 128),
            array(384, 128),
            array(384, 128),
            array(640, 128),
            array(640, 128),
            array(128, 128),
            array(2, 5, 32, 128),
            array(4, 5, 16, 128),
            array(2, 5, 32, 128),
            array(2, 5, 32, 128),
            array(2, 5, 16, 128),
            dma((16,)),
            dma((2, 8)),
            dma((2, 8)),
            dma((10,)),
            dma((10,)),
            dma((8, NGX - 1)),
            dma((8, NGX - 1)),
            dma((8,)),
            dma((4,)),
            dma((4,)),
        ],
        compiler_params=pltpu.CompilerParams(
            collective_id=1, has_side_effects=True, vmem_limit_bytes=LIMIT
        ),
    )(tab, coarse, fine)


def place_kernel(a_ref, b_ref, a_out, b_out, sem):
    copies = [
        pltpu.make_async_copy(a_ref.at[f], a_out.at[f], sem.at[f]) for f in range(5)
    ] + [
        pltpu.make_async_copy(b_ref.at[s, f], b_out.at[s, f], sem.at[5 + 5 * s + f])
        for s in range(2)
        for f in range(5)
    ]
    for copy in copies:
        copy.start()
    for copy in copies:
        copy.wait()


def place(a, b):
    return pl.pallas_call(
        place_kernel,
        out_shape=(jax.ShapeDtypeStruct(a.shape, F32), jax.ShapeDtypeStruct(b.shape, F32)),
        in_specs=[pl.BlockSpec(memory_space=pl.ANY)] * 2,
        out_specs=(pl.BlockSpec(memory_space=pl.ANY),) * 2,
        scratch_shapes=[pltpu.SemaphoreType.DMA((15,))],
        compiler_params=pltpu.CompilerParams(vmem_limit_bytes=PLACE_LIMIT),
    )(a, b)


def per_device(coarse_state, fine_state, corners, slot_patch):
    coarse = coarse_state.reshape(5, 512, 128)
    tab = tables(jnp.transpose(corners, (2, 0, 1)), slot_patch)
    out, fine_next = place(*whole_step(tab, coarse, fine_state.reshape(2, 5, 4, 8, 1024)))
    return out.reshape(coarse_state.shape), fine_next.reshape(fine_state.shape)


def solution(mesh):
    placed = (
        P(None, "gx", "gy", None),
        P("gx", "gy", None, None, None, None),
        P("gy", None, None),
        P("gy", None),
    )
    return jax.shard_map(
        per_device,
        mesh=mesh,
        in_specs=placed,
        out_specs=(P(None, "gx", "gy", None), P("gx", "gy", None, None, None, None)),
        check_vma=False,
    )
```

```python
import jax
import jax.numpy as jnp
from jax import lax
from jax.experimental import pallas as pl
from jax.experimental.pallas import tpu as pltpu
from jax.sharding import PartitionSpec as P

F32 = jnp.float32
I32 = jnp.int32
MESH = pl.DeviceIdType.MESH
VMEM = pltpu.VMEM
SMEM = pltpu.SMEM
NGX = 16
NGY = 8
MOST = 4
PCOL = 32
YE = 48
XE = 20
LIMIT = 56 * 1024 * 1024
PLACE_LIMIT = 4 * 1024 * 1024


def lane_ids(rows=8):
    return lax.broadcasted_iota(I32, (rows, 128), 1)


def take(values, idx):
    return jnp.take_along_axis(values, idx, axis=1)


def prims(state):
    inv = 1.0 / state[0]
    vel = [state[1] * inv, state[2] * inv, state[3] * inv]
    kinetic = 0.5 * (state[1] * vel[0] + state[2] * vel[1] + state[3] * vel[2])
    pressure = 0.4 * (state[4] - kinetic)
    sound = jnp.sqrt(1.4 * pressure * inv)
    return vel, pressure, sound


def flow(state, vel, pressure, normal):
    out = [state[1 + normal], state[1] * vel, state[2] * vel, state[3] * vel, (state[4] + pressure) * vel]
    out[1 + normal] = out[1 + normal] + pressure
    return out


def side(state, normal, pre=None):
    vel, pressure, sound = prims(state) if pre is None else pre
    return state, flow(state, vel[normal], pressure, normal), jnp.abs(vel[normal]) + sound


def twice_flux(low, high):
    fastest = jnp.maximum(low[2], high[2])
    return [
        (low[1][f] + high[1][f]) - fastest * (high[0][f] - low[0][f]) for f in range(5)
    ]


def neighbours():
    gx, gy = lax.axis_index("gx"), lax.axis_index("gy")
    xs = (lax.rem(gx + NGX - 1, NGX), lax.rem(gx + 1, NGX))
    ys = (lax.rem(gy + NGY - 1, NGY), lax.rem(gy + 1, NGY))
    return gx, gy, xs, ys


def greet(devices):
    barrier = pltpu.get_barrier_semaphore()
    for device in devices:
        pl.semaphore_signal(barrier, inc=1, device_id=device, device_id_type=MESH)
    pl.semaphore_wait(barrier, len(devices))


def y_up(v):
    moved = pltpu.roll(v, 96, axis=1)
    return jnp.where(lane_ids() < 96, moved, pltpu.roll(moved, 7, axis=0))


def y_down(v):
    moved = pltpu.roll(v, 32, axis=1)
    return jnp.where(lane_ids() >= 32, moved, pltpu.roll(moved, 1, axis=0))


def z_up(v):
    return pltpu.roll(v, 127, axis=1)


def z_down(v):
    return pltpu.roll(v, 1, axis=1)


def along(mid, pre, normal, up, down, first, last, sign, ghost):
    cell = side(mid, normal, pre)
    shifted = [up(v) for v in mid]
    above = (shifted, flow(shifted, up(pre[0][normal]), up(pre[1]), normal), up(cell[2]))
    inner = twice_flux(cell, above)
    fastest = jnp.maximum(cell[2], ghost[2]) * sign
    edge = [(cell[1][f] + ghost[1][f]) - fastest * (ghost[0][f] - mid[f]) for f in range(5)]
    diff = [
        jnp.where(last, edge[f], inner[f]) - jnp.where(first, edge[f], down(inner[f]))
        for f in range(5)
    ]
    return diff, edge


def pack_rows(v):
    quarter = lane_ids(16) // 32
    return [
        jnp.where(quarter < 3, v[0], pltpu.roll(v[1], 96, axis=1)),
        jnp.where(quarter < 2, pltpu.roll(v[1], 96, axis=1), pltpu.roll(v[2], 64, axis=1)),
        jnp.where(quarter < 1, pltpu.roll(v[2], 64, axis=1), pltpu.roll(v[3], 32, axis=1)),
        v[4],
    ]


def unpack_rows(got, first, stride):
    quarter = lane_ids(16) // 32
    rows = [got[pl.ds(first + i, 16, stride=stride), :] for i in range(4)]
    found = []
    for f in range(5):
        parts = []
        for g in range(3):
            c = 3 * f + g
            shift = (g - c) % 4 * 32
            parts.append(pltpu.roll(rows[c // 4], shift, axis=1) if shift else rows[c // 4])
        found.append(jnp.where(quarter == 0, parts[0], jnp.where(quarter == 1, parts[1], parts[2])))
    return found


def spread_ghosts(s, faces, gp, gx, gy, gz):
    lane = lane_ids()
    z = lax.rem(lane, 32)
    left = lane < 64
    lane16 = lane_ids(16)
    y_pick = 32 + jnp.where(lane16 >= 96, 16, 0) + lax.rem(lane16, 32) // 2
    z_pick = jnp.where(z == 0, 64, 80)
    for f in range(5):
        gp[s, f] = faces[f]
    for f in range(5):
        even = gp[s, f, pl.ds(0, 8, stride=2), :]
        odd = gp[s, f, pl.ds(1, 8, stride=2), :]
        for end in range(2):
            picks = [take(v, 16 * end + z // 2) for v in (even, odd)]
            gx[s, f, end] = jnp.where(left, picks[0], picks[1])
        lines = take(faces[f], y_pick)
        for k in range(16):
            picks = [take(v, z_pick + k) for v in (even, odd)]
            gz[s, f, k] = jnp.where(left, picks[0], picks[1])
            gy[s, f, k] = jnp.broadcast_to(lines[k : k + 1], (8, 128))


def fine_pass(state, gx, gy, gz, put, put_sums):
    lane = lane_ids()
    sub = lax.broadcasted_iota(I32, (8, 128), 0)
    z = lax.rem(lane, 32)
    y_first = (sub == 0) & (lane < 32)
    y_last = (sub == 7) & (lane >= 96)
    z_first = z == 0
    z_last = z == 31
    y_sign = jnp.where(y_last, 1.0, -1.0).astype(F32)
    z_sign = jnp.where(z_last, 1.0, -1.0).astype(F32)

    def one_pair(s, k, below):
        ghost_y = [gy[s, f, k] for f in range(5)]
        ghost_z = [gz[s, f, k] for f in range(5)]
        mids = [[state[s, f, 2 * k + p] for f in range(5)] for p in range(2)]
        at_end = jnp.broadcast_to(k, (8, 128)) == 15
        mids.append(
            [
                jnp.where(at_end, gx[s, f, 1], state[s, f, 2 * k + 2 - 2 * (k // 15)])
                for f in range(5)
            ]
        )
        ghost_y = side(ghost_y, 1)
        ghost_z = side(ghost_z, 2)
        pres = [prims(mid) for mid in mids]
        sides = [side(mids[p], 0, pres[p]) for p in range(3)]
        results, edges_y, edges_z = [], [], []
        for p in range(2):
            above = twice_flux(sides[p], sides[p + 1])
            diff_y, edge_y = along(mids[p], pres[p], 1, y_up, y_down, y_first, y_last, y_sign, ghost_y)
            diff_z, edge_z = along(mids[p], pres[p], 2, z_up, z_down, z_first, z_last, z_sign, ghost_z)
            results.append(
                [
                    mids[p][f] - 0.025 * ((above[f] - below[f]) + diff_y[f] + diff_z[f])
                    for f in range(5)
                ]
            )
            below = above
            edges_y.append(edge_y)
            edges_z.append(edge_z)
        sum_y = [edges_y[0][f] + edges_y[1][f] for f in range(5)]
        sum_z = [edges_z[0][f] + edges_z[1][f] for f in range(5)]
        return below, results, sum_y, sum_z

    starts = []
    for s in range(2):
        ghost_low = side([gx[s, f, 0] for f in range(5)], 0)
        plane0 = side([state[s, f, 0] for f in range(5)], 0)
        starts.append(twice_flux(ghost_low, plane0))

    def pairs(k, carry):
        found = [one_pair(s, k, carry[s]) for s in range(2)]
        for s in range(2):
            put(s, k, found[s][1])
            put_sums(s, k, found[s][2], found[s][3])
        return tuple(found[0][0]), tuple(found[1][0])

    ends = lax.fori_loop(0, 16, pairs, (tuple(starts[0]), tuple(starts[1])))
    return starts, ends


def step_kernel(
    corners, holders, c_ref, fine_ref, out_ref, fine_out,
    tab, rows_of, slots_vec, slots, slots_sem,
    old, new, zc, y_send, c_send, hy, hc, pk, mid_old, mid_new, sel, got_old, got_new, fc_ref,
    buf, state, result, gp, gx_at, gy_at, gz_at, fx, fy, fz, fx2, fy2, fz2, fy_low, fy_high, av, fs,
    rec_f, mid_f, sel_f, back_f, rec_a, mid_a, sel_a, back_a, back_s,
    xs_buf, ys_buf, zs_buf, xa, ya,
    copy_sem, fine_sem, out_sem, halo_send, halo_recv, col_send, col_recv, own_sem, swap_send, swap_recv,
):
    gx, gy, xs, ys = neighbours()
    me = gx
    others = [lax.rem(me + step, NGX) for step in range(1, NGX)]
    loads = []
    for x in range(16):
        loads.append(
            pltpu.make_async_copy(
                c_ref.at[:, pl.ds(32 * x, 32), :],
                old.at[:, pl.ds((x + 2) * YE + 8, 32), :],
                copy_sem.at[x],
            )
        )
    for copy in loads:
        copy.start()
    fine_loads = [
        pltpu.make_async_copy(
            fine_ref.at[s, :, :, :, pl.ds(128 * k, 128)],
            buf.at[s, :, :, pl.ds(8 * k, 8), :],
            fine_sem.at[s, k],
        )
        for s in range(2)
        for k in range(8)
    ]
    for copy in fine_loads:
        copy.start()
    around = [(gx, ys[0]), (gx, ys[1])] + [(xs[a], ys[b]) for a in range(2) for b in range(2)]
    barrier = pltpu.get_barrier_semaphore()
    greeted = [(other, gy) for other in others] + around
    for device in greeted:
        pl.semaphore_signal(barrier, inc=1, device_id=device, device_id_type=MESH)
    mine, count, last, rank = 0, 0, -1, 0
    for q in range(PCOL):
        b = corners[0, 0, q] // 16
        rank = jnp.where(b == last, rank + 1, 0)
        last = b
        rows_of[q] = b * MOST + rank
        mine = mine + jnp.where(b < me, 1, 0)
        count = count + jnp.where(b == me, 1, 0)
    row_lane = lane_ids()
    slot_lane = jnp.zeros((8, 128), I32)
    for i in range(PCOL):
        row = rows_of[holders[0, i]]
        tab[i] = row
        slot_lane = jnp.where(row_lane == row, i, slot_lane)
    slots_vec[...] = slot_lane
    slots_copy = pltpu.make_async_copy(slots_vec, slots, slots_sem)
    slots_copy.start()
    for r in range(MOST):
        q = jnp.minimum(mine + r, PCOL - 1)
        tab[96 + r] = lax.rem(corners[1, 0, q], 32)
        tab[100 + r] = corners[2, 0, q]
    tab[104] = count
    c_send[...] = jnp.zeros_like(c_send)
    rec_a[...] = jnp.zeros_like(rec_a)
    for copy in loads:
        copy.wait()
    for end in range(2):
        for f in range(5):
            for r in range(2):
                y_send[end, f, r] = old[f, pl.ds(2 * YE + 8 + 30 * end + r, 16, stride=YE), :]
    for a in range(2):
        for b in range(2):
            for f in range(5):
                c_send[2 * a + b, pl.ds(f, 1), :] = old[
                    f, pl.ds((2 + 15 * a) * YE + 8 + 31 * b, 1), :
                ]
    pl.semaphore_wait(barrier, len(greeted))
    halos = []

    def send(src, dst, device):
        number = len(halos)
        copy = pltpu.make_async_remote_copy(
            src_ref=src,
            dst_ref=dst,
            send_sem=halo_send.at[number],
            recv_sem=halo_recv.at[number],
            device_id=device,
            device_id_type=MESH,
        )
        copy.start()
        halos.append(copy)

    def send_planes(planes):
        for plane, xi, where in planes:
            send(
                c_ref.at[:, pl.ds(32 * plane, 32), :],
                old.at[:, pl.ds(xi * YE + 8, 32), :],
                (xs[where], gy),
            )

    send_planes(((0, 18, 0), (15, 1, 1)))
    for end in range(2):
        send(y_send.at[end], hy.at[1 - end], (gx, ys[end]))
    for a in range(2):
        for b in range(2):
            send(c_send.at[2 * a + b], hc.at[3 - 2 * a - b], (xs[a], ys[b]))
    near = list(halos)
    send_planes(((1, 19, 0), (14, 0, 1)))
    far = halos[len(near) :]

    lane16 = lane_ids(16)
    is_lo = lax.rem(lane16, 32) < 16
    quarter = lane16 // 32
    sign = jnp.where(is_lo, 1.0, -1.0).astype(F32)
    in16 = lax.rem(lane_ids(32), 16)
    zpick = 16 * (in16 % 8) + jnp.where(in16 < 8, 15, 0)
    zorder = 16 * (in16 % 8) + lane_ids(32) // 16
    group = lane_ids(32) // 16

    def advance(mid, xm, xp, ym, yp):
        pre = prims(mid)
        cx = side(mid, 0, pre)
        diff = twice_flux(cx, side(xp, 0))
        low = twice_flux(side(xm, 0), cx)
        total = [a - b for a, b in zip(diff, low)]
        cy = side(mid, 1, pre)
        up = twice_flux(cy, side(yp, 1))
        low = twice_flux(side(ym, 1), cy)
        total = [t + (a - b) for t, a, b in zip(total, up, low)]
        cz = side(mid, 2, pre)
        next_vel = pltpu.roll(pre[0][2], 127, axis=1)
        next_p = pltpu.roll(pre[1], 127, axis=1)
        next_u = [pltpu.roll(v, 127, axis=1) for v in mid]
        nz = (next_u, flow(next_u, next_vel, next_p, 2), pltpu.roll(cz[2], 127, axis=1))
        up = twice_flux(cz, nz)
        total = [t + (a - pltpu.roll(a, 1, axis=1)) for t, a in zip(total, up)]
        return [u - 0.025 * t for u, t in zip(mid, total)]

    def tiles(bases, stride=None):
        def rows(start):
            if stride is None:
                return [old[f, pl.ds(start, 8), :] for f in range(5)]
            return [old[f, pl.ds(start, 8, stride=stride), :] for f in range(5)]

        results = [
            advance(rows(base), rows(base - YE), rows(base + YE), rows(base - 1), rows(base + 1))
            for base in bases
        ]
        for base, result in zip(bases, results):
            for f in range(5):
                if stride is None:
                    new[f, pl.ds(base, 8), :] = result[f]
                else:
                    new[f, pl.ds(base, 8, stride=stride), :] = result[f]

    def inner_plane(xi, carry):
        tiles([xi * YE + 16, xi * YE + 24])
        return carry

    def outer_plane(xi, carry):
        tiles([xi * YE + 8, xi * YE + 32])
        return carry

    def compress(when, source):
        def field(f, carry):
            halves = []
            for half in range(2):
                acc = None
                for x in range(8):
                    plane = source[f, pl.ds((2 + 8 * half + x) * YE + 8, 32), :]
                    picked = take(plane, zpick)
                    acc = picked if acc is None else jnp.where(group == x, picked, acc)
                halves.append(acc)
            for end in range(2):
                parts = [take(acc, zorder + 8 * end) for acc in halves]
                zc[when, f, end] = jnp.where(in16 < 8, parts[0], parts[1])
            return carry

        lax.fori_loop(0, 5, field, 0)

    lax.fori_loop(3, 17, inner_plane, 0)
    compress(0, old)
    for copy in near:
        copy.wait()
    for f in range(5):
        for r in range(2):
            old[f, pl.ds(2 * YE + 6 + r, 16, stride=YE), :] = hy[0, f, r]
            old[f, pl.ds(2 * YE + 40 + r, 16, stride=YE), :] = hy[1, f, r]
        for a, xi in ((0, 1), (1, 18)):
            for b, yi in ((0, 7), (1, 40)):
                old[f, pl.ds(xi * YE + yi, 1), :] = hc[2 * a + b, pl.ds(f, 1), :]

    def groups(source, when, outer, y0, z0):
        z0 = jnp.broadcast_to(z0, (16, 128))
        group = (lane16 - z0 + 128) % 128 // 16
        masks = [group == g for g in range(5)]
        bits = [(z0 // (16 << b)) % 2 == 1 for b in range(3)]
        upper = jnp.broadcast_to(y0, (16, 128)) > 0
        x_at = (1, 18) if outer else (2, 17)
        y_at = (7, 24) if outer else (8, 23)
        found = []
        for f in range(5):
            faces = [
                jnp.where(
                    upper,
                    source[f, pl.ds(xi * YE + 24, 16), :],
                    source[f, pl.ds(xi * YE + 8, 16), :],
                )
                for xi in x_at
            ]
            for yi in y_at:
                faces.append(
                    jnp.where(
                        upper,
                        source[f, pl.ds(2 * YE + yi + 16, 16, stride=YE), :],
                        source[f, pl.ds(2 * YE + yi, 16, stride=YE), :],
                    )
                )
            tops, bottoms = (
                jnp.where(upper, zc[when, f, end, pl.ds(16, 16), :], zc[when, f, end, pl.ds(0, 16), :])
                for end in range(2)
            )
            faces += [tops, bottoms] if outer else [bottoms, tops]
            shifts = (0, 16, 32, 48) + ((80, 64) if outer else (64, 80))
            value = pltpu.roll(faces[5], shifts[5], axis=1)
            for g in range(5):
                moved = pltpu.roll(faces[g], shifts[g], axis=1) if shifts[g] else faces[g]
                value = jnp.where(masks[g], moved, value)
            for b in range(3):
                value = jnp.where(bits[b], pltpu.roll(value, 128 - (16 << b), axis=1), value)
            found.append(value)
        return found

    def extract(when, source):
        def one_rank(r, carry):
            y0 = tab[96 + r]
            v = groups(source, when, True, y0, tab[100 + r])
            rows = pack_rows(v)
            for i in range(4):
                pk[when, pl.ds(r * 4 + i, 16, stride=16), :] = rows[i]
            return carry

        lax.fori_loop(0, MOST, one_rank, 0)

    mids = (mid_old, mid_new)

    def exchange(src, dst, size, number):
        own = pltpu.make_async_copy(
            src.at[pl.ds(size * me, size), :], dst.at[pl.ds(size * me, size), :], own_sem.at[number]
        )
        own.start()
        copies = [own]
        for at, other in enumerate(others):
            copy = pltpu.make_async_remote_copy(
                src_ref=src.at[pl.ds(size * other, size), :],
                dst_ref=dst.at[pl.ds(size * me, size), :],
                send_sem=col_send.at[number, at],
                recv_sem=col_recv.at[number, at],
                device_id=(other, gy),
                device_id_type=MESH,
            )
            copy.start()
            copies.append(copy)
        return copies

    def scatter(when):
        return exchange(pk.at[when], mids[when], 16, when)

    def forward(when, got):
        def choose(d, carry):
            for s in range(2):
                at = tab[2 * d + s]
                sel[when, pl.ds(8 * d + 4 * s, 4), :] = mids[when][pl.ds(4 * at, 4), :]
            return carry

        lax.fori_loop(0, NGX, choose, 0)
        return exchange(sel.at[when], got, 8, 2 + when)

    extract(0, old)
    old_first = scatter(0)
    lax.fori_loop(3, 17, outer_plane, 0)
    for copy in far:
        copy.wait()
    for xi in (1, 2, 17, 18):
        tiles([xi * YE + 8, xi * YE + 16])
        tiles([xi * YE + 24, xi * YE + 32])
    for yi in (7, 40):
        tiles([2 * YE + yi, 10 * YE + yi], YE)
    writes = []
    for x in range(16):
        writes.append(
            pltpu.make_async_copy(
                new.at[:, pl.ds((x + 2) * YE + 8, 32), :],
                out_ref.at[:, pl.ds(32 * x, 32), :],
                copy_sem.at[x],
            )
        )
    compress(1, new)
    extract(1, new)
    new_first = scatter(1)
    for copy in old_first:
        copy.wait()
    old_second = forward(0, got_old)
    for copy in writes:
        copy.start()

    def by_normal(a, b, c):
        return jnp.where(quarter == 0, a, jnp.where(quarter == 1, b, c))

    def normal_side(state):
        vel, pressure, sound = prims(state)
        along = by_normal(*vel)
        flows = [
            by_normal(state[1], state[2], state[3]),
            state[1] * along + jnp.where(quarter == 0, pressure, 0.0),
            state[2] * along + jnp.where(quarter == 1, pressure, 0.0),
            state[3] * along + jnp.where(quarter >= 2, pressure, 0.0),
            (state[4] + pressure) * along,
        ]
        return state, flows, jnp.abs(along) + sound

    def face_flux(r, carry):
        y0 = tab[96 + r]
        out = groups(old, 0, True, y0, tab[100 + r])
        ins = groups(old, 0, False, y0, tab[100 + r])
        a, b = normal_side(out), normal_side(ins)
        fastest = jnp.maximum(a[2], b[2]) * sign
        for f in range(5):
            fc_ref[r, f] = 0.5 * ((a[1][f] + b[1][f]) - fastest * (ins[f] - out[f]))
        return carry

    lax.fori_loop(0, MOST, face_flux, 0)
    for copy in fine_loads:
        copy.wait()
    for s in range(2):
        for x in range(32):
            for f in range(5):
                state[s, f, x] = buf[s, f, x // 8, pl.ds(x % 8, 8, stride=8), :]
    for copy in new_first:
        copy.wait()
    new_second = forward(1, got_new)
    for copy in old_second:
        copy.wait()
    for s in range(2):
        spread_ghosts(s, unpack_rows(got_old, 4 * s, 8), gp, gx_at, gy_at, gz_at)

    def put(s, k, results):
        for f in range(5):
            for p in range(2):
                state[s, f, 2 * k + p] = results[p][f]

    def put_sums(s, k, sum_y, sum_z):
        for f in range(5):
            fy[s, f, k] = sum_y[f]
            fz[s, f, k] = sum_z[f]

    starts, ends = fine_pass(state, gx_at, gy_at, gz_at, put, put_sums)
    for s in range(2):
        for f in range(5):
            fx[s, 0, f] = starts[s][f]
            fx[s, 1, f] = ends[s][f]
    for copy in new_second:
        copy.wait()
    for s in range(2):
        before, after = unpack_rows(got_old, 4 * s, 8), unpack_rows(got_new, 4 * s, 8)
        spread_ghosts(s, [0.5 * (a + b) for a, b in zip(before, after)], gp, gx_at, gy_at, gz_at)

    def put_last(s, k, results):
        for f in range(5):
            for p in range(2):
                result[s, f, 2 * k + p] = results[p][f]
            av[s, f, k] = results[0][f] + results[1][f]

    def put_last_sums(s, k, sum_y, sum_z):
        for f in range(5):
            fy2[s, f, k] = sum_y[f]
            fz2[s, f, k] = sum_z[f]

    starts, ends = fine_pass(state, gx_at, gy_at, gz_at, put_last, put_last_sums)

    lane = lane_ids()
    z = lax.rem(lane, 32)
    in32 = lax.rem(lane16, 32)
    z_is_lo = z < 16
    fold = 2 * lax.rem(lane, 16)
    fold16 = 2 * lax.rem(lane16, 16)
    half_lane = lax.rem(lane, 64)
    z_place = jnp.where(half_lane < 31, half_lane, half_lane - 31)
    for s in range(2):
        for f in range(5):
            loaded = [fz2[s, f, k] + fz[s, f, k] for k in range(16)]
            packed = None
            for k in range(16):
                v = loaded[k] + pltpu.roll(loaded[k], 96, axis=1)
                if k == 0:
                    packed = v
                else:
                    packed = jnp.where(z_place == k, pltpu.roll(v, k, axis=1), packed)
            fz2[s, f, 0] = packed
            lows = fy2[s, f, :, 0, :] + fy[s, f, :, 0, :]
            highs = fy2[s, f, :, 7, :] + fy[s, f, :, 7, :]
            fy_low[s, f] = lows + pltpu.roll(lows, 127, axis=1)
            fy_high[s, f] = highs + pltpu.roll(highs, 127, axis=1)
            for end, added in enumerate((starts, ends)):
                v = fx[s, end, f] + added[s][f]
                v = v + pltpu.roll(v, 96, axis=1)
                fx2[s, end, f] = v + z_up(v)
    for s in range(2):
        means = []
        for f in range(5):
            y_part = jnp.where(
                in32 < 16, take(fy_low[s, f], fold16), take(fy_high[s, f], 96 + fold16)
            )
            packed = fz2[s, f, 0]
            for h in range(2):
                picked = jnp.where(
                    z_is_lo,
                    take(fx2[s, 0, f], h * 64 + fold),
                    take(fx2[s, 1, f], h * 64 + fold),
                )
                z_part = take(packed, h * 64 + jnp.where(z_is_lo, 0, 31) + lax.rem(lane, 16))
                fs[s, f, pl.ds(h, 8, stride=2), :] = jnp.where(lane < 32, picked, z_part)
            whole = jnp.where((lane16 >= 32) & (lane16 < 64), y_part, fs[s, f])
            means.append(whole * 0.0625)
        rows = pack_rows(means)
        for i in range(4):
            rec_f[pl.ds(4 * s + i, 16, stride=8), :] = rows[i]
    flux_first = exchange(rec_f, mid_f, 8, 4)

    slot_of = lax.rem(lane // 32, 2) * 2 + lax.rem(lane, 2)
    for s in range(2):
        for f in range(5):
            loaded = [av[s, f, k] for k in range(16)]
            loaded = [v + pltpu.roll(v, 96, axis=1) for v in loaded]
            loaded = [0.125 * (v + z_up(v)) for v in loaded]
            for xq in range(4):
                packed = loaded[4 * xq]
                for j in range(1, 4):
                    moved = pltpu.roll(loaded[4 * xq + j], (j // 2) * 32 + j % 2, axis=1)
                    packed = jnp.where(slot_of == j, moved, packed)
                v = 4 * f + xq
                if v < 16:
                    rec_a[pl.ds(24 * v + 8 * s, 8), :] = packed
                else:
                    for c in range(4):
                        at = 24 * (4 * (v - 16) + c) + 16 + 2 * s
                        rec_a[pl.ds(at, 2), :] = packed[2 * c : 2 * c + 2]
    average_first = exchange(rec_a, mid_a, 24, 5)
    for s in range(2):
        for x in range(32):
            for f in range(5):
                buf[s, f, x // 8, pl.ds(x % 8, 8, stride=8), :] = result[s, f, x]
    fine_writes = [
        pltpu.make_async_copy(
            buf.at[s, :, :, pl.ds(8 * k, 8), :],
            fine_out.at[s, :, :, :, pl.ds(128 * k, 128)],
            out_sem.at[s, k],
        )
        for s in range(2)
        for k in range(8)
    ]
    for copy in fine_writes:
        copy.start()

    slots_copy.wait()
    for copy in flux_first:
        copy.wait()

    def choose_flux(i, carry):
        sel_f[pl.ds(4 * i, 4), :] = mid_f[pl.ds(4 * slots[0, i], 4), :]
        return carry

    lax.fori_loop(0, NGX * MOST, choose_flux, 0)
    flux_second = exchange(sel_f, back_f, 16, 6)
    for copy in average_first:
        copy.wait()

    def choose_average(b, carry):
        for r in range(MOST):
            at = slots[0, MOST * b + r]
            sel_a[pl.ds(40 * b + 8 * r, 8), :] = mid_a[pl.ds(24 * (at // 2) + 8 * (at % 2), 8), :]
            sel_a[pl.ds(40 * b + 32 + 2 * r, 2), :] = mid_a[
                pl.ds(24 * (at // 2) + 16 + 2 * (at % 2), 2), :
            ]
        return carry

    lax.fori_loop(0, NGX, choose_average, 0)
    average_second = exchange(sel_a, back_a, 40, 7)

    amount_sign = jnp.where(in32 < 16, -0.05, 0.05).astype(F32)
    count = tab[104]
    y0s = [jnp.where(r < count, tab[96 + r], -1) for r in range(MOST)]
    z0s = [tab[100 + r] for r in range(MOST)]
    rest16 = lax.rem(lane16, 16)
    wanted = [
        [
            (lane16 >= z0s[r])
            & (lane16 < z0s[r] + 16)
            & (jnp.broadcast_to(y0s[r], (16, 128)) == 16 * half)
            for half in range(2)
        ]
        for r in range(MOST)
    ]
    covered = []
    for half in range(2):
        mask = wanted[0][half]
        for r in range(1, MOST):
            mask = mask | wanted[r][half]
        covered.append(mask)
    for copy in flux_second:
        copy.wait()
    means = [unpack_rows(back_f, 4 * r, 16) for r in range(MOST)]
    for f in range(5):
        values = [amount_sign * (means[r][f] - fc_ref[r, f]) for r in range(MOST)]
        for face in range(6):
            picks = [take(value, rest16 + 16 * face) for value in values]
            for half in range(2):
                total = jnp.zeros((16, 128), F32)
                for r in range(MOST):
                    total = jnp.where(wanted[r][half], picks[r], total)
                if face < 2:
                    xs_buf[face, f, pl.ds(16 * half, 16), :] = total
                elif face < 4:
                    ys_buf[half + 2 * (face - 2), f] = total
                else:
                    zs_buf[face - 4, f, pl.ds(16 * half, 16), :] = total
    swaps = []
    for number, (src, dst, device) in enumerate(
        (
            (xs_buf.at[0], xa.at[1], (xs[0], gy)),
            (xs_buf.at[1], xa.at[0], (xs[1], gy)),
            (ys_buf.at[0], ya.at[1], (gx, ys[0])),
            (ys_buf.at[3], ya.at[0], (gx, ys[1])),
        )
    ):
        copy = pltpu.make_async_remote_copy(
            src_ref=src,
            dst_ref=dst,
            send_sem=swap_send.at[number],
            recv_sem=swap_recv.at[number],
            device_id=device,
            device_id_type=MESH,
        )
        copy.start()
        swaps.append(copy)
    for copy in writes + average_second:
        copy.wait()
    for c in range(16):
        for r in range(MOST):
            back_s[pl.ds(((c // 4) * 4 + r) * 8 + 2 * (c % 4), 2), :] = back_a[
                pl.ds(40 * c + 32 + 2 * r, 2), :
            ]

    rest = lax.rem(lane, 16)
    insides = [[wanted[r][half][0:8] for r in range(MOST)] for half in range(2)]

    def assemble(f, xq, packed):
        for h in range(2):
            faces = [
                [zs_buf[end, f, pl.ds(16 * half + h, 8, stride=2), :] for end in range(2)]
                for half in range(2)
            ]
            for j in range(4):
                x = 4 * xq + j
                pick = 2 * rest + (h * 64 + (j // 2) * 32 + j % 2)
                picks = [take(packed[r], pick) for r in range(MOST)]
                low_at = (lane + 1 + x) % 128
                high_at = (lane + 112 + x) % 128
                for half in range(2):
                    rows = pl.ds(32 * x + 16 * half + h, 8, stride=2)
                    value = out_ref[f, rows, :]
                    low = take(faces[half][0], low_at)
                    high = take(faces[half][1], high_at)
                    value = value + jnp.where(rest == 15, low, jnp.where(rest == 0, high, 0.0))
                    for r in range(MOST):
                        value = jnp.where(insides[half][r], picks[r], value)
                    out_ref[f, rows, :] = value

    def assemble_piece(i, carry):
        assemble(i // 4, i % 4, [back_a[pl.ds(40 * i + 8 * r, 8), :] for r in range(MOST)])
        return carry

    def assemble_rest(i, carry):
        assemble(4, i, [back_s[pl.ds(32 * i + 8 * r, 8), :] for r in range(MOST)])
        return carry

    lax.fori_loop(0, 16, assemble_piece, 0)
    lax.fori_loop(0, 4, assemble_rest, 0)
    for copy in swaps:
        copy.wait()
    for f in range(5):
        for end in range(2):
            for half in range(2):
                rows = pl.ds(480 * end + 16 * half, 16)
                out_ref[f, rows, :] = out_ref[f, rows, :] + jnp.where(
                    covered[half], 0.0, xa[end, f, pl.ds(16 * half, 16), :]
                )
        for y, values in ((0, ya[0, f]), (31, ya[1, f]), (15, ys_buf[1, f]), (16, ys_buf[2, f])):
            rows = pl.ds(y, 16, stride=32)
            out_ref[f, rows, :] = out_ref[f, rows, :] + jnp.where(covered[y // 16], 0.0, values)
    for copy in fine_writes:
        copy.wait()


def whole_step(corners, holders, coarse, fine):
    dma = pltpu.SemaphoreType.DMA

    def array(*shape):
        return VMEM(shape, F32)

    return pl.pallas_call(
        step_kernel,
        out_shape=(
            VMEM((5, 512, 128), F32),
            VMEM((2, 5, 4, 8, 1024), F32),
        ),
        in_specs=[
            pl.BlockSpec(memory_space=SMEM),
            pl.BlockSpec(memory_space=SMEM),
            pl.BlockSpec(memory_space=pltpu.HBM),
            pl.BlockSpec(memory_space=pltpu.HBM),
        ],
        out_specs=(pl.BlockSpec(memory_space=VMEM), pl.BlockSpec(memory_space=VMEM)),
        scratch_shapes=[
            SMEM((128,), I32),
            SMEM((PCOL,), I32),
            VMEM((8, 128), I32),
            SMEM((8, 128), I32),
            dma,
            array(5, XE * YE, 128),
            array(5, XE * YE, 128),
            array(2, 5, 2, 32, 128),
            array(2, 5, 2, 16, 128),
            array(4, 8, 128),
            array(2, 5, 2, 16, 128),
            array(4, 8, 128),
            array(2, 256, 128),
            array(256, 128),
            array(256, 128),
            array(2, 128, 128),
            array(128, 128),
            array(128, 128),
            array(MOST, 5, 16, 128),
            array(2, 5, 4, 64, 128),
            array(2, 5, 32, 8, 128),
            array(2, 5, 32, 8, 128),
            array(2, 5, 16, 128),
            array(2, 5, 2, 8, 128),
            array(2, 5, 16, 8, 128),
            array(2, 5, 16, 8, 128),
            array(2, 2, 5, 8, 128),
            array(2, 5, 16, 8, 128),
            array(2, 5, 16, 8, 128),
            array(2, 2, 5, 8, 128),
            array(2, 5, 16, 8, 128),
            array(2, 5, 16, 8, 128),
            array(2, 5, 16, 128),
            array(2, 5, 16, 128),
            array(2, 5, 16, 8, 128),
            array(2, 5, 16, 128),
            array(128, 128),
            array(128, 128),
            array(256, 128),
            array(256, 128),
            array(384, 128),
            array(384, 128),
            array(640, 128),
            array(640, 128),
            array(128, 128),
            array(2, 5, 32, 128),
            array(4, 5, 16, 128),
            array(2, 5, 32, 128),
            array(2, 5, 32, 128),
            array(2, 5, 16, 128),
            dma((16,)),
            dma((2, 8)),
            dma((2, 8)),
            dma((10,)),
            dma((10,)),
            dma((8, NGX - 1)),
            dma((8, NGX - 1)),
            dma((8,)),
            dma((4,)),
            dma((4,)),
        ],
        compiler_params=pltpu.CompilerParams(
            collective_id=1, has_side_effects=True, vmem_limit_bytes=LIMIT
        ),
    )(corners, holders, coarse, fine)


def place_kernel(a_ref, b_ref, a_out, b_out, sem):
    copies = [
        pltpu.make_async_copy(a_ref.at[f], a_out.at[f], sem.at[f]) for f in range(5)
    ] + [
        pltpu.make_async_copy(b_ref.at[s, f], b_out.at[s, f], sem.at[5 + 5 * s + f])
        for s in range(2)
        for f in range(5)
    ]
    for copy in copies:
        copy.start()
    for copy in copies:
        copy.wait()


def place(a, b):
    return pl.pallas_call(
        place_kernel,
        out_shape=(jax.ShapeDtypeStruct(a.shape, F32), jax.ShapeDtypeStruct(b.shape, F32)),
        in_specs=[pl.BlockSpec(memory_space=pl.ANY)] * 2,
        out_specs=(pl.BlockSpec(memory_space=pl.ANY),) * 2,
        scratch_shapes=[pltpu.SemaphoreType.DMA((15,))],
        compiler_params=pltpu.CompilerParams(vmem_limit_bytes=PLACE_LIMIT),
    )(a, b)


def per_device(coarse_state, fine_state, corners, slot_patch):
    coarse = coarse_state.reshape(5, 512, 128)
    out, fine_next = place(
        *whole_step(
            jnp.transpose(corners, (2, 0, 1)),
            slot_patch,
            coarse,
            fine_state.reshape(2, 5, 4, 8, 1024),
        )
    )
    return out.reshape(coarse_state.shape), fine_next.reshape(fine_state.shape)


def solution(mesh):
    placed = (
        P(None, "gx", "gy", None),
        P("gx", "gy", None, None, None, None),
        P("gy", None, None),
        P("gy", None),
    )
    return jax.shard_map(
        per_device,
        mesh=mesh,
        in_specs=placed,
        out_specs=(P(None, "gx", "gy", None), P("gx", "gy", None, None, None, None)),
        check_vma=False,
    )
```

```python
import jax
import jax.numpy as jnp
from jax import lax
from jax.experimental import pallas as pl
from jax.experimental.pallas import tpu as pltpu
from jax.sharding import PartitionSpec as P

F32 = jnp.float32
I32 = jnp.int32
MESH = pl.DeviceIdType.MESH
VMEM = pltpu.VMEM
SMEM = pltpu.SMEM
NGX = 16
NGY = 8
MOST = 4
PCOL = 32
YE = 48
XE = 20
LIMIT = 56 * 1024 * 1024
PLACE_LIMIT = 4 * 1024 * 1024


def lane_ids(rows=8):
    return lax.broadcasted_iota(I32, (rows, 128), 1)


def take(values, idx):
    return jnp.take_along_axis(values, idx, axis=1)


def prims(state):
    inv = 1.0 / state[0]
    vel = [state[1] * inv, state[2] * inv, state[3] * inv]
    kinetic = 0.5 * (state[1] * vel[0] + state[2] * vel[1] + state[3] * vel[2])
    pressure = 0.4 * (state[4] - kinetic)
    sound = jnp.sqrt(1.4 * pressure * inv)
    return vel, pressure, sound


def flow(state, vel, pressure, normal):
    out = [state[1 + normal], state[1] * vel, state[2] * vel, state[3] * vel, (state[4] + pressure) * vel]
    out[1 + normal] = out[1 + normal] + pressure
    return out


def side(state, normal, pre=None):
    vel, pressure, sound = prims(state) if pre is None else pre
    return state, flow(state, vel[normal], pressure, normal), jnp.abs(vel[normal]) + sound


def twice_flux(low, high):
    fastest = jnp.maximum(low[2], high[2])
    return [
        (low[1][f] + high[1][f]) - fastest * (high[0][f] - low[0][f]) for f in range(5)
    ]


def neighbours():
    gx, gy = lax.axis_index("gx"), lax.axis_index("gy")
    xs = (lax.rem(gx + NGX - 1, NGX), lax.rem(gx + 1, NGX))
    ys = (lax.rem(gy + NGY - 1, NGY), lax.rem(gy + 1, NGY))
    return gx, gy, xs, ys


def greet(devices):
    barrier = pltpu.get_barrier_semaphore()
    for device in devices:
        pl.semaphore_signal(barrier, inc=1, device_id=device, device_id_type=MESH)
    pl.semaphore_wait(barrier, len(devices))


def y_up(v):
    moved = pltpu.roll(v, 96, axis=1)
    return jnp.where(lane_ids() < 96, moved, pltpu.roll(moved, 7, axis=0))


def y_down(v):
    moved = pltpu.roll(v, 32, axis=1)
    return jnp.where(lane_ids() >= 32, moved, pltpu.roll(moved, 1, axis=0))


def z_up(v):
    return pltpu.roll(v, 127, axis=1)


def z_down(v):
    return pltpu.roll(v, 1, axis=1)


def along(mid, pre, normal, up, down, first, last, sign, ghost):
    cell = side(mid, normal, pre)
    shifted = [up(v) for v in mid]
    above = (shifted, flow(shifted, up(pre[0][normal]), up(pre[1]), normal), up(cell[2]))
    inner = twice_flux(cell, above)
    fastest = jnp.maximum(cell[2], ghost[2]) * sign
    edge = [(cell[1][f] + ghost[1][f]) - fastest * (ghost[0][f] - mid[f]) for f in range(5)]
    diff = [
        jnp.where(last, edge[f], inner[f]) - jnp.where(first, edge[f], down(inner[f]))
        for f in range(5)
    ]
    return diff, edge


def pack_rows(v):
    quarter = lane_ids(16) // 32
    return [
        jnp.where(quarter < 3, v[0], pltpu.roll(v[1], 96, axis=1)),
        jnp.where(quarter < 2, pltpu.roll(v[1], 96, axis=1), pltpu.roll(v[2], 64, axis=1)),
        jnp.where(quarter < 1, pltpu.roll(v[2], 64, axis=1), pltpu.roll(v[3], 32, axis=1)),
        v[4],
    ]


def unpack_rows(got, first, stride):
    quarter = lane_ids(16) // 32
    rows = [got[pl.ds(first + i, 16, stride=stride), :] for i in range(4)]
    found = []
    for f in range(5):
        parts = []
        for g in range(3):
            c = 3 * f + g
            shift = (g - c) % 4 * 32
            parts.append(pltpu.roll(rows[c // 4], shift, axis=1) if shift else rows[c // 4])
        found.append(jnp.where(quarter == 0, parts[0], jnp.where(quarter == 1, parts[1], parts[2])))
    return found


def spread_ghosts(s, faces, gp, gx, gy, gz):
    lane = lane_ids()
    z = lax.rem(lane, 32)
    left = lane < 64
    lane16 = lane_ids(16)
    y_pick = 32 + jnp.where(lane16 >= 96, 16, 0) + lax.rem(lane16, 32) // 2
    z_pick = jnp.where(z == 0, 64, 80)
    for f in range(5):
        gp[s, f] = faces[f]
    for f in range(5):
        even = gp[s, f, pl.ds(0, 8, stride=2), :]
        odd = gp[s, f, pl.ds(1, 8, stride=2), :]
        for end in range(2):
            picks = [take(v, 16 * end + z // 2) for v in (even, odd)]
            gx[s, f, end] = jnp.where(left, picks[0], picks[1])
        lines = take(faces[f], y_pick)
        for k in range(16):
            picks = [take(v, z_pick + k) for v in (even, odd)]
            gz[s, f, k] = jnp.where(left, picks[0], picks[1])
            gy[s, f, k] = jnp.broadcast_to(lines[k : k + 1], (8, 128))


def fine_pass(state, gx, gy, gz, put, put_sums):
    lane = lane_ids()
    sub = lax.broadcasted_iota(I32, (8, 128), 0)
    z = lax.rem(lane, 32)
    y_first = (sub == 0) & (lane < 32)
    y_last = (sub == 7) & (lane >= 96)
    z_first = z == 0
    z_last = z == 31
    y_sign = jnp.where(y_last, 1.0, -1.0).astype(F32)
    z_sign = jnp.where(z_last, 1.0, -1.0).astype(F32)

    def one_pair(s, k, below):
        ghost_y = [gy[s, f, k] for f in range(5)]
        ghost_z = [gz[s, f, k] for f in range(5)]
        mids = [[state[s, f, 2 * k + p] for f in range(5)] for p in range(2)]
        at_end = jnp.broadcast_to(k, (8, 128)) == 15
        mids.append(
            [
                jnp.where(at_end, gx[s, f, 1], state[s, f, 2 * k + 2 - 2 * (k // 15)])
                for f in range(5)
            ]
        )
        ghost_y = side(ghost_y, 1)
        ghost_z = side(ghost_z, 2)
        pres = [prims(mid) for mid in mids]
        sides = [side(mids[p], 0, pres[p]) for p in range(3)]
        results, edges_y, edges_z = [], [], []
        for p in range(2):
            above = twice_flux(sides[p], sides[p + 1])
            diff_y, edge_y = along(mids[p], pres[p], 1, y_up, y_down, y_first, y_last, y_sign, ghost_y)
            diff_z, edge_z = along(mids[p], pres[p], 2, z_up, z_down, z_first, z_last, z_sign, ghost_z)
            results.append(
                [
                    mids[p][f] - 0.025 * ((above[f] - below[f]) + diff_y[f] + diff_z[f])
                    for f in range(5)
                ]
            )
            below = above
            edges_y.append(edge_y)
            edges_z.append(edge_z)
        sum_y = [edges_y[0][f] + edges_y[1][f] for f in range(5)]
        sum_z = [edges_z[0][f] + edges_z[1][f] for f in range(5)]
        return below, results, sum_y, sum_z

    starts = []
    for s in range(2):
        ghost_low = side([gx[s, f, 0] for f in range(5)], 0)
        plane0 = side([state[s, f, 0] for f in range(5)], 0)
        starts.append(twice_flux(ghost_low, plane0))

    def pairs(k, carry):
        found = [one_pair(s, k, carry[s]) for s in range(2)]
        for s in range(2):
            put(s, k, found[s][1])
            put_sums(s, k, found[s][2], found[s][3])
        return tuple(found[0][0]), tuple(found[1][0])

    ends = lax.fori_loop(0, 16, pairs, (tuple(starts[0]), tuple(starts[1])))
    return starts, ends


def step_kernel(
    corners, holders, c_ref, fine_ref, out_ref, fine_out,
    tab, rows_of, slots_vec, slots, slots_sem,
    old, new, zc, y_send, c_send, hy, hc, pk, mid_old, mid_new, sel, got_old, got_new, fc_ref,
    buf, state, result, gp, gx_at, gy_at, gz_at, fx, fy, fz, fx2, fy2, fz2, fy_low, fy_high, av, fs,
    rec_f, mid_f, sel_f, back_f, rec_a, mid_a, sel_a, back_a, back_s,
    xs_buf, ys_buf, zs_buf, xa, ya,
    copy_sem, fine_sem, out_sem, halo_send, halo_recv, col_send, col_recv, own_sem, swap_send, swap_recv,
):
    gx, gy, xs, ys = neighbours()
    me = gx
    others = [lax.rem(me + step, NGX) for step in range(1, NGX)]
    loads = []
    for x in range(16):
        loads.append(
            pltpu.make_async_copy(
                c_ref.at[:, pl.ds(32 * x, 32), :],
                old.at[:, pl.ds((x + 2) * YE + 8, 32), :],
                copy_sem.at[x],
            )
        )
    for copy in loads:
        copy.start()
    fine_loads = [
        pltpu.make_async_copy(
            fine_ref.at[s, :, :, :, pl.ds(128 * k, 128)],
            buf.at[s, :, :, pl.ds(8 * k, 8), :],
            fine_sem.at[s, k],
        )
        for s in range(2)
        for k in range(8)
    ]
    for copy in fine_loads:
        copy.start()
    around = [(gx, ys[0]), (gx, ys[1])] + [(xs[a], ys[b]) for a in range(2) for b in range(2)]
    barrier = pltpu.get_barrier_semaphore()
    greeted = [(other, gy) for other in others] + around
    for device in greeted:
        pl.semaphore_signal(barrier, inc=1, device_id=device, device_id_type=MESH)
    mine, count, last, rank = 0, 0, -1, 0
    for q in range(PCOL):
        b = corners[0, 0, q] // 16
        rank = jnp.where(b == last, rank + 1, 0)
        last = b
        rows_of[q] = b * MOST + rank
        mine = mine + jnp.where(b < me, 1, 0)
        count = count + jnp.where(b == me, 1, 0)
    row_lane = lane_ids()
    slot_lane = jnp.zeros((8, 128), I32)
    for i in range(PCOL):
        row = rows_of[holders[0, i]]
        tab[i] = row
        slot_lane = jnp.where(row_lane == row, i, slot_lane)
    slots_vec[...] = slot_lane
    slots_copy = pltpu.make_async_copy(slots_vec, slots, slots_sem)
    slots_copy.start()
    for r in range(MOST):
        q = jnp.minimum(mine + r, PCOL - 1)
        tab[96 + r] = lax.rem(corners[1, 0, q], 32)
        tab[100 + r] = corners[2, 0, q]
    tab[104] = count
    c_send[...] = jnp.zeros_like(c_send)
    rec_a[...] = jnp.zeros_like(rec_a)
    for copy in loads:
        copy.wait()
    for end in range(2):
        for f in range(5):
            for r in range(2):
                y_send[end, f, r] = old[f, pl.ds(2 * YE + 8 + 30 * end + r, 16, stride=YE), :]
    for a in range(2):
        for b in range(2):
            for f in range(5):
                c_send[2 * a + b, pl.ds(f, 1), :] = old[
                    f, pl.ds((2 + 15 * a) * YE + 8 + 31 * b, 1), :
                ]
    pl.semaphore_wait(barrier, len(greeted))
    halos = []

    def send(src, dst, device):
        number = len(halos)
        copy = pltpu.make_async_remote_copy(
            src_ref=src,
            dst_ref=dst,
            send_sem=halo_send.at[number],
            recv_sem=halo_recv.at[number],
            device_id=device,
            device_id_type=MESH,
        )
        copy.start()
        halos.append(copy)

    def send_planes(planes):
        for plane, xi, where in planes:
            send(
                c_ref.at[:, pl.ds(32 * plane, 32), :],
                old.at[:, pl.ds(xi * YE + 8, 32), :],
                (xs[where], gy),
            )

    send_planes(((0, 18, 0), (15, 1, 1)))
    for end in range(2):
        send(y_send.at[end], hy.at[1 - end], (gx, ys[end]))
    for a in range(2):
        for b in range(2):
            send(c_send.at[2 * a + b], hc.at[3 - 2 * a - b], (xs[a], ys[b]))
    near = list(halos)
    send_planes(((1, 19, 0), (14, 0, 1)))
    far = halos[len(near) :]

    lane16 = lane_ids(16)
    is_lo = lax.rem(lane16, 32) < 16
    quarter = lane16 // 32
    sign = jnp.where(is_lo, 1.0, -1.0).astype(F32)
    in16 = lax.rem(lane_ids(32), 16)
    zpick = 16 * (in16 % 8) + jnp.where(in16 < 8, 15, 0)
    zorder = 16 * (in16 % 8) + lane_ids(32) // 16
    group = lane_ids(32) // 16

    def advance(mid, xm, xp, ym, yp):
        pre = prims(mid)
        cx = side(mid, 0, pre)
        diff = twice_flux(cx, side(xp, 0))
        low = twice_flux(side(xm, 0), cx)
        total = [a - b for a, b in zip(diff, low)]
        cy = side(mid, 1, pre)
        up = twice_flux(cy, side(yp, 1))
        low = twice_flux(side(ym, 1), cy)
        total = [t + (a - b) for t, a, b in zip(total, up, low)]
        cz = side(mid, 2, pre)
        next_vel = pltpu.roll(pre[0][2], 127, axis=1)
        next_p = pltpu.roll(pre[1], 127, axis=1)
        next_u = [pltpu.roll(v, 127, axis=1) for v in mid]
        nz = (next_u, flow(next_u, next_vel, next_p, 2), pltpu.roll(cz[2], 127, axis=1))
        up = twice_flux(cz, nz)
        total = [t + (a - pltpu.roll(a, 1, axis=1)) for t, a in zip(total, up)]
        return [u - 0.025 * t for u, t in zip(mid, total)]

    def tiles(bases, stride=None):
        def rows(start):
            if stride is None:
                return [old[f, pl.ds(start, 8), :] for f in range(5)]
            return [old[f, pl.ds(start, 8, stride=stride), :] for f in range(5)]

        results = [
            advance(rows(base), rows(base - YE), rows(base + YE), rows(base - 1), rows(base + 1))
            for base in bases
        ]
        for base, result in zip(bases, results):
            for f in range(5):
                if stride is None:
                    new[f, pl.ds(base, 8), :] = result[f]
                else:
                    new[f, pl.ds(base, 8, stride=stride), :] = result[f]

    def inner_plane(xi, carry):
        tiles([xi * YE + 16, xi * YE + 24])
        return carry

    def outer_plane(xi, carry):
        tiles([xi * YE + 8, xi * YE + 32])
        return carry

    def compress(when, source):
        def field(f, carry):
            halves = []
            for half in range(2):
                acc = None
                for x in range(8):
                    plane = source[f, pl.ds((2 + 8 * half + x) * YE + 8, 32), :]
                    picked = take(plane, zpick)
                    acc = picked if acc is None else jnp.where(group == x, picked, acc)
                halves.append(acc)
            for end in range(2):
                parts = [take(acc, zorder + 8 * end) for acc in halves]
                zc[when, f, end] = jnp.where(in16 < 8, parts[0], parts[1])
            return carry

        lax.fori_loop(0, 5, field, 0, unroll=5)

    lax.fori_loop(3, 17, inner_plane, 0)
    compress(0, old)
    for copy in near:
        copy.wait()
    for f in range(5):
        for r in range(2):
            old[f, pl.ds(2 * YE + 6 + r, 16, stride=YE), :] = hy[0, f, r]
            old[f, pl.ds(2 * YE + 40 + r, 16, stride=YE), :] = hy[1, f, r]
        for a, xi in ((0, 1), (1, 18)):
            for b, yi in ((0, 7), (1, 40)):
                old[f, pl.ds(xi * YE + yi, 1), :] = hc[2 * a + b, pl.ds(f, 1), :]

    def groups(source, when, outer, y0, z0):
        z0 = jnp.broadcast_to(z0, (16, 128))
        group = (lane16 - z0 + 128) % 128 // 16
        masks = [group == g for g in range(5)]
        bits = [(z0 // (16 << b)) % 2 == 1 for b in range(3)]
        upper = jnp.broadcast_to(y0, (16, 128)) > 0
        x_at = (1, 18) if outer else (2, 17)
        y_at = (7, 24) if outer else (8, 23)
        found = []
        for f in range(5):
            faces = [
                jnp.where(
                    upper,
                    source[f, pl.ds(xi * YE + 24, 16), :],
                    source[f, pl.ds(xi * YE + 8, 16), :],
                )
                for xi in x_at
            ]
            for yi in y_at:
                faces.append(
                    jnp.where(
                        upper,
                        source[f, pl.ds(2 * YE + yi + 16, 16, stride=YE), :],
                        source[f, pl.ds(2 * YE + yi, 16, stride=YE), :],
                    )
                )
            tops, bottoms = (
                jnp.where(upper, zc[when, f, end, pl.ds(16, 16), :], zc[when, f, end, pl.ds(0, 16), :])
                for end in range(2)
            )
            faces += [tops, bottoms] if outer else [bottoms, tops]
            shifts = (0, 16, 32, 48) + ((80, 64) if outer else (64, 80))
            value = pltpu.roll(faces[5], shifts[5], axis=1)
            for g in range(5):
                moved = pltpu.roll(faces[g], shifts[g], axis=1) if shifts[g] else faces[g]
                value = jnp.where(masks[g], moved, value)
            for b in range(3):
                value = jnp.where(bits[b], pltpu.roll(value, 128 - (16 << b), axis=1), value)
            found.append(value)
        return found

    def extract(when, source):
        def one_rank(r, carry):
            y0 = tab[96 + r]
            v = groups(source, when, True, y0, tab[100 + r])
            rows = pack_rows(v)
            for i in range(4):
                pk[when, pl.ds(r * 4 + i, 16, stride=16), :] = rows[i]
            return carry

        lax.fori_loop(0, MOST, one_rank, 0, unroll=2)

    mids = (mid_old, mid_new)

    def exchange(src, dst, size, number):
        own = pltpu.make_async_copy(
            src.at[pl.ds(size * me, size), :], dst.at[pl.ds(size * me, size), :], own_sem.at[number]
        )
        own.start()
        copies = [own]
        for at, other in enumerate(others):
            copy = pltpu.make_async_remote_copy(
                src_ref=src.at[pl.ds(size * other, size), :],
                dst_ref=dst.at[pl.ds(size * me, size), :],
                send_sem=col_send.at[number, at],
                recv_sem=col_recv.at[number, at],
                device_id=(other, gy),
                device_id_type=MESH,
            )
            copy.start()
            copies.append(copy)
        return copies

    def scatter(when):
        return exchange(pk.at[when], mids[when], 16, when)

    def forward(when, got):
        def choose(d, carry):
            for s in range(2):
                at = tab[2 * d + s]
                sel[when, pl.ds(8 * d + 4 * s, 4), :] = mids[when][pl.ds(4 * at, 4), :]
            return carry

        lax.fori_loop(0, NGX, choose, 0)
        return exchange(sel.at[when], got, 8, 2 + when)

    extract(0, old)
    old_first = scatter(0)
    lax.fori_loop(3, 17, outer_plane, 0)
    for copy in far:
        copy.wait()
    for xi in (1, 2, 17, 18):
        tiles([xi * YE + 8, xi * YE + 16])
        tiles([xi * YE + 24, xi * YE + 32])
    for yi in (7, 40):
        tiles([2 * YE + yi, 10 * YE + yi], YE)
    writes = []
    for x in range(16):
        writes.append(
            pltpu.make_async_copy(
                new.at[:, pl.ds((x + 2) * YE + 8, 32), :],
                out_ref.at[:, pl.ds(32 * x, 32), :],
                copy_sem.at[x],
            )
        )
    compress(1, new)
    extract(1, new)
    new_first = scatter(1)
    for copy in old_first:
        copy.wait()
    old_second = forward(0, got_old)
    for copy in writes:
        copy.start()

    def by_normal(a, b, c):
        return jnp.where(quarter == 0, a, jnp.where(quarter == 1, b, c))

    def normal_side(state):
        vel, pressure, sound = prims(state)
        along = by_normal(*vel)
        flows = [
            by_normal(state[1], state[2], state[3]),
            state[1] * along + jnp.where(quarter == 0, pressure, 0.0),
            state[2] * along + jnp.where(quarter == 1, pressure, 0.0),
            state[3] * along + jnp.where(quarter >= 2, pressure, 0.0),
            (state[4] + pressure) * along,
        ]
        return state, flows, jnp.abs(along) + sound

    def face_flux(r, carry):
        y0 = tab[96 + r]
        out = groups(old, 0, True, y0, tab[100 + r])
        ins = groups(old, 0, False, y0, tab[100 + r])
        a, b = normal_side(out), normal_side(ins)
        fastest = jnp.maximum(a[2], b[2]) * sign
        for f in range(5):
            fc_ref[r, f] = 0.5 * ((a[1][f] + b[1][f]) - fastest * (ins[f] - out[f]))
        return carry

    lax.fori_loop(0, MOST, face_flux, 0)
    for copy in fine_loads:
        copy.wait()
    for s in range(2):
        for x in range(32):
            for f in range(5):
                state[s, f, x] = buf[s, f, x // 8, pl.ds(x % 8, 8, stride=8), :]
    for copy in new_first:
        copy.wait()
    new_second = forward(1, got_new)
    for copy in old_second:
        copy.wait()
    for s in range(2):
        spread_ghosts(s, unpack_rows(got_old, 4 * s, 8), gp, gx_at, gy_at, gz_at)

    def put(s, k, results):
        for f in range(5):
            for p in range(2):
                state[s, f, 2 * k + p] = results[p][f]

    def put_sums(s, k, sum_y, sum_z):
        for f in range(5):
            fy[s, f, k] = sum_y[f]
            fz[s, f, k] = sum_z[f]

    starts, ends = fine_pass(state, gx_at, gy_at, gz_at, put, put_sums)
    for s in range(2):
        for f in range(5):
            fx[s, 0, f] = starts[s][f]
            fx[s, 1, f] = ends[s][f]
    for copy in new_second:
        copy.wait()
    for s in range(2):
        before, after = unpack_rows(got_old, 4 * s, 8), unpack_rows(got_new, 4 * s, 8)
        spread_ghosts(s, [0.5 * (a + b) for a, b in zip(before, after)], gp, gx_at, gy_at, gz_at)

    def put_last(s, k, results):
        for f in range(5):
            for p in range(2):
                result[s, f, 2 * k + p] = results[p][f]
            av[s, f, k] = results[0][f] + results[1][f]

    def put_last_sums(s, k, sum_y, sum_z):
        for f in range(5):
            fy2[s, f, k] = sum_y[f]
            fz2[s, f, k] = sum_z[f]

    starts, ends = fine_pass(state, gx_at, gy_at, gz_at, put_last, put_last_sums)

    lane = lane_ids()
    z = lax.rem(lane, 32)
    in32 = lax.rem(lane16, 32)
    z_is_lo = z < 16
    fold = 2 * lax.rem(lane, 16)
    fold16 = 2 * lax.rem(lane16, 16)
    half_lane = lax.rem(lane, 64)
    z_place = jnp.where(half_lane < 31, half_lane, half_lane - 31)
    for s in range(2):
        for f in range(5):
            loaded = [fz2[s, f, k] + fz[s, f, k] for k in range(16)]
            packed = None
            for k in range(16):
                v = loaded[k] + pltpu.roll(loaded[k], 96, axis=1)
                if k == 0:
                    packed = v
                else:
                    packed = jnp.where(z_place == k, pltpu.roll(v, k, axis=1), packed)
            fz2[s, f, 0] = packed
            lows = fy2[s, f, :, 0, :] + fy[s, f, :, 0, :]
            highs = fy2[s, f, :, 7, :] + fy[s, f, :, 7, :]
            fy_low[s, f] = lows + pltpu.roll(lows, 127, axis=1)
            fy_high[s, f] = highs + pltpu.roll(highs, 127, axis=1)
            for end, added in enumerate((starts, ends)):
                v = fx[s, end, f] + added[s][f]
                v = v + pltpu.roll(v, 96, axis=1)
                fx2[s, end, f] = v + z_up(v)
    for s in range(2):
        means = []
        for f in range(5):
            y_part = jnp.where(
                in32 < 16, take(fy_low[s, f], fold16), take(fy_high[s, f], 96 + fold16)
            )
            packed = fz2[s, f, 0]
            for h in range(2):
                picked = jnp.where(
                    z_is_lo,
                    take(fx2[s, 0, f], h * 64 + fold),
                    take(fx2[s, 1, f], h * 64 + fold),
                )
                z_part = take(packed, h * 64 + jnp.where(z_is_lo, 0, 31) + lax.rem(lane, 16))
                fs[s, f, pl.ds(h, 8, stride=2), :] = jnp.where(lane < 32, picked, z_part)
            whole = jnp.where((lane16 >= 32) & (lane16 < 64), y_part, fs[s, f])
            means.append(whole * 0.0625)
        rows = pack_rows(means)
        for i in range(4):
            rec_f[pl.ds(4 * s + i, 16, stride=8), :] = rows[i]
    flux_first = exchange(rec_f, mid_f, 8, 4)

    slot_of = lax.rem(lane // 32, 2) * 2 + lax.rem(lane, 2)
    for s in range(2):
        for f in range(5):
            loaded = [av[s, f, k] for k in range(16)]
            loaded = [v + pltpu.roll(v, 96, axis=1) for v in loaded]
            loaded = [0.125 * (v + z_up(v)) for v in loaded]
            for xq in range(4):
                packed = loaded[4 * xq]
                for j in range(1, 4):
                    moved = pltpu.roll(loaded[4 * xq + j], (j // 2) * 32 + j % 2, axis=1)
                    packed = jnp.where(slot_of == j, moved, packed)
                v = 4 * f + xq
                if v < 16:
                    rec_a[pl.ds(24 * v + 8 * s, 8), :] = packed
                else:
                    for c in range(4):
                        at = 24 * (4 * (v - 16) + c) + 16 + 2 * s
                        rec_a[pl.ds(at, 2), :] = packed[2 * c : 2 * c + 2]
    average_first = exchange(rec_a, mid_a, 24, 5)
    for s in range(2):
        for x in range(32):
            for f in range(5):
                buf[s, f, x // 8, pl.ds(x % 8, 8, stride=8), :] = result[s, f, x]
    fine_writes = [
        pltpu.make_async_copy(
            buf.at[s, :, :, pl.ds(8 * k, 8), :],
            fine_out.at[s, :, :, :, pl.ds(128 * k, 128)],
            out_sem.at[s, k],
        )
        for s in range(2)
        for k in range(8)
    ]
    for copy in fine_writes:
        copy.start()

    slots_copy.wait()
    for copy in flux_first:
        copy.wait()

    def choose_flux(i, carry):
        sel_f[pl.ds(4 * i, 4), :] = mid_f[pl.ds(4 * slots[0, i], 4), :]
        return carry

    lax.fori_loop(0, NGX * MOST, choose_flux, 0)
    flux_second = exchange(sel_f, back_f, 16, 6)
    for copy in average_first:
        copy.wait()

    def choose_average(b, carry):
        for r in range(MOST):
            at = slots[0, MOST * b + r]
            sel_a[pl.ds(40 * b + 8 * r, 8), :] = mid_a[pl.ds(24 * (at // 2) + 8 * (at % 2), 8), :]
            sel_a[pl.ds(40 * b + 32 + 2 * r, 2), :] = mid_a[
                pl.ds(24 * (at // 2) + 16 + 2 * (at % 2), 2), :
            ]
        return carry

    lax.fori_loop(0, NGX, choose_average, 0)
    average_second = exchange(sel_a, back_a, 40, 7)

    amount_sign = jnp.where(in32 < 16, -0.05, 0.05).astype(F32)
    count = tab[104]
    y0s = [jnp.where(r < count, tab[96 + r], -1) for r in range(MOST)]
    z0s = [tab[100 + r] for r in range(MOST)]
    rest16 = lax.rem(lane16, 16)
    wanted = [
        [
            (lane16 >= z0s[r])
            & (lane16 < z0s[r] + 16)
            & (jnp.broadcast_to(y0s[r], (16, 128)) == 16 * half)
            for half in range(2)
        ]
        for r in range(MOST)
    ]
    covered = []
    for half in range(2):
        mask = wanted[0][half]
        for r in range(1, MOST):
            mask = mask | wanted[r][half]
        covered.append(mask)
    for copy in flux_second:
        copy.wait()
    means = [unpack_rows(back_f, 4 * r, 16) for r in range(MOST)]
    for f in range(5):
        values = [amount_sign * (means[r][f] - fc_ref[r, f]) for r in range(MOST)]
        for face in range(6):
            picks = [take(value, rest16 + 16 * face) for value in values]
            for half in range(2):
                total = jnp.zeros((16, 128), F32)
                for r in range(MOST):
                    total = jnp.where(wanted[r][half], picks[r], total)
                if face < 2:
                    xs_buf[face, f, pl.ds(16 * half, 16), :] = total
                elif face < 4:
                    ys_buf[half + 2 * (face - 2), f] = total
                else:
                    zs_buf[face - 4, f, pl.ds(16 * half, 16), :] = total
    swaps = []
    for number, (src, dst, device) in enumerate(
        (
            (xs_buf.at[0], xa.at[1], (xs[0], gy)),
            (xs_buf.at[1], xa.at[0], (xs[1], gy)),
            (ys_buf.at[0], ya.at[1], (gx, ys[0])),
            (ys_buf.at[3], ya.at[0], (gx, ys[1])),
        )
    ):
        copy = pltpu.make_async_remote_copy(
            src_ref=src,
            dst_ref=dst,
            send_sem=swap_send.at[number],
            recv_sem=swap_recv.at[number],
            device_id=device,
            device_id_type=MESH,
        )
        copy.start()
        swaps.append(copy)
    for copy in writes + average_second:
        copy.wait()
    for c in range(16):
        for r in range(MOST):
            back_s[pl.ds(((c // 4) * 4 + r) * 8 + 2 * (c % 4), 2), :] = back_a[
                pl.ds(40 * c + 32 + 2 * r, 2), :
            ]

    rest = lax.rem(lane, 16)
    insides = [[wanted[r][half][0:8] for r in range(MOST)] for half in range(2)]

    def assemble(f, xq, packed):
        for h in range(2):
            faces = [
                [zs_buf[end, f, pl.ds(16 * half + h, 8, stride=2), :] for end in range(2)]
                for half in range(2)
            ]
            for j in range(4):
                x = 4 * xq + j
                pick = 2 * rest + (h * 64 + (j // 2) * 32 + j % 2)
                picks = [take(packed[r], pick) for r in range(MOST)]
                low_at = (lane + 1 + x) % 128
                high_at = (lane + 112 + x) % 128
                for half in range(2):
                    rows = pl.ds(32 * x + 16 * half + h, 8, stride=2)
                    value = out_ref[f, rows, :]
                    low = take(faces[half][0], low_at)
                    high = take(faces[half][1], high_at)
                    value = value + jnp.where(rest == 15, low, jnp.where(rest == 0, high, 0.0))
                    for r in range(MOST):
                        value = jnp.where(insides[half][r], picks[r], value)
                    out_ref[f, rows, :] = value

    def assemble_piece(i, carry):
        assemble(i // 4, i % 4, [back_a[pl.ds(40 * i + 8 * r, 8), :] for r in range(MOST)])
        return carry

    def assemble_rest(i, carry):
        assemble(4, i, [back_s[pl.ds(32 * i + 8 * r, 8), :] for r in range(MOST)])
        return carry

    lax.fori_loop(0, 16, assemble_piece, 0)
    lax.fori_loop(0, 4, assemble_rest, 0)
    for copy in swaps:
        copy.wait()
    for f in range(5):
        for end in range(2):
            for half in range(2):
                rows = pl.ds(480 * end + 16 * half, 16)
                out_ref[f, rows, :] = out_ref[f, rows, :] + jnp.where(
                    covered[half], 0.0, xa[end, f, pl.ds(16 * half, 16), :]
                )
        for y, values in ((0, ya[0, f]), (31, ya[1, f]), (15, ys_buf[1, f]), (16, ys_buf[2, f])):
            rows = pl.ds(y, 16, stride=32)
            out_ref[f, rows, :] = out_ref[f, rows, :] + jnp.where(covered[y // 16], 0.0, values)
    for copy in fine_writes:
        copy.wait()


def whole_step(corners, holders, coarse, fine):
    dma = pltpu.SemaphoreType.DMA

    def array(*shape):
        return VMEM(shape, F32)

    return pl.pallas_call(
        step_kernel,
        out_shape=(
            VMEM((5, 512, 128), F32),
            VMEM((2, 5, 4, 8, 1024), F32),
        ),
        in_specs=[
            pl.BlockSpec(memory_space=SMEM),
            pl.BlockSpec(memory_space=SMEM),
            pl.BlockSpec(memory_space=pltpu.HBM),
            pl.BlockSpec(memory_space=pltpu.HBM),
        ],
        out_specs=(pl.BlockSpec(memory_space=VMEM), pl.BlockSpec(memory_space=VMEM)),
        scratch_shapes=[
            SMEM((128,), I32),
            SMEM((PCOL,), I32),
            VMEM((8, 128), I32),
            SMEM((8, 128), I32),
            dma,
            array(5, XE * YE, 128),
            array(5, XE * YE, 128),
            array(2, 5, 2, 32, 128),
            array(2, 5, 2, 16, 128),
            array(4, 8, 128),
            array(2, 5, 2, 16, 128),
            array(4, 8, 128),
            array(2, 256, 128),
            array(256, 128),
            array(256, 128),
            array(2, 128, 128),
            array(128, 128),
            array(128, 128),
            array(MOST, 5, 16, 128),
            array(2, 5, 4, 64, 128),
            array(2, 5, 32, 8, 128),
            array(2, 5, 32, 8, 128),
            array(2, 5, 16, 128),
            array(2, 5, 2, 8, 128),
            array(2, 5, 16, 8, 128),
            array(2, 5, 16, 8, 128),
            array(2, 2, 5, 8, 128),
            array(2, 5, 16, 8, 128),
            array(2, 5, 16, 8, 128),
            array(2, 2, 5, 8, 128),
            array(2, 5, 16, 8, 128),
            array(2, 5, 16, 8, 128),
            array(2, 5, 16, 128),
            array(2, 5, 16, 128),
            array(2, 5, 16, 8, 128),
            array(2, 5, 16, 128),
            array(128, 128),
            array(128, 128),
            array(256, 128),
            array(256, 128),
            array(384, 128),
            array(384, 128),
            array(640, 128),
            array(640, 128),
            array(128, 128),
            array(2, 5, 32, 128),
            array(4, 5, 16, 128),
            array(2, 5, 32, 128),
            array(2, 5, 32, 128),
            array(2, 5, 16, 128),
            dma((16,)),
            dma((2, 8)),
            dma((2, 8)),
            dma((10,)),
            dma((10,)),
            dma((8, NGX - 1)),
            dma((8, NGX - 1)),
            dma((8,)),
            dma((4,)),
            dma((4,)),
        ],
        compiler_params=pltpu.CompilerParams(
            collective_id=1, has_side_effects=True, vmem_limit_bytes=LIMIT
        ),
    )(corners, holders, coarse, fine)


def place_kernel(a_ref, b_ref, a_out, b_out, sem):
    copies = [
        pltpu.make_async_copy(a_ref.at[f], a_out.at[f], sem.at[f]) for f in range(5)
    ] + [
        pltpu.make_async_copy(b_ref.at[s, f], b_out.at[s, f], sem.at[5 + 5 * s + f])
        for s in range(2)
        for f in range(5)
    ]
    for copy in copies:
        copy.start()
    for copy in copies:
        copy.wait()


def place(a, b):
    return pl.pallas_call(
        place_kernel,
        out_shape=(jax.ShapeDtypeStruct(a.shape, F32), jax.ShapeDtypeStruct(b.shape, F32)),
        in_specs=[pl.BlockSpec(memory_space=pl.ANY)] * 2,
        out_specs=(pl.BlockSpec(memory_space=pl.ANY),) * 2,
        scratch_shapes=[pltpu.SemaphoreType.DMA((15,))],
        compiler_params=pltpu.CompilerParams(vmem_limit_bytes=PLACE_LIMIT),
    )(a, b)


def per_device(coarse_state, fine_state, corners, slot_patch):
    coarse = coarse_state.reshape(5, 512, 128)
    out, fine_next = place(
        *whole_step(
            jnp.transpose(corners, (2, 0, 1)),
            slot_patch,
            coarse,
            fine_state.reshape(2, 5, 4, 8, 1024),
        )
    )
    return out.reshape(coarse_state.shape), fine_next.reshape(fine_state.shape)


def solution(mesh):
    placed = (
        P(None, "gx", "gy", None),
        P("gx", "gy", None, None, None, None),
        P("gy", None, None),
        P("gy", None),
    )
    return jax.shard_map(
        per_device,
        mesh=mesh,
        in_specs=placed,
        out_specs=(P(None, "gx", "gy", None), P("gx", "gy", None, None, None, None)),
        check_vma=False,
    )
```
